32 devices in a mesh: row: 4 (over x, core), col: 8 (over z, y).
Axes of the slice: x: 2, y: 2, z: 4, core: 2. Of those that a mesh axis runs over, the one named last changes fastest.
Arguments:
- inputs: float32 [1500, 10240], P('row', 'col'), may hold values from -6 to 6
- lengths: int32 [8], P('row'), may hold values from 375 to 1500, as said below
- cotangent: bfloat16 [1500, 10240], P('row', 'col'), may hold values from -6 to 6
- ln1_gain: float32 [1280], P('col'), may hold values from 0.1 to 1.9
- ln1_bias: float32 [1280], P('col'), may hold values from -1.75 to 1.75
- w_query: float32 [1280, 1280], P('row', 'col'), may hold values from -0.15625 to 0.15625
- b_query: float32 [1280], P('col'), may hold values from -3 to 3
- w_key: float32 [1280, 1280], P('row', 'col'), may hold values from -0.15625 to 0.15625
- w_value: float32 [1280, 1280], P('row', 'col'), may hold values from -0.15625 to 0.15625
- b_value: float32 [1280], P('col'), may hold values from -0.3125 to 0.3125
- w_attn_out: float32 [1280, 1280], P('col', 'row'), may hold values from -2 to 2
- b_attn_out: float32 [1280], P('col'), may hold values from -1.75 to 1.75
- ln2_gain: float32 [1280], P('col'), may hold values from 0.1 to 1.9
- ln2_bias: float32 [1280], P('col'), may hold values from -1.75 to 1.75
- w_in: float32 [1280, 5120], P('row', 'col'), may hold values from -0.15625 to 0.15625
- b_in: float32 [5120], P('col'), may hold values from -3 to 3
- w_out: float32 [5120, 1280], P('col', 'row'), may hold values from -0.078125 to 0.078125
- b_out: float32 [1280], P('col'), may hold values from -1.75 to 1.75
Outputs:
- layer_out: float32 [1500, 10240], P('row', 'col')
- input_grad: float32 [1500, 10240], P('row', 'col')
- ln1_gain_grad: float32 [1280], P('col')
- ln1_bias_grad: float32 [1280], P('col')
- w_query_grad: float32 [1280, 1280], P('row', 'col')
- b_query_grad: float32 [1280], P('col')
- w_key_grad: float32 [1280, 1280], P('row', 'col')
- w_value_grad: float32 [1280, 1280], P('row', 'col')
- b_value_grad: float32 [1280], P('col')
- w_attn_out_grad: float32 [1280, 1280], P('col', 'row')
- b_attn_out_grad: float32 [1280], P('col')
- ln2_gain_grad: float32 [1280], P('col')
- ln2_bias_grad: float32 [1280], P('col')
- w_in_grad: float32 [1280, 5120], P('row', 'col')
- b_in_grad: float32 [5120], P('col')
- w_out_grad: float32 [5120, 1280], P('col', 'row')
- b_out_grad: float32 [1280], P('col')
The draws below stay inside these ranges and needn't reach their ends.
Inputs may be any that keep to these rules, and one draw needn't show every extreme that they name: `lengths`: valid tokens of a clip; some clip in every draw has all 1500.
All inputs are finite; a program needn't handle non-finite values.
Results may differ from the reference program's by a relative error of at most 0.015.
Values may be sent and summed in bfloat16 or wider, within the bound.
No kernel may reach another device: no remote copies, remote signals or barrier semaphores. Data moves between devices by JAX's collectives and lax.ppermute only.
A program may use at most 192 MiB of HBM per device.

```python
import jax
import jax.numpy as jnp
from jax import lax

D = 1280
HEADS = 16
HEAD_DIM = 80
FF = 5120
SLOT = 1500
CLIPS = 8
TOKENS = 12000


def draw_lengths(key, part):
    key = jax.random.fold_in(key, 7)
    first_key, second_key = jax.random.split(key)
    drawn_lengths = jax.random.randint(first_key, (CLIPS,), SLOT // 4, SLOT + 1)
    longest = jax.random.randint(second_key, (), 0, CLIPS)
    return jnp.where(jnp.arange(CLIPS) == longest, SLOT, drawn_lengths).astype(jnp.int32)


def shard_levels(own_key, dims, pieces, smallest, largest):
    level = 1.0
    for axis_at, blocks in pieces:
        heights = jax.random.uniform(jax.random.fold_in(jax.random.fold_in(own_key, 6), axis_at), (blocks,), jnp.float32, smallest / len(pieces), largest / len(pieces))
        level = level * jnp.repeat(jnp.exp(heights), dims[axis_at] // blocks).reshape((-1,) + (1,) * (len(dims) - 1 - axis_at))
    return level


def bell_draw(stream_key, shape, scale, most, cuts=(), kind=jnp.bfloat16):
    result = scale * jax.random.normal(stream_key, shape, jnp.float32)
    if cuts:
        result = result * shard_levels(stream_key, shape, cuts, -0.22, 0.18)
    return jnp.clip(result, -most, most).astype(kind)


def setup_inputs(seed: int = 0) -> dict:
    arg_keys = jax.random.split(jax.random.key(seed), 19)
    return {
        "inputs": bell_draw(arg_keys[0], (TOKENS // 8, D * 8), 1.0, 6.0, ((0, 4), (1, 8)), jnp.float32),
        "lengths": draw_lengths(jax.random.fold_in(arg_keys[18], 71), 0),
        "cotangent": bell_draw(arg_keys[2], (TOKENS // 8, D * 8), 1.0, 6.0, ((0, 4), (1, 8))),
        "ln1_gain": jnp.clip(1.0 + 0.18 * jax.random.normal(arg_keys[3], (D,), jnp.float32), 0.1, 1.9),
        "ln1_bias": bell_draw(arg_keys[4], (D,), 0.3, 1.75, ((0, 8),), jnp.float32),
        "w_query": bell_draw(arg_keys[5], (D, D), D ** -0.5, 0.15625, ((0, 4), (1, 8)), jnp.float32),
        "b_query": bell_draw(arg_keys[6], (D,), 0.5, 3.0, ((0, 8),), jnp.float32),
        "w_key": bell_draw(arg_keys[7], (D, D), D ** -0.5, 0.15625, ((0, 4), (1, 8)), jnp.float32),
        "w_value": bell_draw(arg_keys[8], (D, D), D ** -0.5, 0.15625, ((0, 4), (1, 8)), jnp.float32),
        "b_value": bell_draw(arg_keys[9], (D,), 0.05, 0.3125, ((0, 8),), jnp.float32),
        "w_attn_out": bell_draw(arg_keys[10], (D, D), (max(D // 128, 1)) ** -0.5, 2.0, ((0, 8), (1, 4)), jnp.float32),
        "b_attn_out": bell_draw(arg_keys[11], (D,), 0.3, 1.75, ((0, 8),), jnp.float32),
        "ln2_gain": jnp.clip(1.0 + 0.18 * jax.random.normal(arg_keys[12], (D,), jnp.float32), 0.1, 1.9),
        "ln2_bias": bell_draw(arg_keys[13], (D,), 0.3, 1.75, ((0, 8),), jnp.float32),
        "w_in": bell_draw(arg_keys[14], (D, FF), D ** -0.5, 0.15625, ((0, 4), (1, 8)), jnp.float32),
        "b_in": bell_draw(arg_keys[15], (FF,), 0.5, 3.0, ((0, 8),), jnp.float32),
        "w_out": bell_draw(arg_keys[16], (FF, D), FF ** -0.5, 0.078125, ((0, 8), (1, 4)), jnp.float32),
        "b_out": bell_draw(arg_keys[17], (D,), 0.3, 1.75, ((0, 8),), jnp.float32),
    }


@jax.custom_vjp
def low(v):
    return lax.optimization_barrier(v.astype(jnp.bfloat16)).astype(jnp.float32)

@jax.custom_vjp
def low_back(v):
    return v

def low_keep(v):
    return (low(v), None)

def low_pass(kept, grad):
    return (grad,)

def back_keep(v):
    return (v, None)

def back_low(kept, grad):
    return (low(grad),)
low.defvjp(low_keep, low_pass)
low_back.defvjp(back_keep, back_low)

def layer_norm(tensor, norm_gain, norm_shift):
    row_mean = lax.optimization_barrier(jnp.mean(tensor, axis=-1, keepdims=True))
    centered = tensor - row_mean
    spread = lax.optimization_barrier(jnp.mean(centered * centered, axis=-1, keepdims=True))
    return centered * lax.rsqrt(spread + 1e-05) * norm_gain + norm_shift

def matmul(first, second):
    return jnp.dot(first, second, precision=lax.Precision.HIGHEST, preferred_element_type=jnp.float32)

def split_heads(tensor):
    return tensor.reshape(SLOT, HEADS, HEAD_DIM)

def unpack_rows(tensor):
    return tensor.reshape(TOKENS // 8, D, 8).transpose(0, 2, 1).reshape(TOKENS, D)

def pack_rows(tensor):
    return tensor.reshape(TOKENS // 8, 8, D).transpose(0, 2, 1).reshape(TOKENS // 8, D * 8)

def clip_layer(params, clip_rows, clip_length):
    ln1_gain, ln1_bias, w_query, b_query, w_key, w_value, b_value, w_attn_out, b_attn_out, ln2_gain, ln2_bias, w_in, b_in, w_out, b_out = params
    normed = low(layer_norm(clip_rows, ln1_gain, ln1_bias))
    query_rows = low_back(low(matmul(normed, low(w_query)) + b_query))
    key_rows = low_back(low(matmul(normed, low(w_key))))
    value_rows = low_back(low(matmul(normed, low(w_value)) + b_value))
    scores = jnp.einsum('qhd,khd->hqk', split_heads(query_rows), split_heads(key_rows), precision=lax.Precision.HIGHEST) * HEAD_DIM ** (-0.5)
    scores = low_back(scores)
    valid_keys = jnp.arange(SLOT) < clip_length
    scores = jnp.where(valid_keys[None, None, :], scores, -1e+30)
    weights = low(jax.nn.softmax(scores, axis=-1))
    context = jnp.einsum('hqk,khd->qhd', weights, split_heads(value_rows), precision=lax.Precision.HIGHEST).reshape(SLOT, D)
    context = low_back(low(context))
    middle = clip_rows + low_back(matmul(context, low(w_attn_out))) + b_attn_out
    normed_two = low(layer_norm(middle, ln2_gain, ln2_bias))
    hidden = low_back(matmul(normed_two, low(w_in)) + b_in)
    active = low(jax.nn.gelu(hidden, approximate=False))
    return middle + low_back(matmul(active, low(w_out))) + b_out

def reference(inputs, lengths, cotangent, ln1_gain, ln1_bias, w_query, b_query, w_key, w_value, b_value, w_attn_out, b_attn_out, ln2_gain, ln2_bias, w_in, b_in, w_out, b_out):
    params = (ln1_gain, ln1_bias, w_query, b_query, w_key, w_value, b_value, w_attn_out, b_attn_out, ln2_gain, ln2_bias, w_in, b_in, w_out, b_out)
    clip_inputs = unpack_rows(inputs).reshape(CLIPS, SLOT, D)
    clip_grads = unpack_rows(cotangent.astype(jnp.float32)).reshape(CLIPS, SLOT, D)

    def one_clip(totals, scan_item):
        clip_rows, grad_rows, clip_length = scan_item
        output, pullback = jax.vjp(lambda weights_in, rows_in: clip_layer(weights_in, rows_in, clip_length), params, clip_rows)
        row_valid = (jnp.arange(SLOT) < clip_length).astype(jnp.float32)[:, None]
        param_grads, row_grads = pullback(grad_rows * row_valid)
        totals = jax.tree.map(lambda first, second: first + second, totals, param_grads)
        return (totals, (output, row_grads))
    start_totals = jax.tree.map(jnp.zeros_like, params)
    totals, (outputs, row_grads) = lax.scan(one_clip, start_totals, (clip_inputs, clip_grads, lengths))
    g_ln1_gain, g_ln1_bias, g_query, g_bquery, g_key, g_value, g_bvalue, g_attn_out, g_battn_out, g_ln2_gain, g_ln2_bias, g_in, g_bin, g_out, g_bout = totals
    return (pack_rows(outputs.reshape(TOKENS, D)), pack_rows(row_grads.reshape(TOKENS, D)), g_ln1_gain, g_ln1_bias, g_query, g_bquery, g_key, g_value, g_bvalue, g_attn_out, g_battn_out, g_ln2_gain, g_ln2_bias, g_in, g_bin, g_out, g_bout)
```

```python
import functools

import jax
import jax.numpy as jnp
from jax import lax
from jax.experimental import pallas as pl
from jax.experimental.pallas import tpu as pltpu
from jax.sharding import Mesh
from jax.sharding import PartitionSpec as P

HEADS = 16
EPSILON = 1e-05
PAD = 128
LOG2E = 1.4426950408889634
LN2 = 0.6931471805599453
MASKED = -1e30
BF = jnp.bfloat16
F32 = jnp.float32


def dot(first, second, left, right):
    return lax.dot_general(
        first, second, (((left,), (right,)), ((), ())), preferred_element_type=F32
    )


def swap(tensor, axis, step=1):
    size = lax.axis_size(axis)
    return lax.ppermute(tensor, axis, [(i, i ^ step) for i in range(size)])


def pieces_of(tensor, axis):
    return [tensor] + [swap(tensor, axis, d) for d in range(1, lax.axis_size(axis))]


def in_order(pieces, axis):
    mine = lax.axis_index(axis)
    if len(pieces) == 2:
        return [lax.select_n((mine ^ j) == 1, *pieces) for j in range(2)]
    return [lax.select_n(mine ^ j, *pieces) for j in range(len(pieces))]


def pick(tensor, index, axis):
    return lax.dynamic_index_in_dim(tensor, index, axis, keepdims=False)


def gather_group(part):
    rows = []
    for own in pieces_of(part, "y"):
        rows.append(jnp.concatenate([own, swap(own, "k")], axis=0))
    return rows


def reduce_group(partials):
    quarter = partials[0].shape[0] // 2
    sums = [None] * len(partials)
    for d in reversed(range(len(partials))):
        part = partials[d]
        sums[d] = part[:quarter] + swap(part[quarter:].astype(BF), "k").astype(F32)
    total = sums[0]
    for d in range(1, len(partials)):
        total = total + swap(sums[d].astype(BF), "y", d).astype(F32)
    return total


def forward_body(query_ref, key_ref, value_ref, context_ref, weights_ref):
    scores = dot(key_ref[...], query_ref[...], 1, 1)
    top = jnp.max(scores, axis=0, keepdims=True)
    powers = jnp.exp2(scores - top)
    total = jnp.sum(powers, axis=0, keepdims=True)
    weights = (powers * (1.0 / total)).astype(BF)
    weights_ref[0] = weights
    context_ref[...] = dot(value_ref[...], weights, 0, 0).T.astype(BF)


def attend(packed, heads, block):
    slots = packed.shape[0]
    return pl.pallas_call(
        forward_body,
        grid=(heads, slots // block),
        in_specs=[
            pl.BlockSpec((block, PAD), lambda h, i: (i, h)),
            pl.BlockSpec((slots, PAD), lambda h, i: (0, heads + h)),
            pl.BlockSpec((slots, PAD), lambda h, i: (0, 2 * heads + h)),
        ],
        out_specs=[
            pl.BlockSpec((block, PAD), lambda h, i: (i, h)),
            pl.BlockSpec((1, slots, block), lambda h, i: (h, 0, i)),
        ],
        out_shape=[
            jax.ShapeDtypeStruct((slots, heads * PAD), BF),
            jax.ShapeDtypeStruct((heads, slots, slots), BF),
        ],
        compiler_params=pltpu.CompilerParams(vmem_limit_bytes=50 * 2**20),
        cost_estimate=pl.CostEstimate(
            flops=heads * slots * slots * PAD * 12,
            bytes_accessed=heads * slots * slots * 2,
            transcendentals=heads * slots * slots,
        ),
    )(packed, packed, packed)


def backward_body(
    head_dim,
    steps,
    query_ref,
    key_ref,
    value_ref,
    grad_ref,
    context_ref,
    weights_ref,
    out_ref,
    key_total,
    value_total,
):
    step = pl.program_id(1)
    block = query_ref.shape[0]
    grad = grad_ref[...]
    wide = grad.astype(F32)
    inner = jnp.sum(wide * context_ref[...].astype(F32), axis=1, keepdims=True)
    inner_high = inner.astype(BF).astype(F32)
    lane = lax.broadcasted_iota(jnp.int32, grad.shape, 1)
    extended = jnp.where(
        lane == head_dim,
        inner_high,
        jnp.where(lane == head_dim + 1, inner - inner_high, wide),
    ).astype(BF)
    centered = dot(value_ref[...], extended, 1, 1)
    weights = weights_ref[0]
    grad_scores = (weights.astype(F32) * centered).astype(BF)
    grad_value = dot(weights, grad, 1, 0)
    grad_key = dot(grad_scores, query_ref[...], 1, 0)
    grad_query = (dot(key_ref[...], grad_scores, 0, 0) * head_dim**-0.5).T
    out_ref[0, pl.ds(pl.multiple_of(step * block, block), block), :] = grad_query.astype(BF)

    @pl.when(step == 0)
    def _():
        key_total[...] = grad_key
        value_total[...] = grad_value

    @pl.when(step > 0)
    def _():
        key_total[...] += grad_key
        value_total[...] += grad_value

    @pl.when(step == steps - 1)
    def _():
        out_ref[1] = (key_total[...] * LN2).astype(BF)
        out_ref[2] = value_total[...].astype(BF)


def attend_back(packed, grad_context, context, weights, heads, head_dim, block):
    slots = packed.shape[0]
    steps = slots // block
    rows = pl.BlockSpec((block, PAD), lambda h, i: (i, h))
    return pl.pallas_call(
        functools.partial(backward_body, head_dim, steps),
        grid=(heads, steps),
        in_specs=[
            rows,
            pl.BlockSpec((slots, PAD), lambda h, i: (0, heads + h)),
            pl.BlockSpec((slots, PAD), lambda h, i: (0, 2 * heads + h)),
            rows,
            rows,
            pl.BlockSpec((1, slots, block), lambda h, i: (h, 0, i)),
        ],
        out_specs=pl.BlockSpec((3, slots, PAD), lambda h, i: (0, 0, h)),
        out_shape=jax.ShapeDtypeStruct((3, slots, heads * PAD), BF),
        scratch_shapes=[pltpu.VMEM((slots, PAD), F32)] * 2,
        compiler_params=pltpu.CompilerParams(vmem_limit_bytes=50 * 2**20),
        cost_estimate=pl.CostEstimate(
            flops=heads * slots * slots * PAD * 16,
            bytes_accessed=heads * slots * slots * 2,
            transcendentals=0,
        ),
    )(packed, packed, packed, grad_context, context, weights)


def norm_forward(tensor, gain, shift):
    centered = tensor - jnp.mean(tensor, axis=1, keepdims=True)
    scale = lax.rsqrt(jnp.mean(centered * centered, axis=1, keepdims=True) + EPSILON)
    normal = centered * scale
    return normal, scale, (normal * gain + shift).astype(BF)


def norm_backward(grad, normal, scale, gain):
    weighted = grad * gain
    return scale * (
        weighted
        - jnp.mean(weighted, axis=1, keepdims=True)
        - normal * jnp.mean(weighted * normal, axis=1, keepdims=True)
    )


def local(
    inputs,
    lengths,
    cotangent,
    ln1_gain,
    ln1_bias,
    w_query,
    b_query,
    w_key,
    w_value,
    b_value,
    w_attn_out,
    b_attn_out,
    ln2_gain,
    ln2_bias,
    w_in,
    b_in,
    w_out,
    b_out,
):
    x_size, z_size, y_size = (lax.axis_size(a) for a in ("x", "z", "y"))
    x, k, z, y = (lax.axis_index(a) for a in ("x", "k", "z", "y"))
    pack_count, packed_width = inputs.shape
    features = packed_width // 8
    columns = z_size * y_size
    width = features * columns
    clips = lengths.shape[0]
    slot = pack_count * 8 // clips
    group = 2 * y_size
    quarter = -(-slot // (128 * group)) * 128 if group <= 4 else -(-slot // (16 * group)) * 16
    while (quarter * group) % 128:
        quarter += 16
    slots = quarter * group
    rows = w_query.shape[0]
    block_heads = HEADS // columns
    head_dim = width // HEADS
    split = block_heads % 2 == 0
    part_heads = block_heads // 2 if split else block_heads
    heads = z_size * block_heads // 2
    units = w_in.shape[1]
    half_units = units // 2

    def to_tokens(tensor):
        tokens = (
            tensor.astype(BF)
            .reshape(pack_count, features, 8)
            .transpose(0, 2, 1)
            .reshape(clips, slot, features)
        )
        tokens = jnp.pad(tokens, ((0, 0), (0, slots - slot), (0, 0)))
        tokens = tokens.reshape(clips, y_size, 2, quarter, features)
        kept = pick(tokens, k, 2)
        other = swap(pick(tokens, 1 - k, 2), "k")
        ordered = jnp.concatenate(in_order([kept, other], "k"), axis=0)
        ordered = ordered.reshape(columns, quarter, features)
        moved = lax.all_to_all(ordered, ("z", "y"), 0, 0)
        return moved.transpose(1, 0, 2).reshape(quarter, width)

    def from_tokens(tensor):
        blocks = tensor.astype(BF).reshape(quarter, columns, features).transpose(1, 0, 2)
        moved = lax.all_to_all(blocks, ("z", "y"), 0, 0)
        moved = moved.reshape(2, clips, y_size, quarter, features)
        kept = pick(moved, k, 0)
        other = swap(pick(moved, 1 - k, 0), "k")
        ordered = jnp.stack(in_order([kept, other], "k"), axis=2)
        ordered = ordered.reshape(clips, slots, features)[:, :slot]
        return (
            ordered.reshape(pack_count, 8, features)
            .transpose(0, 2, 1)
            .reshape(pack_count, packed_width)
        )

    def by_core(tensor, parts):
        if not parts:
            return jnp.broadcast_to(tensor[None], (2,) + tensor.shape)
        return tensor.reshape((2, tensor.shape[0] // 2) + tensor.shape[1:])

    turned = [t.astype(BF).T for t in (w_query, w_key, w_value)] + [w_attn_out.astype(BF)]
    head_parts = jnp.stack([by_core(t, split) for t in turned], axis=1)
    head_parts = head_parts.reshape(2, 4 * part_heads * head_dim, rows)
    in_parts = by_core(w_in.astype(BF).T, True)
    out_parts = by_core(w_out.astype(BF), True)
    all_parts = jnp.concatenate([head_parts, in_parts, out_parts], axis=1)
    kept = pick(all_parts, k, 0)
    other = swap(pick(all_parts, 1 - k, 0), "k")
    shard = jnp.concatenate(in_order([kept, other], "k"), axis=1)
    head_rows = head_parts.shape[1]

    def gather_weights(part):
        stacked = jnp.concatenate(pieces_of(part, "z"), axis=0)
        return jnp.concatenate(in_order(pieces_of(stacked, "x"), "x"), axis=1)

    head_weights = gather_weights(shard[:head_rows])
    in_weights = gather_weights(shard[head_rows : head_rows + half_units])
    out_weights = gather_weights(shard[head_rows + half_units :])

    head_weights = head_weights.reshape(z_size, 4, part_heads, head_dim, width)
    if not split:
        head_weights = lax.dynamic_slice_in_dim(head_weights, k * (z_size // 2), z_size // 2, 0)
    head_weights = head_weights.transpose(1, 0, 2, 3, 4).reshape(4, heads, head_dim, width)
    head_weights = jnp.pad(head_weights, ((0, 0), (0, 0), (0, PAD - head_dim), (0, 0)))
    head_weights = head_weights.reshape(4, heads * PAD, width)
    qkv_weights = head_weights[:3].reshape(3 * heads * PAD, width)
    attn_weights = head_weights[3]

    full_vectors = jnp.stack([ln1_gain, ln1_bias, ln2_gain, ln2_bias, b_attn_out, b_out])
    full_count = full_vectors.shape[0]
    full_by_y = jnp.stack(in_order(pieces_of(full_vectors, "y"), "y"))
    part_vector = jnp.concatenate([b_query, b_value, b_in])
    vector_pieces = pieces_of(jnp.concatenate([full_by_y.reshape(-1), part_vector]), "z")
    full_size = full_by_y.size
    full_by_z = jnp.stack(in_order([p[:full_size] for p in vector_pieces], "z"))
    full_by_z = full_by_z.reshape(columns, full_count, features)
    gain_one, shift_one, gain_two, shift_two, attn_shift, out_shift = (
        full_by_z.transpose(1, 0, 2).reshape(full_count, 1, width)
    )
    part_by_z = jnp.stack([p[full_size:] for p in vector_pieces])

    def head_vector(tensor):
        tensor = tensor.reshape(z_size, block_heads, head_dim)
        if split:
            tensor = pick(tensor.reshape(z_size, 2, part_heads, head_dim), k, 1)
        else:
            tensor = lax.dynamic_slice_in_dim(tensor, k * (z_size // 2), z_size // 2, 0)
        tensor = tensor.reshape(heads, head_dim)
        return jnp.pad(tensor, ((0, 0), (0, PAD - head_dim)))

    query_shift = head_vector(part_by_z[:, :features])
    value_shift = head_vector(part_by_z[:, features : 2 * features])
    unit_shift = pick(part_by_z[:, 2 * features :].reshape(z_size, 2, half_units), k, 1).reshape(-1)

    all_lengths = jnp.concatenate(in_order(pieces_of(lengths, "k"), "k"))
    clip_length = pick(all_lengths, z, 0)

    quarter_slots = jnp.arange(quarter)
    own_valid = (y * 2 + k) * quarter + quarter_slots < clip_length
    slot_order = jnp.concatenate(
        [((y ^ dy) * 2 + (k ^ dk)) * quarter + quarter_slots for dy in range(y_size) for dk in range(2)]
    )
    key_mask = jnp.where(slot_order < clip_length, 0.0, MASKED)

    lane = jnp.arange(PAD)[None, :]
    none = jnp.zeros((heads, PAD), F32)
    is_first = jnp.broadcast_to(lane == head_dim, (heads, PAD)).astype(F32)
    is_extra = jnp.broadcast_to((lane >= head_dim) & (lane < head_dim + 2), (heads, PAD)).astype(F32)
    qkv_shift = jnp.concatenate([query_shift, none, value_shift]).reshape(1, -1)
    qkv_scale = jnp.concatenate([none + head_dim**-0.5 * LOG2E, none + 1, none + 1]).reshape(1, -1)
    qkv_extra = jnp.concatenate([is_first, none, -is_extra]).reshape(1, -1)
    mask_lane = jnp.concatenate([none, is_first, none]).reshape(1, -1)

    tokens = to_tokens(inputs).astype(F32)
    normal_one, scale_one, normed_part = norm_forward(tokens, gain_one, shift_one)
    normed_rows = gather_group(normed_part)
    grad_low = to_tokens(cotangent)
    grad_low = jnp.where(own_valid[:, None], grad_low, jnp.zeros_like(grad_low))
    grad_rows = gather_group(grad_low)
    grad_out = grad_low.astype(F32)

    packed = []
    for d, rows_d in enumerate(normed_rows):
        mask_d = key_mask[d * 2 * quarter : (d + 1) * 2 * quarter, None]
        product = (dot(rows_d, qkv_weights, 1, 1) + qkv_shift) * qkv_scale
        packed.append((product + qkv_extra + mask_d * mask_lane).astype(BF))
    packed = jnp.concatenate(packed, axis=0)
    block = slots // 2
    context, weights = attend(packed, heads, block)

    attn_part = reduce_group(
        [
            dot(context[d * 2 * quarter : (d + 1) * 2 * quarter], attn_weights, 1, 0)
            for d in range(y_size)
        ]
    )
    attn_part = attn_part + attn_shift
    middle = tokens + attn_part
    normal_two, scale_two, normed_two_part = norm_forward(middle, gain_two, shift_two)
    normed_two_rows = gather_group(normed_two_part)

    active_rows, grad_hidden_rows = [], []
    for rows_d, grad_d in zip(normed_two_rows, grad_rows):
        hidden = dot(rows_d, in_weights, 1, 1) + unit_shift
        below = 0.5 * (1.0 + lax.erf(hidden * 0.5**0.5))
        active_rows.append((hidden * below).astype(BF))
        slope = below + hidden * (jnp.exp(-0.5 * hidden * hidden) * (0.5 / jnp.pi) ** 0.5)
        grad_hidden_rows.append((dot(grad_d, out_weights, 1, 1) * slope).astype(BF))
    grad_normed_two = reduce_group([dot(g, in_weights, 1, 0) for g in grad_hidden_rows])
    grad_middle = grad_out + norm_backward(grad_normed_two, normal_two, scale_two, gain_two)
    grad_mid_part = grad_middle.astype(BF)
    grad_mid_rows = gather_group(grad_mid_part)

    normed = jnp.concatenate(normed_rows, axis=0)
    normed_two = jnp.concatenate(normed_two_rows, axis=0)
    active = jnp.concatenate(active_rows, axis=0)
    grad_hidden = jnp.concatenate(grad_hidden_rows, axis=0)
    grad_full = jnp.concatenate(grad_rows, axis=0)

    def reduce_weights(total):
        total = total.astype(BF)
        side = 2 * rows
        own = lax.dynamic_slice_in_dim(total, x * side, side, 1).astype(F32)
        for d in range(1, x_size):
            own = own + swap(lax.dynamic_slice_in_dim(total, (x ^ d) * side, side, 1), "x", d).astype(F32)
        own = own.reshape(z_size, -1, side)
        result = own[0]
        for d in range(1, z_size):
            result = result + swap(own[d].astype(BF), "z", d).astype(F32)
        return result

    def to_cores(total, parts):
        kept = lax.dynamic_slice_in_dim(total, k * rows, rows, 1)
        other = swap(lax.dynamic_slice_in_dim(total, (1 - k) * rows, rows, 1).astype(BF), "k").astype(F32)
        if not parts:
            return kept + other
        return jnp.stack(in_order([kept, other], "k"))

    out_total = reduce_weights(dot(active, grad_full, 0, 0))
    in_total = reduce_weights(dot(grad_hidden, normed_two, 0, 0))
    delta_part = reduce_group([dot(a, out_weights, 1, 0) for a in active_rows])
    delta = attn_part + delta_part + out_shift
    layer_out = inputs + from_tokens(delta).astype(F32)

    grad_mid_full = jnp.concatenate(grad_mid_rows, axis=0)
    grad_context = dot(grad_mid_full, attn_weights, 1, 1).astype(BF)
    grads = attend_back(packed, grad_context, context, weights, heads, head_dim, block)
    qkv_cube = qkv_weights.reshape(3, heads * PAD, width)
    grad_normed = reduce_group(
        [
            sum(dot(grads[j, d * 2 * quarter : (d + 1) * 2 * quarter], qkv_cube[j], 1, 0) for j in range(3))
            for d in range(y_size)
        ]
    )
    grad_tokens = norm_backward(grad_normed, normal_one, scale_one, gain_one)
    input_grad = from_tokens(grad_middle + grad_tokens).astype(F32)

    head_totals = [dot(grads[j], normed, 0, 0) for j in range(3)] + [dot(context, grad_mid_full, 0, 0)]
    head_totals = jnp.stack(head_totals).reshape(4, -1, part_heads, PAD, width)[:, :, :, :head_dim]
    head_totals = head_totals.transpose(1, 0, 2, 3, 4)
    if not split:
        blank = jnp.zeros((z_size,) + head_totals.shape[1:], F32)
        head_totals = lax.dynamic_update_slice_in_dim(blank, head_totals, k * (z_size // 2), 0)
    head_total = reduce_weights(head_totals.reshape(-1, width))
    head_blocks = to_cores(head_total, split).reshape(-1, 4, part_heads * head_dim, rows)
    grad_query_w, grad_key_w, grad_value_w, grad_attn_w = (
        head_blocks[:, j].reshape(features, rows) for j in range(4)
    )
    grad_in_w = to_cores(in_total, True).reshape(units, rows).T
    grad_out_w = to_cores(out_total, True).reshape(units, rows)

    full_sums = jnp.stack(
        [
            jnp.sum(v, axis=0)
            for v in (
                grad_normed * normal_one,
                grad_normed,
                grad_middle,
                grad_normed_two * normal_two,
                grad_normed_two,
                grad_out,
            )
        ]
    )

    def head_sums(tensor):
        total = jnp.sum(tensor.astype(F32), axis=0).reshape(-1, part_heads, PAD)[:, :, :head_dim]
        if not split:
            blank = jnp.zeros((z_size,) + total.shape[1:], F32)
            total = lax.dynamic_update_slice_in_dim(blank, total, k * (z_size // 2), 0)
        return total.reshape(z_size, -1)

    part_sums = jnp.concatenate(
        [
            head_sums(grads[0]),
            head_sums(grads[2]),
            jnp.sum(grad_hidden.astype(F32), axis=0).reshape(z_size, half_units),
        ],
        axis=1,
    )
    full_sums = full_sums.reshape(full_count, z_size, y_size, features).transpose(1, 2, 0, 3)
    flat = jnp.concatenate([full_sums.reshape(-1), part_sums.reshape(-1)])
    flat = sum(pieces_of(flat, "x"))
    full_cut = full_sums.size
    full_flat = flat[:full_cut].reshape(z_size, -1)
    part_flat = flat[full_cut:].reshape(z_size, -1)
    received = None
    for d in range(z_size):
        piece = jnp.concatenate([pick(full_flat, z ^ d, 0), part_flat[d]])
        received = piece if d == 0 else received + swap(piece, "z", d)
    cut = full_flat.shape[1]
    by_y = received[:cut].reshape(y_size, -1)
    mine = pick(by_y, y, 0)
    for d in range(1, y_size):
        mine = mine + swap(pick(by_y, y ^ d, 0), "y", d)
    last = jnp.concatenate([mine, received[cut:]])
    last_pair = [last, swap(last, "k")]
    own_size = mine.shape[0]
    vec_one_gain, vec_one_bias, vec_battn, vec_two_gain, vec_two_bias, vec_bout = (
        last_pair[0][:own_size] + last_pair[1][:own_size]
    ).reshape(full_count, features)
    head_size = part_heads * head_dim
    cores = in_order([p[own_size:] for p in last_pair], "k")
    if split:
        vec_bquery = jnp.concatenate([c[:head_size] for c in cores])
        vec_bvalue = jnp.concatenate([c[head_size : 2 * head_size] for c in cores])
    else:
        vec_bquery = cores[0][:head_size] + cores[1][:head_size]
        vec_bvalue = cores[0][head_size : 2 * head_size] + cores[1][head_size : 2 * head_size]
    vec_bin = jnp.concatenate([c[2 * head_size :] for c in cores])

    return (
        layer_out,
        input_grad,
        vec_one_gain,
        vec_one_bias,
        grad_query_w.T,
        vec_bquery,
        grad_key_w.T,
        grad_value_w.T,
        vec_bvalue,
        grad_attn_w,
        vec_battn,
        vec_two_gain,
        vec_two_bias,
        grad_in_w,
        vec_bin,
        grad_out_w,
        vec_bout,
    )


def solution(mesh):
    row_size, col_size = mesh.shape["row"], mesh.shape["col"]
    grid = Mesh(mesh.devices.reshape(row_size // 2, 2, 4, col_size // 4), ("x", "k", "z", "y"))
    row, col = ("x", "k"), ("z", "y")
    return jax.shard_map(
        local,
        mesh=grid,
        in_specs=(
            P(row, col),
            P(row),
            P(row, col),
            P(col),
            P(col),
            P(row, col),
            P(col),
            P(row, col),
            P(row, col),
            P(col),
            P(col, row),
            P(col),
            P(col),
            P(col),
            P(row, col),
            P(col),
            P(col, row),
            P(col),
        ),
        out_specs=(
            P(row, col),
            P(row, col),
            P(col),
            P(col),
            P(row, col),
            P(col),
            P(row, col),
            P(row, col),
            P(col),
            P(col, row),
            P(col),
            P(col),
            P(col),
            P(row, col),
            P(col),
            P(col, row),
            P(col),
        ),
        check_vma=False,
    )
```

```python
import functools

import jax
import jax.numpy as jnp
from jax import lax
from jax.experimental import pallas as pl
from jax.experimental.pallas import tpu as pltpu
from jax.sharding import Mesh
from jax.sharding import PartitionSpec as P

HEADS = 16
EPSILON = 1e-05
PAD = 128
LOG2E = 1.4426950408889634
LN2 = 0.6931471805599453
MASKED = -1e30
BF = jnp.bfloat16
F32 = jnp.float32


def dot(first, second, left, right):
    return lax.dot_general(
        first, second, (((left,), (right,)), ((), ())), preferred_element_type=F32
    )


GROUP = ("zl", "yl")


def size_of(axis):
    names = axis if isinstance(axis, tuple) else (axis,)
    total = 1
    for name in names:
        total *= lax.axis_size(name)
    return total


def swap(tensor, axis, step=1):
    return lax.ppermute(tensor, axis, [(i, i ^ step) for i in range(size_of(axis))])


def in_order(pieces, axis):
    mine = lax.axis_index(axis)
    if len(pieces) == 1:
        return pieces
    if len(pieces) == 2:
        return [lax.select_n((mine ^ j) == 1, *pieces) for j in range(2)]
    return [lax.select_n(mine ^ j, *pieces) for j in range(len(pieces))]


def pieces_of(tensor, axis):
    return [tensor] + [swap(tensor, axis, d) for d in range(1, size_of(axis))]


def pick(tensor, index, axis):
    return lax.dynamic_index_in_dim(tensor, index, axis, keepdims=False)


def sync(*values):
    return lax.optimization_barrier(values)


def far_pieces(part):
    return [swap(part, GROUP, d) for d in range(1, size_of(GROUP))]


def with_core(part):
    return jnp.concatenate([part, swap(part, "k")], axis=0)


def cores_sum(product, blocks):
    given = swap(product(blocks[1]).astype(BF), "k").astype(F32)
    return product(blocks[0]) + given


def send_far(sums):
    total = swap(sums[0].astype(BF), GROUP, 1).astype(F32)
    for d in range(2, len(sums) + 1):
        total = total + swap(sums[d - 1].astype(BF), GROUP, d).astype(F32)
    return total


def send_units(total, axis):
    return total[0], swap(total[1], axis)


def send_rows(total):
    x, count = lax.axis_index("x"), lax.axis_size("x")
    last = total.ndim - 1
    side = total.shape[last] // count
    parts = [lax.dynamic_slice_in_dim(total, (x ^ d) * side, side, last) for d in range(count)]
    return tuple(parts[:1] + [swap(parts[d], "x", d) for d in range(1, count)])


def summed(parts):
    return sum(p.astype(F32) for p in parts).astype(BF)


def join_body(pad_rows, x_ref, *refs):
    pieces, out_ref = refs[:-1], refs[-1]
    side = pieces[0].shape[-1]
    for d, piece in enumerate(pieces):
        for j in range(len(pieces)):

            @pl.when((x_ref[0] ^ d) == j)
            def _(piece=piece, j=j):
                columns = slice(j * side, (j + 1) * side)
                if not pad_rows:
                    out_ref[:, columns] = piece[...]
                    return
                count, head_dim = pad_rows
                for p in range(piece.shape[0]):
                    for h in range(count):
                        at = (p * count + h) * PAD
                        out_ref[at : at + head_dim, columns] = piece[p, 0, h * head_dim : (h + 1) * head_dim]
                        out_ref[at + head_dim : at + PAD, columns] = jnp.zeros((PAD - head_dim, side), BF)


def join_rows(pieces, in_spec, grid, out_block, pad_rows=None):
    width = pieces[0].shape[-1] * len(pieces)
    x = lax.axis_index("x").astype(jnp.int32).reshape(1)
    return pl.pallas_call(
        functools.partial(join_body, pad_rows),
        grid=(grid,),
        in_specs=[pl.BlockSpec(memory_space=pltpu.SMEM)] + [in_spec] * len(pieces),
        out_specs=pl.BlockSpec((out_block, width), lambda i: (i, 0)),
        out_shape=jax.ShapeDtypeStruct((grid * out_block, width), BF),
        compiler_params=pltpu.CompilerParams(vmem_limit_bytes=32 * 2**20),
        cost_estimate=pl.CostEstimate(flops=0, bytes_accessed=8 * pieces[0].size * len(pieces), transcendentals=0),
    )(x, *pieces)


def first_rows(slot, clips):
    return [[(slot * c - j + 7) // 8 for j in range(8)] for c in range(clips + 1)]


def take_body(starts, lanes, lines, packed_ref, out_ref, low):
    part = pl.program_id(0)
    count, packed_width = packed_ref.shape
    features = packed_width // 8
    choices = [(c, n) for c, row in enumerate(starts) for n in range(len(row))]

    @pl.when(part == 0)
    def _():
        packed = packed_ref[...].astype(F32)
        tail = max(row[-1][0] for row in starts) + lines - count
        packed = jnp.concatenate([packed, jnp.zeros((tail + -(tail + count) % 8, packed_width), F32)], axis=0)
        for at, (c, n) in enumerate(choices):
            start = starts[c][n][0]
            low[at] = packed[start : start + lines].astype(BF)

    source = lax.broadcasted_iota(jnp.int32, (packed_width, features), 0)
    target = lax.broadcasted_iota(jnp.int32, (packed_width, features), 1)
    for clip, row in enumerate(starts):
        taken = []
        for lane in range(lanes):
            position = part * lanes + lane
            choose = jnp.where(source == target * 8 + position, 1.0, 0.0).astype(BF)
            at = choices.index((clip, 0))
            for n in range(1, len(row)):
                at = jnp.where(position < row[n][1], choices.index((clip, n)), at)
            taken.append(dot(choose, low[at], 0, 1))
        out_ref[0, clip, 0] = jnp.concatenate(taken, axis=1).astype(BF)


def starts_by_clip(slot, clips):
    result = []
    for row in first_rows(slot, clips)[:-1]:
        result.append([(value, sum(v >= value for v in row)) for value in sorted(set(row))])
    return result


def take_positions(packed, slot, clips, lanes, lines):
    count, packed_width = packed.shape
    features = packed_width // 8
    starts = starts_by_clip(slot, clips)
    chips = 8 // (2 * lanes)
    return pl.pallas_call(
        functools.partial(take_body, starts, lanes, lines),
        grid=(8 // lanes,),
        in_specs=[pl.BlockSpec((count, packed_width), lambda j: (0, 0))],
        out_specs=pl.BlockSpec((1, clips, 1, features, lanes * lines), lambda j: (j % 2, 0, j // 2, 0, 0)),
        out_shape=jax.ShapeDtypeStruct((2, clips, chips, features, lanes * lines), BF),
        scratch_shapes=[pltpu.VMEM((sum(len(r) for r in starts), lines, packed_width), BF)],
        compiler_params=pltpu.CompilerParams(vmem_limit_bytes=32 * 2**20),
        cost_estimate=pl.CostEstimate(
            flops=4 * count * packed_width**2, bytes_accessed=8 * count * packed_width, transcendentals=0
        ),
    )(packed)


def put_body(rows, lanes, lines, added, *refs):
    base_ref, tokens_ref, out_ref, total = refs if added else (None,) + refs
    half = pl.program_id(0)
    count, packed_width = out_ref.shape
    features = packed_width // 8
    chips = tokens_ref.shape[2]
    source = lax.broadcasted_iota(jnp.int32, (4 * features, packed_width), 0)
    target = lax.broadcasted_iota(jnp.int32, (4 * features, packed_width), 1)
    position = source // features
    wanted = (source - position * features) * 8 + position + 4 * half
    choose = jnp.where(wanted == target, 1.0, 0.0).astype(BF)
    line = lax.broadcasted_iota(jnp.int32, (lines, 1), 0)

    @pl.when(half == 0)
    def _():
        total[...] = jnp.zeros_like(total)

    for clip in range(len(rows) - 1):
        blocks = [
            tokens_ref[core, clip, chip][:, lane * lines : (lane + 1) * lines]
            for chip in range(chips)
            for core in range(2)
            for lane in range(lanes)
        ]
        placed = dot(jnp.concatenate(blocks, axis=0), choose, 0, 0)
        for h in range(2):
            start, stop = rows[clip][4 * h], rows[clip + 1][4 * h]

            @pl.when(half == h)
            def _(start=start, stop=stop, placed=placed):
                total[start : start + lines] += jnp.where(line < stop - start, placed, 0.0)

    @pl.when(half == 1)
    def _():
        out_ref[...] = total[:count] + base_ref[...] if added else total[:count]


def put_positions(tokens, slot, count, lanes, lines, base=None):
    _, clips, chips, features, quarter = tokens.shape
    packed_width = features * 8
    rows = first_rows(slot, clips)
    assert all(len(set(row[:4])) == 1 and len(set(row[4:])) == 1 for row in rows)
    whole = pl.BlockSpec((count, packed_width), lambda h: (0, 0))
    in_specs = [pl.BlockSpec((2, clips, chips // 2, features, quarter), lambda h: (0, 0, h, 0, 0))]
    given = [tokens]
    if base is not None:
        in_specs, given = [whole] + in_specs, [base] + given
    last = max(max(row) for row in rows[:-1]) + lines
    return pl.pallas_call(
        functools.partial(put_body, rows, lanes, lines, base is not None),
        grid=(2,),
        in_specs=in_specs,
        out_specs=whole,
        out_shape=jax.ShapeDtypeStruct((count, packed_width), F32),
        scratch_shapes=[pltpu.VMEM((-(-last // 16) * 16, packed_width), F32)],
        compiler_params=pltpu.CompilerParams(vmem_limit_bytes=40 * 2**20),
        cost_estimate=pl.CostEstimate(
            flops=4 * count * packed_width**2, bytes_accessed=8 * count * packed_width, transcendentals=0
        ),
    )(*given)


def forward_body(query_ref, key_ref, value_ref, context_ref, wide_ref, weights_ref):
    scores = dot(key_ref[...], query_ref[...], 1, 1)
    top = jnp.max(scores, axis=0, keepdims=True)
    powers = jnp.exp2(scores - top)
    total = jnp.sum(powers, axis=0, keepdims=True)
    weights = (powers * (1.0 / total)).astype(BF)
    weights_ref[0] = weights
    context = dot(value_ref[...], weights, 0, 0).T
    context_ref[...] = context.astype(BF)
    wide_ref[...] = context


def attend(packed, heads, part):
    slots = packed.shape[0]
    block = slots // 2
    return pl.pallas_call(
        forward_body,
        grid=(heads,),
        in_specs=[
            pl.BlockSpec((block, PAD), lambda h: (part, h)),
            pl.BlockSpec((slots, PAD), lambda h: (0, heads + h)),
            pl.BlockSpec((slots, PAD), lambda h: (0, 2 * heads + h)),
        ],
        out_specs=[
            pl.BlockSpec((block, PAD), lambda h: (0, h)),
            pl.BlockSpec((block, PAD), lambda h: (0, h)),
            pl.BlockSpec((1, slots, block), lambda h: (h, 0, 0)),
        ],
        out_shape=[
            jax.ShapeDtypeStruct((block, heads * PAD), BF),
            jax.ShapeDtypeStruct((block, heads * PAD), F32),
            jax.ShapeDtypeStruct((heads, slots, block), BF),
        ],
        compiler_params=pltpu.CompilerParams(vmem_limit_bytes=50 * 2**20),
        cost_estimate=pl.CostEstimate(
            flops=heads * slots * slots * PAD * 6,
            bytes_accessed=heads * slots * slots,
            transcendentals=heads * slots * block,
        ),
    )(packed, packed, packed)


def backward_part(head_dim, query, key, value, grad, context, weights):
    wide = grad.astype(F32)
    inner = jnp.sum(wide * context, axis=1, keepdims=True)
    inner_high = inner.astype(BF).astype(F32)
    lane = lax.broadcasted_iota(jnp.int32, grad.shape, 1)
    extended = jnp.where(
        lane == head_dim,
        inner_high,
        jnp.where(lane == head_dim + 1, inner - inner_high, wide),
    ).astype(BF)
    centered = dot(value, extended, 1, 1)
    grad_scores = (weights.astype(F32) * centered).astype(BF)
    grad_value = dot(weights, grad, 1, 0)
    grad_key = dot(grad_scores, query, 1, 0)
    grad_query = (dot(key, grad_scores, 0, 0) * head_dim**-0.5).T
    return grad_query.astype(BF), grad_key, grad_value


def first_body(head_dim, query, key, value, grad, context, weights, query_out, key_out, value_out):
    query_out[...], key_out[...], value_out[...] = backward_part(
        head_dim, query[...], key[...], value[...], grad[...], context[...], weights[0]
    )


def second_body(
    head_dim, query, key, value, grad, context, weights, first_query, first_key, first_value, out_ref
):
    grad_query, grad_key, grad_value = backward_part(
        head_dim, query[...], key[...], value[...], grad[...], context[...], weights[0]
    )
    block = grad_query.shape[0]
    out_ref[0, :block] = first_query[...]
    out_ref[0, block:] = grad_query
    out_ref[1] = ((grad_key + first_key[...]) * LN2).astype(BF)
    out_ref[2] = (grad_value + first_value[...]).astype(BF)


def attend_back(packed, grad_context, context, weights, heads, head_dim, part, first=None):
    slots = packed.shape[0]
    block = slots // 2
    half = pl.BlockSpec((block, PAD), lambda h: (0, h))
    whole = pl.BlockSpec((slots, PAD), lambda h: (0, h))
    in_specs = [
        pl.BlockSpec((block, PAD), lambda h: (part, h)),
        pl.BlockSpec((slots, PAD), lambda h: (0, heads + h)),
        pl.BlockSpec((slots, PAD), lambda h: (0, 2 * heads + h)),
        half,
        half,
        pl.BlockSpec((1, slots, block), lambda h: (h, 0, 0)),
    ]
    given = [packed, packed, packed, grad_context, context, weights]
    if first is None:
        body = first_body
        out_specs = [half, whole, whole]
        out_shape = [
            jax.ShapeDtypeStruct((block, heads * PAD), BF),
            jax.ShapeDtypeStruct((slots, heads * PAD), F32),
            jax.ShapeDtypeStruct((slots, heads * PAD), F32),
        ]
    else:
        body = second_body
        in_specs += [half, whole, whole]
        given += first
        out_specs = pl.BlockSpec((3, slots, PAD), lambda h: (0, 0, h))
        out_shape = jax.ShapeDtypeStruct((3, slots, heads * PAD), BF)
    return pl.pallas_call(
        functools.partial(body, head_dim),
        grid=(heads,),
        in_specs=in_specs,
        out_specs=out_specs,
        out_shape=out_shape,
        compiler_params=pltpu.CompilerParams(vmem_limit_bytes=56 * 2**20),
        cost_estimate=pl.CostEstimate(
            flops=heads * slots * slots * PAD * 8,
            bytes_accessed=heads * slots * slots,
            transcendentals=0,
        ),
    )(*given)


def norm_forward(tensor, gain, shift):
    centered = tensor - jnp.mean(tensor, axis=1, keepdims=True)
    scale = lax.rsqrt(jnp.mean(centered * centered, axis=1, keepdims=True) + EPSILON)
    normal = centered * scale
    return normal, scale, (normal * gain + shift).astype(BF)


def norm_backward(grad, normal, scale, gain):
    weighted = grad * gain
    return scale * (
        weighted
        - jnp.mean(weighted, axis=1, keepdims=True)
        - normal * jnp.mean(weighted * normal, axis=1, keepdims=True)
    )


def local(
    inputs,
    lengths,
    cotangent,
    ln1_gain,
    ln1_bias,
    w_query,
    b_query,
    w_key,
    w_value,
    b_value,
    w_attn_out,
    b_attn_out,
    ln2_gain,
    ln2_bias,
    w_in,
    b_in,
    w_out,
    b_out,
):
    chips = size_of(GROUP)
    yl_size = lax.axis_size("yl")
    columns = 8 * yl_size
    k, zh, yh = (lax.axis_index(a) for a in ("k", "zh", "yh"))
    chip = lax.axis_index(GROUP)
    pack_count, packed_width = inputs.shape
    features = packed_width // 8
    width = features * columns
    clips = lengths.shape[0]
    slot = pack_count * 8 // clips
    group = 2 * chips
    lines = -(-(slot // 8 + 1) // 64) * 64
    lanes = 8 // group
    quarter = lanes * lines
    slots = 8 * lines
    half = slots // 2
    rows = w_query.shape[0]
    block_heads = HEADS // columns
    head_dim = width // HEADS
    split = block_heads % 2 == 0
    part_heads = block_heads // 2 if split else block_heads
    heads = 2 * block_heads
    units = w_in.shape[1]
    half_units = units // 2

    def start_of(clip, j):
        return (slot * clip - j + 7) // 8

    def order_tokens(own, other):
        ordered = jnp.stack(in_order([own, other], "k")).reshape(2, 2, 2, yl_size, features, quarter)
        return ordered.transpose(0, 2, 1, 3, 4, 5).reshape(columns, features, quarter)

    def exchange(blocks):
        return lax.all_to_all(blocks, ("zh", "zl", "yh", "yl"), 0, 0)

    def join(moved):
        return moved.reshape(width, quarter).T

    def cut(tensor):
        return tensor.T.reshape(columns, features, quarter)

    def by_core(tensor, parts):
        if not parts:
            return jnp.broadcast_to(tensor[None], (2,) + tensor.shape)
        return tensor.reshape((2, tensor.shape[0] // 2) + tensor.shape[1:])

    def double(part, axis):
        return part, swap(part, axis)

    def stacked(parts):
        return jnp.stack(parts)

    def arrange_heads(pieces):
        if not split:
            pieces = [lax.dynamic_slice_in_dim(p, k * (p.shape[0] // 2), p.shape[0] // 2, 0) for p in pieces]
        pieces = [p.reshape(-1, 4, part_heads * head_dim, 2 * rows) for p in pieces]
        block = (pieces[0].shape[0], 1) + pieces[0].shape[2:]
        return join_rows(
            pieces, pl.BlockSpec(block, lambda i: (0, i, 0, 0)), 4, heads * PAD, (part_heads, head_dim)
        )

    def arrange_units(pieces):
        return join_rows(pieces, pl.BlockSpec((half_units, 2 * rows), lambda i: (i, 0)), 4, half_units)

    full_vectors = jnp.stack([ln1_gain, ln1_bias, ln2_gain, ln2_bias, b_attn_out, b_out])
    part_vector = jnp.concatenate([b_query, b_value, b_in])
    full_count = full_vectors.shape[0]
    full_by = jnp.stack(in_order(pieces_of(full_vectors, GROUP), GROUP))
    all_lengths = jnp.concatenate(in_order(pieces_of(lengths, "k"), "k"))

    turned = [t.astype(BF).T for t in (w_query, w_key, w_value)] + [w_attn_out.astype(BF)]
    head_parts = jnp.stack([by_core(t, split) for t in turned], axis=1)
    head_parts = head_parts.reshape(2, 4 * part_heads * head_dim, rows)
    size = head_parts.shape[1]
    own_parts, other_parts = pick(head_parts, k, 0), swap(pick(head_parts, 1 - k, 0), "k")
    inputs_then, own_parts, full_by = sync(inputs, own_parts, full_by)
    full_size = full_by.size
    vector_pieces = pieces_of(jnp.concatenate([full_by.reshape(-1), part_vector]), "zh")
    taken = take_positions(inputs_then, slot, clips, lanes, lines)
    taken, vector_pieces = sync(taken, vector_pieces)
    full_by = jnp.stack(in_order([p[:full_size] for p in vector_pieces], "zh"))
    part_by = jnp.stack([p[full_size:] for p in vector_pieces])
    full_size = full_by.size
    vector_pieces = pieces_of(jnp.concatenate([full_by.reshape(-1), part_by.reshape(-1)]), "yh")
    own_tokens, other_tokens = pick(taken, k, 0), swap(pick(taken, 1 - k, 0), "k")
    head_shard = jnp.concatenate(in_order([own_parts, other_parts], "k"), axis=1)
    ordered, head_shard, vector_pieces = sync(order_tokens(own_tokens, other_tokens), head_shard, vector_pieces)
    head_pair = double(head_shard, "zh")
    moved = exchange(ordered)

    ordered, cotangent, w_in, w_out = sync(ordered, cotangent, w_in, w_out)
    unit_parts = jnp.stack([by_core(w_in.astype(BF).T, True), by_core(w_out.astype(BF), True)], axis=1)
    unit_parts = unit_parts.reshape(2, units, rows)
    own_parts, other_parts = pick(unit_parts, k, 0), swap(pick(unit_parts, 1 - k, 0), "k")
    own_parts, cotangent, head_pair = sync(own_parts, cotangent, head_pair)
    head_pair = double(stacked(head_pair), "yh")
    taken = take_positions(cotangent, slot, clips, lanes, lines)
    own_tokens, other_tokens = pick(taken, k, 0), swap(pick(taken, 1 - k, 0), "k")
    unit_shard = jnp.concatenate(in_order([own_parts, other_parts], "k"), axis=1)
    unit_shard = unit_shard.reshape(2, half_units, 2 * rows)
    ordered_grads = order_tokens(own_tokens, other_tokens)

    full_by = jnp.stack(in_order([p[:full_size] for p in vector_pieces], "yh"))
    part_by = jnp.stack([p[full_size:].reshape(part_by.shape) for p in vector_pieces]).reshape(4, -1)
    full_by = full_by.reshape(2, 2, 2, yl_size, full_count, features).transpose(4, 1, 2, 0, 3, 5)
    gain_one, shift_one, gain_two, shift_two, attn_shift, out_shift = full_by.reshape(full_count, 1, width)

    def head_vector(tensor):
        tensor = tensor.reshape(4, block_heads, head_dim)
        if split:
            tensor = pick(tensor.reshape(4, 2, part_heads, head_dim), k, 1)
        else:
            tensor = lax.dynamic_slice_in_dim(tensor, 2 * k, 2, 0)
        tensor = tensor.reshape(heads, head_dim)
        return jnp.pad(tensor, ((0, 0), (0, PAD - head_dim)))

    query_shift = head_vector(part_by[:, :features])
    value_shift = head_vector(part_by[:, features : 2 * features])
    unit_shift = pick(part_by[:, 2 * features :].reshape(4, 2, half_units), k, 1).reshape(-1)

    clip_length = pick(all_lengths, zh * 2 + yh, 0)

    def slots_of(part):
        j = part * lanes + jnp.repeat(jnp.arange(lanes), lines)
        return 8 * (start_of(yh, j) + jnp.tile(jnp.arange(lines), lanes)) + j - slot * yh

    own_valid = slots_of(chip * 2 + k) < clip_length
    slot_order = jnp.concatenate([slots_of((chip ^ d) * 2 + (k ^ c)) for d in range(chips) for c in range(2)])
    key_mask = jnp.where(slot_order < clip_length, 0.0, MASKED)

    lane = jnp.arange(PAD)[None, :]
    none = jnp.zeros((heads, PAD), F32)
    is_first = jnp.broadcast_to(lane == head_dim, (heads, PAD)).astype(F32)
    is_extra = jnp.broadcast_to((lane >= head_dim) & (lane < head_dim + 2), (heads, PAD)).astype(F32)
    qkv_shift = jnp.concatenate([query_shift, none, value_shift]).reshape(1, -1)
    qkv_scale = jnp.concatenate([none + head_dim**-0.5 * LOG2E, none + 1, none + 1]).reshape(1, -1)
    qkv_extra = jnp.concatenate([is_first, none, -is_extra]).reshape(1, -1)
    mask_lane = jnp.concatenate([none, is_first, none]).reshape(1, -1)

    def blocks_of(tensor):
        count = tensor.shape[0] // (2 * quarter)
        return [
            [tensor[(2 * d + c) * quarter : (2 * d + c + 1) * quarter] for c in range(2)]
            for d in range(count)
        ]

    moved, ordered_grads, unit_shard, gain_one, shift_one = sync(
        moved, ordered_grads, unit_shard, gain_one, shift_one
    )
    tokens = join(moved).astype(F32)
    normal_one, scale_one, normed_part = norm_forward(tokens, gain_one, shift_one)
    tokens, normal_one, scale_one, normed_part, head_pair = sync(
        tokens, normal_one, scale_one, normed_part, head_pair
    )
    normed_far = far_pieces(normed_part)
    head_pieces = pieces_of(stacked(head_pair).reshape(4 * size, 2 * rows), "x")
    in_pair = double(unit_shard[0], "zh")
    normed_near = with_core(normed_part)
    normed_near, in_pair = sync(normed_near, in_pair)
    in_pair = double(stacked(in_pair), "yh")
    out_pair = double(unit_shard[1], "zh")
    normed_near, normed_far, in_pair = sync(normed_near, normed_far, in_pair)
    in_pieces = pieces_of(stacked(in_pair).reshape(4 * half_units, 2 * rows), "x")
    head_pieces, normed_near, ordered_grads, out_pair = sync(head_pieces, normed_near, ordered_grads, out_pair)
    out_pair = double(stacked(out_pair), "yh")
    moved_grads = exchange(ordered_grads)
    head_weights = arrange_heads(head_pieces).reshape(4, heads * PAD, width)
    qkv_weights = head_weights[:3].reshape(3 * heads * PAD, width)
    attn_weights = head_weights[3]

    def qkv(rows_d, d):
        mask_d = key_mask[d * 2 * quarter : (d + 1) * 2 * quarter, None]
        product = (dot(rows_d, qkv_weights, 1, 1) + qkv_shift) * qkv_scale
        return (product + qkv_extra + mask_d * mask_lane).astype(BF)

    packed_near = qkv(normed_near, 0)
    normed_rows = [normed_near] + [with_core(v) for v in normed_far]
    packed = jnp.concatenate(
        [packed_near] + [qkv(v, d) for d, v in enumerate(normed_rows) if d], axis=0
    )
    far_context, far_wide, far_weights = attend(packed, heads, 1)

    def attn_product(v):
        return dot(v, attn_weights, 1, 0)

    near_chips = chips // 2
    far_sums = [cores_sum(attn_product, b).astype(BF) for b in blocks_of(far_context)]
    far_sums, packed, moved_grads = sync(far_sums, packed, moved_grads)
    far_total = send_far(far_sums) if near_chips == 1 else None
    near_context, near_wide, near_weights = attend(packed, heads, 0)
    grad_low = jnp.where(own_valid[:, None], join(moved_grads), jnp.zeros((quarter, width), BF))
    near_context, grad_low, far_total, out_pair = sync(near_context, grad_low, far_total, out_pair)
    out_pieces = pieces_of(stacked(out_pair).reshape(4 * half_units, 2 * rows), "x")
    near_sums = [cores_sum(attn_product, b) for b in blocks_of(near_context)]
    if near_chips > 1:
        far_total = send_far((near_sums + far_sums)[1:])
    near_sums, far_total, in_pieces = sync(near_sums, far_total, in_pieces)
    grad_far = far_pieces(grad_low)
    grad_near = with_core(grad_low)
    attn_part = near_sums[0] + far_total + attn_shift
    middle = tokens + attn_part
    normal_two, scale_two, normed_two_part = norm_forward(middle, gain_two, shift_two)
    normal_two, scale_two, normed_two_part, grad_near = sync(normal_two, scale_two, normed_two_part, grad_near)
    two_near = with_core(normed_two_part)
    two_far = far_pieces(normed_two_part)
    in_weights = arrange_units(in_pieces)

    def feed(rows_d):
        hidden = dot(rows_d, in_weights, 1, 1) + unit_shift
        below = 0.5 * (1.0 + lax.erf(hidden * 0.5**0.5))
        slope = below + hidden * (jnp.exp(-0.5 * hidden * hidden) * (0.5 / jnp.pi) ** 0.5)
        return (hidden * below).astype(BF), slope

    def feed_back(grad_d, slope):
        return (dot(grad_d, out_weights, 1, 1) * slope).astype(BF)

    near_active, near_slope = feed(two_near)
    near_active, near_slope, two_far = sync(near_active, near_slope, two_far)
    two_rows = [two_near] + [with_core(v) for v in two_far]
    far_feed = [feed(v) for v in two_rows[1:]]
    near_slope, far_feed, out_pieces, grad_far = sync(near_slope, far_feed, out_pieces, grad_far)
    out_weights = arrange_units(out_pieces)
    grad_rows = [grad_near] + [with_core(v) for v in grad_far]
    near_hidden = feed_back(grad_near, near_slope)
    grad_hidden = jnp.concatenate(
        [near_hidden] + [feed_back(g, f[1]) for g, f in zip(grad_rows[1:], far_feed)], axis=0
    )
    active = jnp.concatenate([near_active] + [f[0] for f in far_feed], axis=0)

    def in_product(v):
        return dot(v, in_weights, 1, 0)

    hidden_blocks = blocks_of(grad_hidden)
    far_two = [cores_sum(in_product, b).astype(BF) for b in hidden_blocks[1:]]
    grad_hidden, near_blocks, far_two, active = sync(grad_hidden, hidden_blocks[0], far_two, active)
    near_two = cores_sum(in_product, near_blocks)
    normed = jnp.concatenate(normed_rows, axis=0)
    normed_two = jnp.concatenate(two_rows, axis=0)
    grad_full = jnp.concatenate(grad_rows, axis=0)
    out_total = dot(active, grad_full, 0, 0).astype(BF)
    out_total, grad_hidden, near_two = sync(out_total, grad_hidden, near_two)
    out_half = send_units(out_total.reshape(2, -1, width), "yh")
    in_total = dot(grad_hidden, normed_two, 0, 0).astype(BF)
    in_total, near_two = sync(in_total, near_two)
    in_half = send_rows(in_total)
    grad_two = near_two + send_far(far_two)
    grad_out = grad_low.astype(F32)
    grad_middle = grad_out + norm_backward(grad_two, normal_two, scale_two, gain_two)
    grad_mid_part = grad_middle.astype(BF)
    grad_middle, grad_mid_part, active, grad_two = sync(grad_middle, grad_mid_part, active, grad_two)
    mid_far = far_pieces(grad_mid_part)
    mid_near = with_core(grad_mid_part)

    def context_grad(v):
        return dot(v, attn_weights, 1, 1).astype(BF)

    def out_product(v):
        return dot(v, out_weights, 1, 0)

    active_blocks = blocks_of(active)
    far_delta = [cores_sum(out_product, b).astype(BF) for b in active_blocks[1:]]
    near_delta = cores_sum(out_product, active_blocks[0])
    mid_half = jnp.concatenate([mid_near] + [with_core(v) for v in mid_far[: near_chips - 1]], axis=0)
    near_grad = context_grad(mid_half)
    near_grad, far_delta, near_delta = sync(near_grad, far_delta, near_delta)
    first = attend_back(packed, near_grad, near_wide, near_weights, heads, head_dim, 0)
    first, mid_far, out_half, in_half, far_delta = sync(first, mid_far, out_half, in_half, far_delta)
    delta_far = send_far(far_delta)
    out_half = send_rows(summed(out_half))
    in_half = send_units(summed(in_half).reshape(2, -1, 2 * rows), "yh")
    mid_rows = [mid_near] + [with_core(v) for v in mid_far]
    mid_full = jnp.concatenate(mid_rows, axis=0)
    far_grad = context_grad(mid_full[half:])
    grads = attend_back(packed, far_grad, far_wide, far_weights, heads, head_dim, 1, list(first))
    qkv_cube = qkv_weights.reshape(3, heads * PAD, width)

    def qkv_product(v):
        return sum(dot(v[j], qkv_cube[j], 1, 0) for j in range(3))

    grad_blocks = [
        [grads[:, (2 * d + c) * quarter : (2 * d + c + 1) * quarter] for c in range(2)] for d in range(chips)
    ]
    far_one = [cores_sum(qkv_product, b).astype(BF) for b in grad_blocks[1:]]
    grads, far_one, near_blocks, delta_far = sync(grads, far_one, grad_blocks[0], delta_far)
    far_arrived = send_far(far_one)
    near_one = cores_sum(qkv_product, near_blocks)
    delta = (attn_part + near_delta + delta_far + out_shift).astype(BF)
    moved_delta = exchange(cut(delta))

    def trim(total):
        return total.reshape(-1, part_heads, PAD, width)[:, :, :head_dim].reshape(-1, part_heads * head_dim, width)

    def head_chunk(totals):
        chunk = jnp.stack([trim(t) for t in totals], axis=1).reshape(-1, len(totals) * part_heads * head_dim, width)
        if not split:
            blank = jnp.zeros((4,) + chunk.shape[1:], BF)
            chunk = lax.dynamic_update_slice_in_dim(blank, chunk, 2 * k, 0)
        return chunk.reshape((2, 2) + chunk.shape[1:])

    context = jnp.concatenate([near_context, far_context], axis=0)
    query_key = head_chunk([dot(grads[j], normed, 0, 0).astype(BF) for j in range(2)])
    query_key, grads, near_one, far_arrived, out_half, in_half = sync(
        query_key, grads, near_one, far_arrived, out_half, in_half
    )
    grad_one = near_one + far_arrived
    grad_tokens = norm_backward(grad_one, normal_one, scale_one, gain_one)
    last_part = (grad_middle + grad_tokens).astype(BF)
    last_blocks, grad_one, moved_delta, query_key, grads, out_half, in_half = sync(
        cut(last_part), grad_one, moved_delta, query_key, grads, out_half, in_half
    )
    moved_last = exchange(last_blocks)
    query_key_half = send_rows(query_key)
    value_attn = head_chunk([dot(grads[2], normed, 0, 0).astype(BF), dot(context, mid_full, 0, 0).astype(BF)])
    value_attn, out_half, in_half, moved_delta = sync(value_attn, out_half, in_half, moved_delta)
    value_attn_half = send_units(value_attn, "yh")
    out_half = send_units(summed(out_half).reshape(2, -1, 2 * rows), "zh")
    in_half = send_units(summed(in_half).reshape(2, -1, 2 * rows), "zh")

    def two_cores(total, two):
        kept = lax.dynamic_slice_in_dim(total, k * rows, rows, 1)
        other = swap(lax.dynamic_slice_in_dim(total, (1 - k) * rows, rows, 1), "k")
        if not two:
            return kept.astype(F32) + other.astype(F32)
        return jnp.stack(in_order([kept, other], "k")).astype(F32)

    def kept_tokens(moved):
        moved = moved.reshape(2, 2, 2, yl_size, features, quarter).transpose(0, 2, 1, 3, 4, 5)
        kept = pick(moved, k, 0)
        other = swap(pick(moved, 1 - k, 0), "k")
        ordered = jnp.stack(in_order([kept, other], "k"))
        return ordered.reshape(2, clips, chips, features, quarter)

    def put(tokens, base=None):
        return put_positions(tokens, slot, pack_count, lanes, lines, base)

    layer_out = put(kept_tokens(moved_delta), inputs)
    layer_out, query_key_half, moved_last, grad_one = sync(layer_out, query_key_half, moved_last, grad_one)
    query_key_half = send_units(summed(query_key_half), "yh")
    input_grad = put(kept_tokens(moved_last))
    input_grad, value_attn_half, query_key_half, out_half, in_half = sync(
        input_grad, value_attn_half, query_key_half, out_half, in_half
    )
    value_attn_half = send_rows(summed(value_attn_half))
    query_key_half = send_units(summed(query_key_half), "zh")
    grad_out_w = two_cores(summed(out_half), True).reshape(units, rows)
    grad_in_w = two_cores(summed(in_half), True).reshape(units, rows).T
    grad_out_w, grad_in_w, value_attn_half = sync(grad_out_w, grad_in_w, value_attn_half)
    value_attn_half = send_units(summed(value_attn_half), "zh")
    head_parts = [
        two_cores(summed(t), split).reshape(-1, 2, part_heads * head_dim, rows)
        for t in (query_key_half, value_attn_half)
    ]
    grad_query_w, grad_key_w, grad_value_w, grad_attn_w = (
        t[:, j].reshape(features, rows) for t in head_parts for j in range(2)
    )

    full_sums = jnp.stack(
        [
            jnp.sum(v, axis=0)
            for v in (
                grad_one * normal_one,
                grad_one,
                grad_middle,
                grad_two * normal_two,
                grad_two,
                grad_out,
            )
        ]
    )

    def head_sums(tensor):
        total = jnp.sum(tensor.astype(F32), axis=0).reshape(-1, part_heads, PAD)[:, :, :head_dim]
        if not split:
            blank = jnp.zeros((4,) + total.shape[1:], F32)
            total = lax.dynamic_update_slice_in_dim(blank, total, 2 * k, 0)
        return total.reshape(4, -1)

    part_sums = jnp.concatenate(
        [
            head_sums(grads[0]),
            head_sums(grads[2]),
            jnp.sum(grad_hidden.astype(F32), axis=0).reshape(4, half_units),
        ],
        axis=1,
    )
    full_sums = full_sums.reshape(full_count, 2, 2, 2, yl_size, features).transpose(3, 1, 2, 4, 0, 5)
    full_size = full_sums.size
    flat = jnp.concatenate([full_sums.reshape(-1), part_sums.reshape(-1)])
    flat = sum(pieces_of(flat, "x"))
    full_flat, part_flat = flat[:full_size], flat[full_size:]
    for axis, index in (("yh", yh), ("zh", zh)):
        full_flat, part_flat = full_flat.reshape(2, -1), part_flat.reshape(2, -1)
        given = swap(jnp.concatenate([pick(full_flat, 1 - index, 0), part_flat[1]]), axis)
        cut_at = full_flat.shape[1]
        full_flat = pick(full_flat, index, 0) + given[:cut_at]
        part_flat = part_flat[0] + given[cut_at:]
    by_chip = full_flat.reshape(chips, -1)
    mine = pick(by_chip, chip, 0)
    for d in range(1, chips):
        mine = mine + swap(pick(by_chip, chip ^ d, 0), GROUP, d)
    own_size = mine.shape[0]
    last_pair = pieces_of(jnp.concatenate([mine, part_flat]), "k")
    vec_one_gain, vec_one_bias, vec_battn, vec_two_gain, vec_two_bias, vec_bout = (
        last_pair[0][:own_size] + last_pair[1][:own_size]
    ).reshape(full_count, features)
    head_size = part_heads * head_dim
    cores = in_order([p[own_size:] for p in last_pair], "k")
    if split:
        vec_bquery = jnp.concatenate([c[:head_size] for c in cores])
        vec_bvalue = jnp.concatenate([c[head_size : 2 * head_size] for c in cores])
    else:
        vec_bquery = cores[0][:head_size] + cores[1][:head_size]
        vec_bvalue = cores[0][head_size : 2 * head_size] + cores[1][head_size : 2 * head_size]
    vec_bin = jnp.concatenate([c[2 * head_size :] for c in cores])

    return (
        layer_out,
        input_grad,
        vec_one_gain,
        vec_one_bias,
        grad_query_w.T,
        vec_bquery,
        grad_key_w.T,
        grad_value_w.T,
        vec_bvalue,
        grad_attn_w,
        vec_battn,
        vec_two_gain,
        vec_two_bias,
        grad_in_w,
        vec_bin,
        grad_out_w,
        vec_bout,
    )


def solution(mesh):
    row_size, col_size = mesh.shape["row"], mesh.shape["col"]
    shape = (row_size // 2, 2, 2, 2, 2, col_size // 8)
    row, col = ("x", "k"), ("zh", "zl", "yh", "yl")
    grid = Mesh(mesh.devices.reshape(shape), row + col)
    return jax.shard_map(
        local,
        mesh=grid,
        in_specs=(
            P(row, col),
            P(row),
            P(row, col),
            P(col),
            P(col),
            P(row, col),
            P(col),
            P(row, col),
            P(row, col),
            P(col),
            P(col, row),
            P(col),
            P(col),
            P(col),
            P(row, col),
            P(col),
            P(col, row),
            P(col),
        ),
        out_specs=(
            P(row, col),
            P(row, col),
            P(col),
            P(col),
            P(row, col),
            P(col),
            P(row, col),
            P(row, col),
            P(col),
            P(col, row),
            P(col),
            P(col),
            P(col),
            P(row, col),
            P(col),
            P(col, row),
            P(col),
        ),
        check_vma=False,
    )
```

```python
import functools

import jax
import jax.numpy as jnp
from jax import lax
from jax.experimental import pallas as pl
from jax.experimental.pallas import tpu as pltpu
from jax.sharding import Mesh
from jax.sharding import PartitionSpec as P

HEADS = 16
EPSILON = 1e-05
PAD = 128
LOG2E = 1.4426950408889634
LN2 = 0.6931471805599453
MASKED = -1e30
BF = jnp.bfloat16
F32 = jnp.float32


def dot(first, second, left, right):
    return lax.dot_general(
        first, second, (((left,), (right,)), ((), ())), preferred_element_type=F32
    )


GROUP = ("zl", "yl")
OTHERS = ("x", "zh", "yh")


def size_of(axis):
    names = axis if isinstance(axis, tuple) else (axis,)
    total = 1
    for name in names:
        total *= lax.axis_size(name)
    return total


def swap(tensor, axis, step=1):
    return lax.ppermute(tensor, axis, [(i, i ^ step) for i in range(size_of(axis))])


def in_order(pieces, axis):
    mine = lax.axis_index(axis)
    if len(pieces) == 1:
        return pieces
    if len(pieces) == 2:
        return [lax.select_n((mine ^ j) == 1, *pieces) for j in range(2)]
    return [lax.select_n(mine ^ j, *pieces) for j in range(len(pieces))]


def pieces_of(tensor, axis):
    return [tensor] + [swap(tensor, axis, d) for d in range(1, size_of(axis))]


def pick(tensor, index, axis):
    return lax.dynamic_index_in_dim(tensor, index, axis, keepdims=False)


def sync(*values):
    return lax.optimization_barrier(values)


def far_pieces(part):
    return [swap(part, GROUP, d) for d in range(1, size_of(GROUP))]


def with_core(part):
    return jnp.concatenate([part, swap(part, "k")], axis=0)


def cores_sum(product, blocks):
    given = swap(product(blocks[1]).astype(BF), "k").astype(F32)
    return product(blocks[0]) + given


def send_far(sums):
    total = swap(sums[0].astype(BF), GROUP, 1).astype(F32)
    for d in range(2, len(sums) + 1):
        total = total + swap(sums[d - 1].astype(BF), GROUP, d).astype(F32)
    return total


def send_units(total, axis, dim):
    mine = lax.axis_index(axis)
    return pick(total, mine, dim), swap(pick(total, 1 - mine, dim), axis)


def send_rows(total):
    x, count = lax.axis_index("x"), lax.axis_size("x")
    last = total.ndim - 1
    side = total.shape[last] // count
    parts = [lax.dynamic_slice_in_dim(total, (x ^ d) * side, side, last) for d in range(count)]
    return tuple(parts[:1] + [swap(parts[d], "x", d) for d in range(1, count)])


def summed(parts):
    return sum(p.astype(F32) for p in parts).astype(BF)


def join_body(padded, stack_ref, out_ref):
    count, blocks = stack_ref.shape[:2]
    side = stack_ref.shape[-1]
    for x in range(count):
        columns = slice(x * side, (x + 1) * side)
        if not padded:
            out_ref[:, columns] = stack_ref[x, 0, 0]
            continue
        head_dim = stack_ref.shape[-2]
        for p in range(blocks):
            for h in range(stack_ref.shape[3]):
                at = (p * stack_ref.shape[3] + h) * PAD
                out_ref[at : at + head_dim, columns] = stack_ref[x, p, 0, h]
                out_ref[at + head_dim : at + PAD, columns] = jnp.zeros((PAD - head_dim, side), BF)


def join_rows(stack, in_spec, grid, out_block, padded):
    width = stack.shape[-1] * stack.shape[0]
    return pl.pallas_call(
        functools.partial(join_body, padded),
        grid=(grid,),
        in_specs=[in_spec],
        out_specs=pl.BlockSpec((out_block, width), lambda i: (i, 0)),
        out_shape=jax.ShapeDtypeStruct((grid * out_block, width), BF),
        compiler_params=pltpu.CompilerParams(vmem_limit_bytes=32 * 2**20),
        cost_estimate=pl.CostEstimate(flops=1000, bytes_accessed=1000, transcendentals=0),
    )(stack)


def first_rows(slot, clips):
    return [[(slot * c - j + 7) // 8 for j in range(8)] for c in range(clips + 1)]


def take_body(starts, lanes, lines, packed_ref, out_ref, low):
    part = pl.program_id(0)
    count, packed_width = packed_ref.shape
    features = packed_width // 8
    choices = [(c, n) for c, row in enumerate(starts) for n in range(len(row))]

    @pl.when(part == 0)
    def _():
        packed = packed_ref[...].astype(F32)
        tail = max(row[-1][0] for row in starts) + lines - count
        packed = jnp.concatenate([packed, jnp.zeros((tail + -(tail + count) % 8, packed_width), F32)], axis=0)
        for at, (c, n) in enumerate(choices):
            start = starts[c][n][0]
            low[at] = packed[start : start + lines].astype(BF)

    source = lax.broadcasted_iota(jnp.int32, (packed_width, features), 0)
    target = lax.broadcasted_iota(jnp.int32, (packed_width, features), 1)
    for clip, row in enumerate(starts):
        taken = []
        for lane in range(lanes):
            position = part * lanes + lane
            choose = jnp.where(source == target * 8 + position, 1.0, 0.0).astype(BF)
            at = choices.index((clip, 0))
            for n in range(1, len(row)):
                at = jnp.where(position < row[n][1], choices.index((clip, n)), at)
            taken.append(dot(choose, low[at], 0, 1))
        out_ref[0, clip, 0] = jnp.concatenate(taken, axis=1).astype(BF)


def starts_by_clip(slot, clips):
    result = []
    for row in first_rows(slot, clips)[:-1]:
        result.append([(value, sum(v >= value for v in row)) for value in sorted(set(row))])
    return result


def take_positions(packed, slot, clips, lanes, lines):
    count, packed_width = packed.shape
    features = packed_width // 8
    starts = starts_by_clip(slot, clips)
    chips = 8 // (2 * lanes)
    return pl.pallas_call(
        functools.partial(take_body, starts, lanes, lines),
        grid=(8 // lanes,),
        in_specs=[pl.BlockSpec((count, packed_width), lambda j: (0, 0))],
        out_specs=pl.BlockSpec((1, clips, 1, features, lanes * lines), lambda j: (j % 2, 0, j // 2, 0, 0)),
        out_shape=jax.ShapeDtypeStruct((2, clips, chips, features, lanes * lines), BF),
        scratch_shapes=[pltpu.VMEM((sum(len(r) for r in starts), lines, packed_width), BF)],
        compiler_params=pltpu.CompilerParams(vmem_limit_bytes=32 * 2**20),
        cost_estimate=pl.CostEstimate(flops=1000, bytes_accessed=1000, transcendentals=0),
    )(packed)


def put_body(rows, lanes, lines, added, *refs):
    base_ref, tokens_ref, out_ref, total = refs if added else (None,) + refs
    half = pl.program_id(0)
    count, packed_width = out_ref.shape
    features = packed_width // 8
    chips = tokens_ref.shape[2]
    source = lax.broadcasted_iota(jnp.int32, (4 * features, packed_width), 0)
    target = lax.broadcasted_iota(jnp.int32, (4 * features, packed_width), 1)
    position = source // features
    wanted = (source - position * features) * 8 + position + 4 * half
    choose = jnp.where(wanted == target, 1.0, 0.0).astype(BF)
    line = lax.broadcasted_iota(jnp.int32, (lines, 1), 0)

    @pl.when(half == 0)
    def _():
        total[...] = jnp.zeros_like(total)

    for clip in range(len(rows) - 1):
        blocks = [
            tokens_ref[core, clip, chip][:, lane * lines : (lane + 1) * lines]
            for chip in range(chips)
            for core in range(2)
            for lane in range(lanes)
        ]
        placed = dot(jnp.concatenate(blocks, axis=0), choose, 0, 0)
        for h in range(2):
            start, stop = rows[clip][4 * h], rows[clip + 1][4 * h]

            @pl.when(half == h)
            def _(start=start, stop=stop, placed=placed):
                total[start : start + lines] += jnp.where(line < stop - start, placed, 0.0)

    @pl.when(half == 1)
    def _():
        out_ref[...] = total[:count] + base_ref[...] if added else total[:count]


def put_positions(tokens, slot, count, lanes, lines, base=None):
    _, clips, chips, features, quarter = tokens.shape
    packed_width = features * 8
    rows = first_rows(slot, clips)
    assert all(len(set(row[:4])) == 1 and len(set(row[4:])) == 1 for row in rows)
    whole = pl.BlockSpec((count, packed_width), lambda h: (0, 0))
    in_specs = [pl.BlockSpec((2, clips, chips // 2, features, quarter), lambda h: (0, 0, h, 0, 0))]
    given = [tokens]
    if base is not None:
        in_specs, given = [whole] + in_specs, [base] + given
    last = max(max(row) for row in rows[:-1]) + lines
    return pl.pallas_call(
        functools.partial(put_body, rows, lanes, lines, base is not None),
        grid=(2,),
        in_specs=in_specs,
        out_specs=whole,
        out_shape=jax.ShapeDtypeStruct((count, packed_width), F32),
        scratch_shapes=[pltpu.VMEM((-(-last // 16) * 16, packed_width), F32)],
        compiler_params=pltpu.CompilerParams(vmem_limit_bytes=40 * 2**20),
        cost_estimate=pl.CostEstimate(flops=1000, bytes_accessed=1000, transcendentals=0),
    )(*given)


def forward_body(query_ref, key_ref, value_ref, context_ref, wide_ref, weights_ref):
    scores = dot(key_ref[...], query_ref[...], 1, 1)
    top = jnp.max(scores, axis=0, keepdims=True)
    powers = jnp.exp2(scores - top)
    total = jnp.sum(powers, axis=0, keepdims=True)
    weights = (powers * (1.0 / total)).astype(BF)
    weights_ref[0] = weights
    context = dot(value_ref[...], weights, 0, 0).T
    context_ref[...] = context.astype(BF)
    wide_ref[...] = context


def attend(packed, heads, part):
    slots = packed.shape[0]
    block = slots // 2
    return pl.pallas_call(
        forward_body,
        grid=(heads,),
        in_specs=[
            pl.BlockSpec((block, PAD), lambda h: (part, h)),
            pl.BlockSpec((slots, PAD), lambda h: (0, heads + h)),
            pl.BlockSpec((slots, PAD), lambda h: (0, 2 * heads + h)),
        ],
        out_specs=[
            pl.BlockSpec((block, PAD), lambda h: (0, h)),
            pl.BlockSpec((block, PAD), lambda h: (0, h)),
            pl.BlockSpec((1, slots, block), lambda h: (h, 0, 0)),
        ],
        out_shape=[
            jax.ShapeDtypeStruct((block, heads * PAD), BF),
            jax.ShapeDtypeStruct((block, heads * PAD), F32),
            jax.ShapeDtypeStruct((heads, slots, block), BF),
        ],
        compiler_params=pltpu.CompilerParams(vmem_limit_bytes=50 * 2**20),
        cost_estimate=pl.CostEstimate(flops=1000, bytes_accessed=1000, transcendentals=0),
    )(packed, packed, packed)


def backward_part(head_dim, query, key, value, grad, context, weights):
    wide = grad.astype(F32)
    inner = jnp.sum(wide * context, axis=1, keepdims=True)
    inner_high = inner.astype(BF).astype(F32)
    lane = lax.broadcasted_iota(jnp.int32, grad.shape, 1)
    extended = jnp.where(
        lane == head_dim,
        inner_high,
        jnp.where(lane == head_dim + 1, inner - inner_high, wide),
    ).astype(BF)
    centered = dot(value, extended, 1, 1)
    grad_scores = (weights.astype(F32) * centered).astype(BF)
    grad_value = dot(weights, grad, 1, 0)
    grad_key = dot(grad_scores, query, 1, 0)
    grad_query = (dot(key, grad_scores, 0, 0) * head_dim**-0.5).T
    return grad_query.astype(BF), grad_key, grad_value


def first_body(head_dim, query, key, value, grad, context, weights, query_out, key_out, value_out):
    query_out[...], key_out[...], value_out[...] = backward_part(
        head_dim, query[...], key[...], value[...], grad[...], context[...], weights[0]
    )


def second_body(
    head_dim, query, key, value, grad, context, weights, first_query, first_key, first_value, out_ref
):
    grad_query, grad_key, grad_value = backward_part(
        head_dim, query[...], key[...], value[...], grad[...], context[...], weights[0]
    )
    block = grad_query.shape[0]
    out_ref[0, :block] = first_query[...]
    out_ref[0, block:] = grad_query
    out_ref[1] = ((grad_key + first_key[...]) * LN2).astype(BF)
    out_ref[2] = (grad_value + first_value[...]).astype(BF)


def attend_back(packed, grad_context, context, weights, heads, head_dim, part, first=None):
    slots = packed.shape[0]
    block = slots // 2
    half = pl.BlockSpec((block, PAD), lambda h: (0, h))
    whole = pl.BlockSpec((slots, PAD), lambda h: (0, h))
    in_specs = [
        pl.BlockSpec((block, PAD), lambda h: (part, h)),
        pl.BlockSpec((slots, PAD), lambda h: (0, heads + h)),
        pl.BlockSpec((slots, PAD), lambda h: (0, 2 * heads + h)),
        half,
        half,
        pl.BlockSpec((1, slots, block), lambda h: (h, 0, 0)),
    ]
    given = [packed, packed, packed, grad_context, context, weights]
    if first is None:
        body = first_body
        out_specs = [half, whole, whole]
        out_shape = [
            jax.ShapeDtypeStruct((block, heads * PAD), BF),
            jax.ShapeDtypeStruct((slots, heads * PAD), F32),
            jax.ShapeDtypeStruct((slots, heads * PAD), F32),
        ]
    else:
        body = second_body
        in_specs += [half, whole, whole]
        given += first
        out_specs = pl.BlockSpec((3, slots, PAD), lambda h: (0, 0, h))
        out_shape = jax.ShapeDtypeStruct((3, slots, heads * PAD), BF)
    return pl.pallas_call(
        functools.partial(body, head_dim),
        grid=(heads,),
        in_specs=in_specs,
        out_specs=out_specs,
        out_shape=out_shape,
        compiler_params=pltpu.CompilerParams(vmem_limit_bytes=56 * 2**20),
        cost_estimate=pl.CostEstimate(flops=1000, bytes_accessed=1000, transcendentals=0),
    )(*given)


def norm_forward(tensor, gain, shift):
    centered = tensor - jnp.mean(tensor, axis=1, keepdims=True)
    scale = lax.rsqrt(jnp.mean(centered * centered, axis=1, keepdims=True) + EPSILON)
    normal = centered * scale
    return normal, scale, (normal * gain + shift).astype(BF)


def norm_backward(grad, normal, scale, gain):
    weighted = grad * gain
    return scale * (
        weighted
        - jnp.mean(weighted, axis=1, keepdims=True)
        - normal * jnp.mean(weighted * normal, axis=1, keepdims=True)
    )


def local(
    inputs,
    lengths,
    cotangent,
    ln1_gain,
    ln1_bias,
    w_query,
    b_query,
    w_key,
    w_value,
    b_value,
    w_attn_out,
    b_attn_out,
    ln2_gain,
    ln2_bias,
    w_in,
    b_in,
    w_out,
    b_out,
):
    chips = size_of(GROUP)
    yl_size = lax.axis_size("yl")
    columns = 8 * yl_size
    k, zh, yh = (lax.axis_index(a) for a in ("k", "zh", "yh"))
    chip = lax.axis_index(GROUP)
    pack_count, packed_width = inputs.shape
    features = packed_width // 8
    width = features * columns
    clips = lengths.shape[0]
    slot = pack_count * 8 // clips
    group = 2 * chips
    lines = -(-(slot // 8 + 1) // 64) * 64
    lanes = 8 // group
    quarter = lanes * lines
    slots = 8 * lines
    half = slots // 2
    rows = w_query.shape[0]
    block_heads = HEADS // columns
    head_dim = width // HEADS
    split = block_heads % 2 == 0
    part_heads = block_heads // 2 if split else block_heads
    heads = 2 * block_heads
    units = w_in.shape[1]
    half_units = units // 2

    def start_of(clip, j):
        return (slot * clip - j + 7) // 8

    def order_tokens(own, other):
        ordered = jnp.stack(in_order([own, other], "k")).reshape(2, 2, 2, yl_size, features, quarter)
        return ordered.transpose(0, 2, 1, 3, 4, 5).reshape(columns, features, quarter)

    def exchange(blocks):
        return lax.all_to_all(blocks, ("zh", "zl", "yh", "yl"), 0, 0)

    def join(moved):
        return moved.reshape(width, quarter).T

    def cut(tensor):
        return tensor.T.reshape(columns, features, quarter)

    def by_core(tensor, parts):
        if not parts:
            return jnp.broadcast_to(tensor[None], (2,) + tensor.shape)
        return tensor.reshape((2, tensor.shape[0] // 2) + tensor.shape[1:])

    def gather_others(shard):
        return lax.all_gather(shard, OTHERS, axis=0)

    def arrange_heads(stack):
        stack = stack.reshape(-1, 4, 4, part_heads, head_dim, 2 * rows)
        if not split:
            stack = lax.dynamic_slice_in_dim(stack, 2 * k, 2, 1)
        block = stack.shape[:2] + (1,) + stack.shape[3:]
        return join_rows(stack, pl.BlockSpec(block, lambda i: (0, 0, i, 0, 0, 0)), 4, heads * PAD, True)

    def arrange_units(stack, which):
        stack = stack.reshape(-1, 4, 2, half_units, 2 * rows)
        block = (stack.shape[0], 1, 1) + stack.shape[3:]
        return join_rows(stack, pl.BlockSpec(block, lambda i: (0, i, which, 0, 0)), 4, half_units, False)

    full_vectors = jnp.stack([ln1_gain, ln1_bias, ln2_gain, ln2_bias, b_attn_out, b_out])
    part_vector = jnp.concatenate([b_query, b_value, b_in])
    full_count = full_vectors.shape[0]
    full_by = jnp.stack(in_order(pieces_of(full_vectors, GROUP), GROUP))
    all_lengths = jnp.concatenate(in_order(pieces_of(lengths, "k"), "k"))

    taken = take_positions(inputs, slot, clips, lanes, lines)
    own_tokens, other_tokens = pick(taken, k, 0), swap(pick(taken, 1 - k, 0), "k")
    turned = [t.astype(BF).T for t in (w_query, w_key, w_value)] + [w_attn_out.astype(BF)]
    head_parts = jnp.stack([by_core(t, split) for t in turned], axis=1)
    head_parts = head_parts.reshape(2, 4 * part_heads * head_dim, rows)
    own_parts, other_parts = pick(head_parts, k, 0), swap(pick(head_parts, 1 - k, 0), "k")
    head_shard = jnp.concatenate(in_order([own_parts, other_parts], "k"), axis=1)
    head_stacked = gather_others(head_shard)

    ordered, cotangent, w_in, w_out, full_by = sync(
        order_tokens(own_tokens, other_tokens), cotangent, w_in, w_out, full_by
    )
    moved = exchange(ordered)
    full_size = full_by.size
    vector_pieces = in_order(pieces_of(jnp.concatenate([full_by.reshape(-1), part_vector]), "zh"), "zh")
    vector_pieces = in_order(pieces_of(jnp.stack(vector_pieces), "yh"), "yh")
    unit_parts = jnp.stack([by_core(w_in.astype(BF).T, True), by_core(w_out.astype(BF), True)], axis=1)
    unit_parts = unit_parts.reshape(2, units, rows)
    own_parts, other_parts = pick(unit_parts, k, 0), swap(pick(unit_parts, 1 - k, 0), "k")
    unit_shard = jnp.concatenate(in_order([own_parts, other_parts], "k"), axis=1)
    unit_shard = unit_shard.reshape(2, half_units, 2 * rows)
    unit_stacked = gather_others(unit_shard)
    taken = take_positions(cotangent, slot, clips, lanes, lines)
    own_tokens, other_tokens = pick(taken, k, 0), swap(pick(taken, 1 - k, 0), "k")
    ordered_grads = order_tokens(own_tokens, other_tokens)

    all_vectors = jnp.stack(vector_pieces, axis=1)
    part_by = all_vectors[:, :, full_size:].reshape(4, -1)
    full_by = all_vectors[:, :, :full_size].reshape(2, 2, 2, yl_size, full_count, features)
    full_by = full_by.transpose(4, 0, 2, 1, 3, 5)
    gain_one, shift_one, gain_two, shift_two, attn_shift, out_shift = full_by.reshape(full_count, 1, width)

    def head_vector(tensor):
        tensor = tensor.reshape(4, block_heads, head_dim)
        if split:
            tensor = pick(tensor.reshape(4, 2, part_heads, head_dim), k, 1)
        else:
            tensor = lax.dynamic_slice_in_dim(tensor, 2 * k, 2, 0)
        tensor = tensor.reshape(heads, head_dim)
        return jnp.pad(tensor, ((0, 0), (0, PAD - head_dim)))

    query_shift = head_vector(part_by[:, :features])
    value_shift = head_vector(part_by[:, features : 2 * features])
    unit_shift = pick(part_by[:, 2 * features :].reshape(4, 2, half_units), k, 1).reshape(-1)

    clip_length = pick(all_lengths, zh * 2 + yh, 0)

    def slots_of(part):
        j = part * lanes + jnp.repeat(jnp.arange(lanes), lines)
        return 8 * (start_of(yh, j) + jnp.tile(jnp.arange(lines), lanes)) + j - slot * yh

    own_valid = slots_of(chip * 2 + k) < clip_length
    slot_order = jnp.concatenate([slots_of((chip ^ d) * 2 + (k ^ c)) for d in range(chips) for c in range(2)])
    key_mask = jnp.where(slot_order < clip_length, 0.0, MASKED)

    lane = jnp.arange(PAD)[None, :]
    none = jnp.zeros((heads, PAD), F32)
    is_first = jnp.broadcast_to(lane == head_dim, (heads, PAD)).astype(F32)
    is_extra = jnp.broadcast_to((lane >= head_dim) & (lane < head_dim + 2), (heads, PAD)).astype(F32)
    qkv_shift = jnp.concatenate([query_shift, none, value_shift]).reshape(1, -1)
    qkv_scale = jnp.concatenate([none + head_dim**-0.5 * LOG2E, none + 1, none + 1]).reshape(1, -1)
    qkv_extra = jnp.concatenate([is_first, none, -is_extra]).reshape(1, -1)
    mask_lane = jnp.concatenate([none, is_first, none]).reshape(1, -1)

    def blocks_of(tensor):
        count = tensor.shape[0] // (2 * quarter)
        return [
            [tensor[(2 * d + c) * quarter : (2 * d + c + 1) * quarter] for c in range(2)]
            for d in range(count)
        ]

    tokens = join(moved).astype(F32)
    normal_one, scale_one, normed_part = norm_forward(tokens, gain_one, shift_one)
    normed_far = far_pieces(normed_part)
    normed_near = with_core(normed_part)
    normed_near, head_stacked = sync(normed_near, head_stacked)
    head_weights = arrange_heads(head_stacked).reshape(4, heads * PAD, width)
    normed_far, ordered_grads = sync(normed_far, ordered_grads)
    moved_grads = exchange(ordered_grads)
    qkv_weights = head_weights[:3].reshape(3 * heads * PAD, width)
    attn_weights = head_weights[3]

    def qkv(rows_d, d):
        mask_d = key_mask[d * 2 * quarter : (d + 1) * 2 * quarter, None]
        product = (dot(rows_d, qkv_weights, 1, 1) + qkv_shift) * qkv_scale
        return (product + qkv_extra + mask_d * mask_lane).astype(BF)

    packed_near = qkv(normed_near, 0)
    normed_rows = [normed_near] + [with_core(v) for v in normed_far]
    packed = jnp.concatenate(
        [packed_near] + [qkv(v, d) for d, v in enumerate(normed_rows) if d], axis=0
    )
    far_context, far_wide, far_weights = attend(packed, heads, 1)

    def attn_product(v):
        return dot(v, attn_weights, 1, 0)

    near_chips = chips // 2
    far_sums = [cores_sum(attn_product, b).astype(BF) for b in blocks_of(far_context)]
    far_sums, packed, moved_grads = sync(far_sums, packed, moved_grads)
    far_total = send_far(far_sums) if near_chips == 1 else None
    near_context, near_wide, near_weights = attend(packed, heads, 0)
    normed = jnp.concatenate(normed_rows, axis=0)
    grad_low = jnp.where(own_valid[:, None], join(moved_grads), jnp.zeros((quarter, width), BF))
    if near_chips == 1:
        near_context, far_total, normed, grad_low = sync(near_context, far_total, normed, grad_low)
    near_sums = [cores_sum(attn_product, b) for b in blocks_of(near_context)]
    if near_chips > 1:
        far_total = send_far((near_sums + far_sums)[1:])
    grad_far = far_pieces(grad_low)
    grad_near = with_core(grad_low)
    attn_part = near_sums[0] + far_total + attn_shift
    middle = tokens + attn_part
    normal_two, scale_two, normed_two_part = norm_forward(middle, gain_two, shift_two)
    two_near = with_core(normed_two_part)
    two_far = far_pieces(normed_two_part)
    two_near, unit_stacked, grad_far = sync(two_near, unit_stacked, grad_far)
    in_weights = arrange_units(unit_stacked, 0)
    out_weights = arrange_units(unit_stacked, 1)

    def feed(rows_d):
        hidden = dot(rows_d, in_weights, 1, 1) + unit_shift
        below = 0.5 * (1.0 + lax.erf(hidden * 0.5**0.5))
        slope = below + hidden * (jnp.exp(-0.5 * hidden * hidden) * (0.5 / jnp.pi) ** 0.5)
        return (hidden * below).astype(BF), slope

    def feed_back(grad_d, slope):
        return (dot(grad_d, out_weights, 1, 1) * slope).astype(BF)

    near_active, near_slope = feed(two_near)
    near_hidden = feed_back(grad_near, near_slope)
    near_hidden, two_far = sync(near_hidden, two_far)
    two_rows = [two_near] + [with_core(v) for v in two_far]
    far_feed = [feed(v) for v in two_rows[1:]]
    grad_rows = [grad_near] + [with_core(v) for v in grad_far]
    grad_hidden = jnp.concatenate(
        [near_hidden] + [feed_back(g, f[1]) for g, f in zip(grad_rows[1:], far_feed)], axis=0
    )
    active = jnp.concatenate([near_active] + [f[0] for f in far_feed], axis=0)

    def in_product(v):
        return dot(v, in_weights, 1, 0)

    hidden_blocks = blocks_of(grad_hidden)
    far_two = [cores_sum(in_product, b).astype(BF) for b in hidden_blocks[1:]]
    grad_hidden, near_blocks, far_two, active = sync(grad_hidden, hidden_blocks[0], far_two, active)
    near_two = cores_sum(in_product, near_blocks)
    normed_two = jnp.concatenate(two_rows, axis=0)
    grad_full = jnp.concatenate(grad_rows, axis=0)

    out_total = dot(active, grad_full, 0, 0).astype(BF).reshape(2, 2, half_units, width)
    in_total = dot(grad_hidden, normed_two, 0, 0).astype(BF).reshape(2, 2, half_units, width)
    out_half = send_units(out_total, "yh", 1)
    in_half = send_rows(in_total)
    two_arrived, active = sync(send_far(far_two), active)
    grad_two = near_two + two_arrived
    grad_out = grad_low.astype(F32)
    grad_middle = grad_out + norm_backward(grad_two, normal_two, scale_two, gain_two)
    grad_mid_part = grad_middle.astype(BF)
    mid_far = far_pieces(grad_mid_part)
    mid_near = with_core(grad_mid_part)

    def context_grad(v):
        return dot(v, attn_weights, 1, 1).astype(BF)

    def out_product(v):
        return dot(v, out_weights, 1, 0)

    mid_half = jnp.concatenate([mid_near] + [with_core(v) for v in mid_far[: near_chips - 1]], axis=0)
    near_grad = context_grad(mid_half)
    active_blocks = blocks_of(active)
    delta_given = swap(jnp.concatenate([out_product(b[1]).astype(BF) for b in active_blocks]), "k")
    delta_cores = [
        out_product(b[0]) + delta_given[d * quarter : (d + 1) * quarter].astype(F32)
        for d, b in enumerate(active_blocks)
    ]
    near_delta, far_delta = delta_cores[0], [v.astype(BF) for v in delta_cores[1:]]
    near_grad, near_delta, far_delta = sync(near_grad, near_delta, far_delta)
    first = attend_back(packed, near_grad, near_wide, near_weights, heads, head_dim, 0)
    first, mid_far, far_delta, out_half, in_half = sync(first, mid_far, far_delta, out_half, in_half)
    delta_far = send_far(far_delta)
    out_half = send_rows(summed(out_half))
    in_half = send_units(summed(in_half), "yh", 1)
    mid_rows = [mid_near] + [with_core(v) for v in mid_far]
    mid_full = jnp.concatenate(mid_rows, axis=0)
    far_grad = context_grad(mid_full[half:])
    grads = attend_back(packed, far_grad, far_wide, far_weights, heads, head_dim, 1, list(first))
    qkv_cube = qkv_weights.reshape(3, heads * PAD, width)

    def qkv_product(v):
        return sum(dot(v[j], qkv_cube[j], 1, 0) for j in range(3))

    grad_blocks = [
        [grads[:, (2 * d + c) * quarter : (2 * d + c + 1) * quarter] for c in range(2)] for d in range(chips)
    ]
    far_one = [cores_sum(qkv_product, b).astype(BF) for b in grad_blocks[1:]]
    grads, far_one, near_blocks, out_half, in_half = sync(grads, far_one, grad_blocks[0], out_half, in_half)
    far_arrived = send_far(far_one)
    near_one = cores_sum(qkv_product, near_blocks)
    unit_sums = jnp.stack([summed(out_half), summed(in_half)])
    far_arrived, unit_sums = sync(far_arrived, unit_sums)
    unit_half = send_units(unit_sums, "zh", 1)
    context = jnp.concatenate([near_context, far_context], axis=0)
    grads, near_one, delta_far, context, mid_full = sync(grads, near_one, delta_far, context, mid_full)

    def trim(total):
        return total.reshape(-1, part_heads, PAD, width)[:, :, :head_dim].reshape(-1, part_heads * head_dim, width)

    def head_chunk(totals):
        chunk = jnp.stack([trim(t) for t in totals], axis=1).reshape(-1, len(totals) * part_heads * head_dim, width)
        if not split:
            blank = jnp.zeros((4,) + chunk.shape[1:], BF)
            chunk = lax.dynamic_update_slice_in_dim(blank, chunk, 2 * k, 0)
        return chunk.reshape((2, 2) + chunk.shape[1:])

    query_key = head_chunk([dot(grads[j], normed, 0, 0).astype(BF) for j in range(2)])
    value_attn = head_chunk([dot(grads[2], normed, 0, 0).astype(BF), dot(context, mid_full, 0, 0).astype(BF)])
    query_key_half = send_rows(query_key)
    value_attn_half = send_units(value_attn, "yh", 1)
    grad_one = near_one + far_arrived
    grad_tokens = norm_backward(grad_one, normal_one, scale_one, gain_one)
    last_part = (grad_middle + grad_tokens).astype(BF)
    moved_last = exchange(cut(last_part))
    query_key_half = send_units(summed(query_key_half), "yh", 1)
    value_attn_half = send_rows(summed(value_attn_half))
    delta = (attn_part + near_delta + delta_far + out_shift).astype(BF)

    full_sums = jnp.stack(
        [
            jnp.sum(v, axis=0)
            for v in (
                grad_one * normal_one,
                grad_one,
                grad_middle,
                grad_two * normal_two,
                grad_two,
                grad_out,
            )
        ]
    )

    def head_sums(tensor):
        total = jnp.sum(tensor.astype(F32), axis=0).reshape(-1, part_heads, PAD)[:, :, :head_dim]
        if not split:
            blank = jnp.zeros((4,) + total.shape[1:], F32)
            total = lax.dynamic_update_slice_in_dim(blank, total, 2 * k, 0)
        return total.reshape(4, -1)

    part_sums = jnp.concatenate(
        [
            head_sums(grads[0]),
            head_sums(grads[2]),
            jnp.sum(grad_hidden.astype(F32), axis=0).reshape(4, half_units),
        ],
        axis=1,
    )
    full_sums = full_sums.reshape(full_count, 2, 2, 2, yl_size, features).transpose(1, 3, 2, 4, 0, 5)
    full_size = full_sums[0, 0].size
    flat = jnp.concatenate([full_sums.reshape(2, 2, -1), part_sums.reshape(2, 2, -1)], axis=2)
    flat_pieces = pieces_of(flat, "x")
    moved_last, query_key_half, value_attn_half, delta_blocks, flat_pieces, unit_half = sync(
        moved_last, query_key_half, value_attn_half, cut(delta), flat_pieces, unit_half
    )
    moved_delta = exchange(delta_blocks)
    head_half = send_units(jnp.stack([summed(query_key_half), summed(value_attn_half)]), "zh", 1)

    def two_cores(total, two):
        last = total.ndim - 1
        kept = lax.dynamic_slice_in_dim(total, k * rows, rows, last)
        other = swap(lax.dynamic_slice_in_dim(total, (1 - k) * rows, rows, last), "k")
        if not two:
            return kept.astype(F32) + other.astype(F32)
        return jnp.stack(in_order([kept, other], "k"), axis=1).astype(F32)

    def kept_tokens(moved):
        moved = moved.reshape(2, 2, 2, yl_size, features, quarter).transpose(0, 2, 1, 3, 4, 5)
        kept = pick(moved, k, 0)
        other = swap(pick(moved, 1 - k, 0), "k")
        ordered = jnp.stack(in_order([kept, other], "k"))
        return ordered.reshape(2, clips, chips, features, quarter)

    def put(tokens, base=None):
        return put_positions(tokens, slot, pack_count, lanes, lines, base)

    flat_half = send_units(sum(flat_pieces), "yh", 1)
    input_grad, moved_delta, flat_half = sync(put(kept_tokens(moved_last)), moved_delta, flat_half)
    flat = sum(send_units(sum(flat_half), "zh", 0))
    full_flat, part_flat = flat[:full_size], flat[full_size:]

    by_chip = full_flat.reshape(chips, -1)
    mine = pick(by_chip, chip, 0)
    for d in range(1, chips):
        mine = mine + swap(pick(by_chip, chip ^ d, 0), GROUP, d)
    unit_cores = two_cores(summed(unit_half), True)
    grad_out_w = unit_cores[0].reshape(units, rows)
    grad_in_w = unit_cores[1].reshape(units, rows).T
    layer_out = put(kept_tokens(moved_delta), inputs)
    input_grad, head_half, mine = sync(input_grad, head_half, mine)
    head_cores = two_cores(summed(head_half), split)
    head_cores = head_cores.reshape(2, -1, 2, part_heads * head_dim, rows)
    grad_query_w, grad_key_w, grad_value_w, grad_attn_w = (
        head_cores[i, :, j].reshape(features, rows) for i in range(2) for j in range(2)
    )

    own_size = mine.shape[0]
    last_pair = pieces_of(jnp.concatenate([mine, part_flat]), "k")
    vec_one_gain, vec_one_bias, vec_battn, vec_two_gain, vec_two_bias, vec_bout = (
        last_pair[0][:own_size] + last_pair[1][:own_size]
    ).reshape(full_count, features)
    head_size = part_heads * head_dim
    cores = in_order([p[own_size:] for p in last_pair], "k")
    if split:
        vec_bquery = jnp.concatenate([c[:head_size] for c in cores])
        vec_bvalue = jnp.concatenate([c[head_size : 2 * head_size] for c in cores])
    else:
        vec_bquery = cores[0][:head_size] + cores[1][:head_size]
        vec_bvalue = cores[0][head_size : 2 * head_size] + cores[1][head_size : 2 * head_size]
    vec_bin = jnp.concatenate([c[2 * head_size :] for c in cores])

    return (
        layer_out,
        input_grad,
        vec_one_gain,
        vec_one_bias,
        grad_query_w.T,
        vec_bquery,
        grad_key_w.T,
        grad_value_w.T,
        vec_bvalue,
        grad_attn_w,
        vec_battn,
        vec_two_gain,
        vec_two_bias,
        grad_in_w,
        vec_bin,
        grad_out_w,
        vec_bout,
    )


def solution(mesh):
    row_size, col_size = mesh.shape["row"], mesh.shape["col"]
    shape = (row_size // 2, 2, 2, 2, 2, col_size // 8)
    row, col = ("x", "k"), ("zh", "zl", "yh", "yl")
    grid = Mesh(mesh.devices.reshape(shape), row + col)
    return jax.shard_map(
        local,
        mesh=grid,
        in_specs=(
            P(row, col),
            P(row),
            P(row, col),
            P(col),
            P(col),
            P(row, col),
            P(col),
            P(row, col),
            P(row, col),
            P(col),
            P(col, row),
            P(col),
            P(col),
            P(col),
            P(row, col),
            P(col),
            P(col, row),
            P(col),
        ),
        out_specs=(
            P(row, col),
            P(row, col),
            P(col),
            P(col),
            P(row, col),
            P(col),
            P(row, col),
            P(row, col),
            P(col),
            P(col, row),
            P(col),
            P(col),
            P(col),
            P(row, col),
            P(col),
            P(col, row),
            P(col),
        ),
        check_vma=False,
    )
```

```python
import functools

import jax
import jax.numpy as jnp
from jax import lax
from jax.experimental import pallas as pl
from jax.experimental.pallas import tpu as pltpu
from jax.sharding import Mesh
from jax.sharding import PartitionSpec as P

HEADS = 16
EPSILON = 1e-05
PAD = 128
LOG2E = 1.4426950408889634
LN2 = 0.6931471805599453
MASKED = -1e30
BF = jnp.bfloat16
F32 = jnp.float32


def dot(first, second, left, right):
    return lax.dot_general(
        first, second, (((left,), (right,)), ((), ())), preferred_element_type=F32
    )


GROUP = ("zl", "yl")
OTHERS = ("x", "zh", "yh")


def size_of(axis):
    names = axis if isinstance(axis, tuple) else (axis,)
    total = 1
    for name in names:
        total *= lax.axis_size(name)
    return total


def swap(tensor, axis, step=1):
    return lax.ppermute(tensor, axis, [(i, i ^ step) for i in range(size_of(axis))])


def in_order(pieces, axis):
    mine = lax.axis_index(axis)
    if len(pieces) == 1:
        return pieces
    if len(pieces) == 2:
        return [lax.select_n((mine ^ j) == 1, *pieces) for j in range(2)]
    return [lax.select_n(mine ^ j, *pieces) for j in range(len(pieces))]


def pieces_of(tensor, axis):
    return [tensor] + [swap(tensor, axis, d) for d in range(1, size_of(axis))]


def pick(tensor, index, axis):
    return lax.dynamic_index_in_dim(tensor, index, axis, keepdims=False)


def sync(*values):
    return lax.optimization_barrier(values)


def far_pieces(part):
    return [swap(part, GROUP, d) for d in range(1, size_of(GROUP))]


def with_core(part):
    return jnp.concatenate([part, swap(part, "k")], axis=0)


def cores_sum(product, blocks):
    given = swap(product(blocks[1]).astype(BF), "k").astype(F32)
    return product(blocks[0]) + given


def send_far(sums):
    total = swap(sums[0].astype(BF), GROUP, 1).astype(F32)
    for d in range(2, len(sums) + 1):
        total = total + swap(sums[d - 1].astype(BF), GROUP, d).astype(F32)
    return total


def send_units(total, axis, dim):
    mine = lax.axis_index(axis)
    return pick(total, mine, dim), swap(pick(total, 1 - mine, dim), axis)


def send_rows(total):
    x, count = lax.axis_index("x"), lax.axis_size("x")
    last = total.ndim - 1
    side = total.shape[last] // count
    parts = [lax.dynamic_slice_in_dim(total, (x ^ d) * side, side, last) for d in range(count)]
    return tuple(parts[:1] + [swap(parts[d], "x", d) for d in range(1, count)])


def summed(parts):
    return sum(p.astype(F32) for p in parts).astype(BF)


def join_body(padded, stack_ref, out_ref):
    count, blocks = stack_ref.shape[:2]
    side = stack_ref.shape[-1]
    for x in range(count):
        columns = slice(x * side, (x + 1) * side)
        if not padded:
            out_ref[:, columns] = stack_ref[x, 0, 0]
            continue
        head_dim = stack_ref.shape[-2]
        for p in range(blocks):
            for h in range(stack_ref.shape[3]):
                at = (p * stack_ref.shape[3] + h) * PAD
                out_ref[at : at + head_dim, columns] = stack_ref[x, p, 0, h]
                out_ref[at + head_dim : at + PAD, columns] = jnp.zeros((PAD - head_dim, side), BF)


def join_rows(stack, in_spec, grid, out_block, padded):
    width = stack.shape[-1] * stack.shape[0]
    return pl.pallas_call(
        functools.partial(join_body, padded),
        grid=(grid,),
        in_specs=[in_spec],
        out_specs=pl.BlockSpec((out_block, width), lambda i: (i, 0)),
        out_shape=jax.ShapeDtypeStruct((grid * out_block, width), BF),
        compiler_params=pltpu.CompilerParams(vmem_limit_bytes=32 * 2**20),
        cost_estimate=pl.CostEstimate(flops=1000, bytes_accessed=1000, transcendentals=0),
    )(stack)


def first_rows(slot, clips):
    return [[(slot * c - j + 7) // 8 for j in range(8)] for c in range(clips + 1)]


def take_body(starts, lanes, lines, packed_ref, out_ref, low):
    part = pl.program_id(0)
    count, packed_width = packed_ref.shape
    features = packed_width // 8
    choices = [(c, n) for c, row in enumerate(starts) for n in range(len(row))]

    @pl.when(part == 0)
    def _():
        packed = packed_ref[...].astype(F32)
        tail = max(row[-1][0] for row in starts) + lines - count
        packed = jnp.concatenate([packed, jnp.zeros((tail + -(tail + count) % 8, packed_width), F32)], axis=0)
        for at, (c, n) in enumerate(choices):
            start = starts[c][n][0]
            low[at] = packed[start : start + lines].astype(BF)

    source = lax.broadcasted_iota(jnp.int32, (packed_width, features), 0)
    target = lax.broadcasted_iota(jnp.int32, (packed_width, features), 1)
    for clip, row in enumerate(starts):
        taken = []
        for lane in range(lanes):
            position = part * lanes + lane
            choose = jnp.where(source == target * 8 + position, 1.0, 0.0).astype(BF)
            at = choices.index((clip, 0))
            for n in range(1, len(row)):
                at = jnp.where(position < row[n][1], choices.index((clip, n)), at)
            taken.append(dot(choose, low[at], 0, 1))
        out_ref[0, clip, 0] = jnp.concatenate(taken, axis=1).astype(BF)


def starts_by_clip(slot, clips):
    result = []
    for row in first_rows(slot, clips)[:-1]:
        result.append([(value, sum(v >= value for v in row)) for value in sorted(set(row))])
    return result


def take_positions(packed, slot, clips, lanes, lines):
    count, packed_width = packed.shape
    features = packed_width // 8
    starts = starts_by_clip(slot, clips)
    chips = 8 // (2 * lanes)
    return pl.pallas_call(
        functools.partial(take_body, starts, lanes, lines),
        grid=(8 // lanes,),
        in_specs=[pl.BlockSpec((count, packed_width), lambda j: (0, 0))],
        out_specs=pl.BlockSpec((1, clips, 1, features, lanes * lines), lambda j: (j % 2, 0, j // 2, 0, 0)),
        out_shape=jax.ShapeDtypeStruct((2, clips, chips, features, lanes * lines), BF),
        scratch_shapes=[pltpu.VMEM((sum(len(r) for r in starts), lines, packed_width), BF)],
        compiler_params=pltpu.CompilerParams(vmem_limit_bytes=32 * 2**20),
        cost_estimate=pl.CostEstimate(flops=1000, bytes_accessed=1000, transcendentals=0),
    )(packed)


def put_body(rows, lanes, lines, added, *refs):
    base_ref, tokens_ref, out_ref, total = refs if added else (None,) + refs
    half = pl.program_id(0)
    count, packed_width = out_ref.shape
    features = packed_width // 8
    chips = tokens_ref.shape[2]
    source = lax.broadcasted_iota(jnp.int32, (4 * features, packed_width), 0)
    target = lax.broadcasted_iota(jnp.int32, (4 * features, packed_width), 1)
    position = source // features
    wanted = (source - position * features) * 8 + position + 4 * half
    choose = jnp.where(wanted == target, 1.0, 0.0).astype(BF)
    line = lax.broadcasted_iota(jnp.int32, (lines, 1), 0)

    @pl.when(half == 0)
    def _():
        total[...] = jnp.zeros_like(total)

    for clip in range(len(rows) - 1):
        blocks = [
            tokens_ref[core, clip, chip][:, lane * lines : (lane + 1) * lines]
            for chip in range(chips)
            for core in range(2)
            for lane in range(lanes)
        ]
        placed = dot(jnp.concatenate(blocks, axis=0), choose, 0, 0)
        for h in range(2):
            start, stop = rows[clip][4 * h], rows[clip + 1][4 * h]

            @pl.when(half == h)
            def _(start=start, stop=stop, placed=placed):
                total[start : start + lines] += jnp.where(line < stop - start, placed, 0.0)

    @pl.when(half == 1)
    def _():
        out_ref[...] = total[:count] + base_ref[...] if added else total[:count]


def put_positions(tokens, slot, count, lanes, lines, base=None):
    _, clips, chips, features, quarter = tokens.shape
    packed_width = features * 8
    rows = first_rows(slot, clips)
    assert all(len(set(row[:4])) == 1 and len(set(row[4:])) == 1 for row in rows)
    whole = pl.BlockSpec((count, packed_width), lambda h: (0, 0))
    in_specs = [pl.BlockSpec((2, clips, chips // 2, features, quarter), lambda h: (0, 0, h, 0, 0))]
    given = [tokens]
    if base is not None:
        in_specs, given = [whole] + in_specs, [base] + given
    last = max(max(row) for row in rows[:-1]) + lines
    return pl.pallas_call(
        functools.partial(put_body, rows, lanes, lines, base is not None),
        grid=(2,),
        in_specs=in_specs,
        out_specs=whole,
        out_shape=jax.ShapeDtypeStruct((count, packed_width), F32),
        scratch_shapes=[pltpu.VMEM((-(-last // 16) * 16, packed_width), F32)],
        compiler_params=pltpu.CompilerParams(vmem_limit_bytes=40 * 2**20),
        cost_estimate=pl.CostEstimate(flops=1000, bytes_accessed=1000, transcendentals=0),
    )(*given)


def forward_body(query_ref, key_ref, value_ref, context_ref, wide_ref, weights_ref):
    scores = dot(key_ref[...], query_ref[...], 1, 1)
    top = jnp.max(scores, axis=0, keepdims=True)
    powers = jnp.exp2(scores - top)
    total = jnp.sum(powers, axis=0, keepdims=True)
    weights = (powers * (1.0 / total)).astype(BF)
    weights_ref[0] = weights
    context = dot(value_ref[...], weights, 0, 0).T
    context_ref[...] = context.astype(BF)
    wide_ref[...] = context


def attend(packed, heads, part):
    slots = packed.shape[0]
    block = slots // 2
    return pl.pallas_call(
        forward_body,
        grid=(heads,),
        in_specs=[
            pl.BlockSpec((block, PAD), lambda h: (part, h)),
            pl.BlockSpec((slots, PAD), lambda h: (0, heads + h)),
            pl.BlockSpec((slots, PAD), lambda h: (0, 2 * heads + h)),
        ],
        out_specs=[
            pl.BlockSpec((block, PAD), lambda h: (0, h)),
            pl.BlockSpec((block, PAD), lambda h: (0, h)),
            pl.BlockSpec((1, slots, block), lambda h: (h, 0, 0)),
        ],
        out_shape=[
            jax.ShapeDtypeStruct((block, heads * PAD), BF),
            jax.ShapeDtypeStruct((block, heads * PAD), F32),
            jax.ShapeDtypeStruct((heads, slots, block), BF),
        ],
        compiler_params=pltpu.CompilerParams(vmem_limit_bytes=50 * 2**20),
        cost_estimate=pl.CostEstimate(flops=1000, bytes_accessed=1000, transcendentals=0),
    )(packed, packed, packed)


def backward_part(head_dim, query, key, value, grad, context, weights):
    wide = grad.astype(F32)
    inner = jnp.sum(wide * context, axis=1, keepdims=True)
    inner_high = inner.astype(BF).astype(F32)
    lane = lax.broadcasted_iota(jnp.int32, grad.shape, 1)
    extended = jnp.where(
        lane == head_dim,
        inner_high,
        jnp.where(lane == head_dim + 1, inner - inner_high, wide),
    ).astype(BF)
    centered = dot(value, extended, 1, 1)
    grad_scores = (weights.astype(F32) * centered).astype(BF)
    grad_value = dot(weights, grad, 1, 0)
    grad_key = dot(grad_scores, query, 1, 0)
    grad_query = (dot(key, grad_scores, 0, 0) * head_dim**-0.5).T
    return grad_query.astype(BF), grad_key, grad_value


def first_body(head_dim, query, key, value, grad, context, weights, query_out, key_out, value_out):
    query_out[...], key_out[...], value_out[...] = backward_part(
        head_dim, query[...], key[...], value[...], grad[...], context[...], weights[0]
    )


def second_body(
    head_dim, query, key, value, grad, context, weights, first_query, first_key, first_value, out_ref
):
    grad_query, grad_key, grad_value = backward_part(
        head_dim, query[...], key[...], value[...], grad[...], context[...], weights[0]
    )
    block = grad_query.shape[0]
    out_ref[0, :block] = first_query[...]
    out_ref[0, block:] = grad_query
    out_ref[1] = ((grad_key + first_key[...]) * LN2).astype(BF)
    out_ref[2] = (grad_value + first_value[...]).astype(BF)


def attend_back(packed, grad_context, context, weights, heads, head_dim, part, first=None):
    slots = packed.shape[0]
    block = slots // 2
    half = pl.BlockSpec((block, PAD), lambda h: (0, h))
    whole = pl.BlockSpec((slots, PAD), lambda h: (0, h))
    in_specs = [
        pl.BlockSpec((block, PAD), lambda h: (part, h)),
        pl.BlockSpec((slots, PAD), lambda h: (0, heads + h)),
        pl.BlockSpec((slots, PAD), lambda h: (0, 2 * heads + h)),
        half,
        half,
        pl.BlockSpec((1, slots, block), lambda h: (h, 0, 0)),
    ]
    given = [packed, packed, packed, grad_context, context, weights]
    if first is None:
        body = first_body
        out_specs = [half, whole, whole]
        out_shape = [
            jax.ShapeDtypeStruct((block, heads * PAD), BF),
            jax.ShapeDtypeStruct((slots, heads * PAD), F32),
            jax.ShapeDtypeStruct((slots, heads * PAD), F32),
        ]
    else:
        body = second_body
        in_specs += [half, whole, whole]
        given += first
        out_specs = pl.BlockSpec((3, slots, PAD), lambda h: (0, 0, h))
        out_shape = jax.ShapeDtypeStruct((3, slots, heads * PAD), BF)
    return pl.pallas_call(
        functools.partial(body, head_dim),
        grid=(heads,),
        in_specs=in_specs,
        out_specs=out_specs,
        out_shape=out_shape,
        compiler_params=pltpu.CompilerParams(vmem_limit_bytes=56 * 2**20),
        cost_estimate=pl.CostEstimate(flops=1000, bytes_accessed=1000, transcendentals=0),
    )(*given)


def norm_forward(tensor, gain, shift):
    centered = tensor - jnp.mean(tensor, axis=1, keepdims=True)
    scale = lax.rsqrt(jnp.mean(centered * centered, axis=1, keepdims=True) + EPSILON)
    normal = centered * scale
    return normal, scale, (normal * gain + shift).astype(BF)


def norm_backward(grad, normal, scale, gain):
    weighted = grad * gain
    return scale * (
        weighted
        - jnp.mean(weighted, axis=1, keepdims=True)
        - normal * jnp.mean(weighted * normal, axis=1, keepdims=True)
    )


def local(
    inputs,
    lengths,
    cotangent,
    ln1_gain,
    ln1_bias,
    w_query,
    b_query,
    w_key,
    w_value,
    b_value,
    w_attn_out,
    b_attn_out,
    ln2_gain,
    ln2_bias,
    w_in,
    b_in,
    w_out,
    b_out,
):
    chips = size_of(GROUP)
    yl_size = lax.axis_size("yl")
    columns = 8 * yl_size
    k, zh, yh = (lax.axis_index(a) for a in ("k", "zh", "yh"))
    chip = lax.axis_index(GROUP)
    pack_count, packed_width = inputs.shape
    features = packed_width // 8
    width = features * columns
    clips = lengths.shape[0]
    slot = pack_count * 8 // clips
    group = 2 * chips
    lines = -(-(slot // 8 + 1) // 64) * 64
    lanes = 8 // group
    quarter = lanes * lines
    slots = 8 * lines
    half = slots // 2
    rows = w_query.shape[0]
    block_heads = HEADS // columns
    head_dim = width // HEADS
    split = block_heads % 2 == 0
    part_heads = block_heads // 2 if split else block_heads
    heads = 2 * block_heads
    units = w_in.shape[1]
    half_units = units // 2

    def start_of(clip, j):
        return (slot * clip - j + 7) // 8

    def order_tokens(own, other):
        ordered = jnp.stack(in_order([own, other], "k")).reshape(2, 2, 2, yl_size, features, quarter)
        return ordered.transpose(0, 2, 1, 3, 4, 5).reshape(columns, features, quarter)

    def exchange(blocks):
        return lax.all_to_all(blocks, ("zh", "zl", "yh", "yl"), 0, 0)

    def join(moved):
        return moved.reshape(width, quarter).T

    def cut(tensor):
        return tensor.T.reshape(columns, features, quarter)

    def by_core(tensor, parts):
        if not parts:
            return jnp.broadcast_to(tensor[None], (2,) + tensor.shape)
        return tensor.reshape((2, tensor.shape[0] // 2) + tensor.shape[1:])

    def gather_others(shard):
        return lax.all_gather(shard, OTHERS, axis=0)

    def arrange_heads(stack):
        stack = stack.reshape(-1, 4, 4, part_heads, head_dim, 2 * rows)
        if not split:
            stack = lax.dynamic_slice_in_dim(stack, 2 * k, 2, 1)
        block = stack.shape[:2] + (1,) + stack.shape[3:]
        return join_rows(stack, pl.BlockSpec(block, lambda i: (0, 0, i, 0, 0, 0)), 4, heads * PAD, True)

    def arrange_units(stack, which):
        stack = stack.reshape(-1, 4, 2, half_units, 2 * rows)
        block = (stack.shape[0], 1, 1) + stack.shape[3:]
        return join_rows(stack, pl.BlockSpec(block, lambda i: (0, i, which, 0, 0)), 4, half_units, False)

    full_vectors = jnp.stack([ln1_gain, ln1_bias, ln2_gain, ln2_bias, b_attn_out, b_out])
    part_vector = jnp.concatenate([b_query, b_value, b_in])
    full_count = full_vectors.shape[0]
    full_by = jnp.stack(in_order(pieces_of(full_vectors, GROUP), GROUP))
    all_lengths = jnp.concatenate(in_order(pieces_of(lengths, "k"), "k"))

    taken = take_positions(inputs, slot, clips, lanes, lines)
    own_tokens, other_tokens = pick(taken, k, 0), swap(pick(taken, 1 - k, 0), "k")
    turned = [t.astype(BF).T for t in (w_query, w_key, w_value)] + [w_attn_out.astype(BF)]
    head_parts = jnp.stack([by_core(t, split) for t in turned], axis=1)
    head_parts = head_parts.reshape(2, 4 * part_heads * head_dim, rows)
    own_parts, other_parts = pick(head_parts, k, 0), swap(pick(head_parts, 1 - k, 0), "k")
    head_shard = jnp.concatenate(in_order([own_parts, other_parts], "k"), axis=1)
    head_stacked = gather_others(head_shard)

    ordered, cotangent, w_in, w_out, full_by = sync(
        order_tokens(own_tokens, other_tokens), cotangent, w_in, w_out, full_by
    )
    moved = exchange(ordered)
    full_size = full_by.size
    vector_pieces = in_order(pieces_of(jnp.concatenate([full_by.reshape(-1), part_vector]), "zh"), "zh")
    vector_pieces = in_order(pieces_of(jnp.stack(vector_pieces), "yh"), "yh")
    unit_parts = jnp.stack([by_core(w_in.astype(BF).T, True), by_core(w_out.astype(BF), True)], axis=1)
    unit_parts = unit_parts.reshape(2, units, rows)
    own_parts, other_parts = pick(unit_parts, k, 0), swap(pick(unit_parts, 1 - k, 0), "k")
    unit_shard = jnp.concatenate(in_order([own_parts, other_parts], "k"), axis=1)
    unit_shard = unit_shard.reshape(2, half_units, 2 * rows)
    unit_stacked = gather_others(unit_shard)
    taken = take_positions(cotangent, slot, clips, lanes, lines)
    own_tokens, other_tokens = pick(taken, k, 0), swap(pick(taken, 1 - k, 0), "k")
    ordered_grads = order_tokens(own_tokens, other_tokens)

    all_vectors = jnp.stack(vector_pieces, axis=1)
    part_by = all_vectors[:, :, full_size:].reshape(4, -1)
    full_by = all_vectors[:, :, :full_size].reshape(2, 2, 2, yl_size, full_count, features)
    full_by = full_by.transpose(4, 0, 2, 1, 3, 5)
    gain_one, shift_one, gain_two, shift_two, attn_shift, out_shift = full_by.reshape(full_count, 1, width)

    def head_vector(tensor):
        tensor = tensor.reshape(4, block_heads, head_dim)
        if split:
            tensor = pick(tensor.reshape(4, 2, part_heads, head_dim), k, 1)
        else:
            tensor = lax.dynamic_slice_in_dim(tensor, 2 * k, 2, 0)
        tensor = tensor.reshape(heads, head_dim)
        return jnp.pad(tensor, ((0, 0), (0, PAD - head_dim)))

    query_shift = head_vector(part_by[:, :features])
    value_shift = head_vector(part_by[:, features : 2 * features])
    unit_shift = pick(part_by[:, 2 * features :].reshape(4, 2, half_units), k, 1).reshape(-1)

    clip_length = pick(all_lengths, zh * 2 + yh, 0)

    def slots_of(part):
        j = part * lanes + jnp.repeat(jnp.arange(lanes), lines)
        return 8 * (start_of(yh, j) + jnp.tile(jnp.arange(lines), lanes)) + j - slot * yh

    own_valid = slots_of(chip * 2 + k) < clip_length
    slot_order = jnp.concatenate([slots_of((chip ^ d) * 2 + (k ^ c)) for d in range(chips) for c in range(2)])
    key_mask = jnp.where(slot_order < clip_length, 0.0, MASKED)

    lane = jnp.arange(PAD)[None, :]
    none = jnp.zeros((heads, PAD), F32)
    is_first = jnp.broadcast_to(lane == head_dim, (heads, PAD)).astype(F32)
    is_extra = jnp.broadcast_to((lane >= head_dim) & (lane < head_dim + 2), (heads, PAD)).astype(F32)
    qkv_shift = jnp.concatenate([query_shift, none, value_shift]).reshape(1, -1)
    qkv_scale = jnp.concatenate([none + head_dim**-0.5 * LOG2E, none + 1, none + 1]).reshape(1, -1)
    qkv_extra = jnp.concatenate([is_first, none, -is_extra]).reshape(1, -1)
    mask_lane = jnp.concatenate([none, is_first, none]).reshape(1, -1)

    def blocks_of(tensor):
        count = tensor.shape[0] // (2 * quarter)
        return [
            [tensor[(2 * d + c) * quarter : (2 * d + c + 1) * quarter] for c in range(2)]
            for d in range(count)
        ]

    tokens = join(moved).astype(F32)
    normal_one, scale_one, normed_part = norm_forward(tokens, gain_one, shift_one)
    normed_far = far_pieces(normed_part)
    normed_near = with_core(normed_part)
    normed_near, head_stacked = sync(normed_near, head_stacked)
    head_weights = arrange_heads(head_stacked).reshape(4, heads * PAD, width)
    normed_far, ordered_grads = sync(normed_far, ordered_grads)
    moved_grads = exchange(ordered_grads)
    qkv_weights = head_weights[:3].reshape(3 * heads * PAD, width)
    attn_weights = head_weights[3]

    def qkv(rows_d, d):
        mask_d = key_mask[d * 2 * quarter : (d + 1) * 2 * quarter, None]
        product = (dot(rows_d, qkv_weights, 1, 1) + qkv_shift) * qkv_scale
        return (product + qkv_extra + mask_d * mask_lane).astype(BF)

    packed_near = qkv(normed_near, 0)
    normed_rows = [normed_near] + [with_core(v) for v in normed_far]
    packed = jnp.concatenate(
        [packed_near] + [qkv(v, d) for d, v in enumerate(normed_rows) if d], axis=0
    )
    far_context, far_wide, far_weights = attend(packed, heads, 1)

    def attn_product(v):
        return dot(v, attn_weights, 1, 0)

    near_chips = chips // 2
    far_sums = [cores_sum(attn_product, b).astype(BF) for b in blocks_of(far_context)]
    far_sums, packed, moved_grads = sync(far_sums, packed, moved_grads)
    far_total = send_far(far_sums) if near_chips == 1 else None
    near_context, near_wide, near_weights = attend(packed, heads, 0)
    normed = jnp.concatenate(normed_rows, axis=0)
    grad_low = jnp.where(own_valid[:, None], join(moved_grads), jnp.zeros((quarter, width), BF))
    if near_chips == 1:
        near_context, far_total, normed, grad_low = sync(near_context, far_total, normed, grad_low)
    near_sums = [cores_sum(attn_product, b) for b in blocks_of(near_context)]
    if near_chips > 1:
        far_total = send_far((near_sums + far_sums)[1:])
    grad_far = far_pieces(grad_low)
    grad_near = with_core(grad_low)
    attn_part = near_sums[0] + far_total + attn_shift
    middle = tokens + attn_part
    normal_two, scale_two, normed_two_part = norm_forward(middle, gain_two, shift_two)
    two_near = with_core(normed_two_part)
    two_far = far_pieces(normed_two_part)
    two_near, unit_stacked, grad_far = sync(two_near, unit_stacked, grad_far)
    in_weights = arrange_units(unit_stacked, 0)
    out_weights = arrange_units(unit_stacked, 1)

    def feed(rows_d):
        hidden = dot(rows_d, in_weights, 1, 1) + unit_shift
        below = 0.5 * (1.0 + lax.erf(hidden * 0.5**0.5))
        slope = below + hidden * (jnp.exp(-0.5 * hidden * hidden) * (0.5 / jnp.pi) ** 0.5)
        return (hidden * below).astype(BF), slope

    def feed_back(grad_d, slope):
        return (dot(grad_d, out_weights, 1, 1) * slope).astype(BF)

    near_active, near_slope = feed(two_near)
    near_hidden = feed_back(grad_near, near_slope)
    near_hidden, two_far = sync(near_hidden, two_far)
    two_rows = [two_near] + [with_core(v) for v in two_far]
    far_feed = [feed(v) for v in two_rows[1:]]
    grad_rows = [grad_near] + [with_core(v) for v in grad_far]
    grad_hidden = jnp.concatenate(
        [near_hidden] + [feed_back(g, f[1]) for g, f in zip(grad_rows[1:], far_feed)], axis=0
    )
    active = jnp.concatenate([near_active] + [f[0] for f in far_feed], axis=0)

    def in_product(v):
        return dot(v, in_weights, 1, 0)

    hidden_blocks = blocks_of(grad_hidden)
    far_two = [cores_sum(in_product, b).astype(BF) for b in hidden_blocks[1:]]
    grad_hidden, near_blocks, far_two, active = sync(grad_hidden, hidden_blocks[0], far_two, active)
    near_two = cores_sum(in_product, near_blocks)
    normed_two = jnp.concatenate(two_rows, axis=0)
    grad_full = jnp.concatenate(grad_rows, axis=0)

    out_total = dot(active, grad_full, 0, 0).astype(BF).reshape(2, 2, half_units, width)
    in_total = dot(grad_hidden, normed_two, 0, 0).astype(BF).reshape(2, 2, half_units, width)
    two_arrived, active, out_total, in_total = sync(send_far(far_two), active, out_total, in_total)
    out_half = send_units(out_total, "yh", 1)
    in_half = send_rows(in_total)
    grad_two = near_two + two_arrived
    grad_out = grad_low.astype(F32)
    grad_middle = grad_out + norm_backward(grad_two, normal_two, scale_two, gain_two)
    grad_mid_part = grad_middle.astype(BF)
    mid_far = far_pieces(grad_mid_part)
    mid_near = with_core(grad_mid_part)

    def context_grad(v):
        return dot(v, attn_weights, 1, 1).astype(BF)

    def out_product(v):
        return dot(v, out_weights, 1, 0)

    mid_half = jnp.concatenate([mid_near] + [with_core(v) for v in mid_far[: near_chips - 1]], axis=0)
    near_grad = context_grad(mid_half)
    active_blocks = blocks_of(active)
    delta_given = swap(jnp.concatenate([out_product(b[1]).astype(BF) for b in active_blocks]), "k")
    delta_cores = [
        out_product(b[0]) + delta_given[d * quarter : (d + 1) * quarter].astype(F32)
        for d, b in enumerate(active_blocks)
    ]
    near_delta, far_delta = delta_cores[0], [v.astype(BF) for v in delta_cores[1:]]
    near_grad, near_delta, far_delta = sync(near_grad, near_delta, far_delta)
    first = attend_back(packed, near_grad, near_wide, near_weights, heads, head_dim, 0)
    first, mid_far, far_delta, out_half, in_half = sync(first, mid_far, far_delta, out_half, in_half)
    delta_far = send_far(far_delta)
    out_half = send_rows(summed(out_half))
    in_half = send_units(summed(in_half), "yh", 1)
    mid_rows = [mid_near] + [with_core(v) for v in mid_far]
    mid_full = jnp.concatenate(mid_rows, axis=0)
    far_grad = context_grad(mid_full[half:])
    grads = attend_back(packed, far_grad, far_wide, far_weights, heads, head_dim, 1, list(first))
    qkv_cube = qkv_weights.reshape(3, heads * PAD, width)

    def qkv_product(v):
        return sum(dot(v[j], qkv_cube[j], 1, 0) for j in range(3))

    grad_blocks = [
        [grads[:, (2 * d + c) * quarter : (2 * d + c + 1) * quarter] for c in range(2)] for d in range(chips)
    ]
    far_one = [cores_sum(qkv_product, b).astype(BF) for b in grad_blocks[1:]]
    grads, far_one, near_blocks, out_half, in_half = sync(grads, far_one, grad_blocks[0], out_half, in_half)
    far_arrived = send_far(far_one)
    near_one = cores_sum(qkv_product, near_blocks)
    unit_sums = jnp.stack([summed(out_half), summed(in_half)])
    far_arrived, unit_sums = sync(far_arrived, unit_sums)
    unit_half = send_units(unit_sums, "zh", 1)
    context = jnp.concatenate([near_context, far_context], axis=0)
    grads, near_one, delta_far, context, mid_rows = sync(grads, near_one, delta_far, context, mid_rows)
    mid_full = jnp.concatenate(mid_rows, axis=0)

    def trim(total):
        return total.reshape(-1, part_heads, PAD, width)[:, :, :head_dim].reshape(-1, part_heads * head_dim, width)

    def head_chunk(totals):
        chunk = jnp.stack([trim(t) for t in totals], axis=1).reshape(-1, len(totals) * part_heads * head_dim, width)
        if not split:
            blank = jnp.zeros((4,) + chunk.shape[1:], BF)
            chunk = lax.dynamic_update_slice_in_dim(blank, chunk, 2 * k, 0)
        return chunk.reshape((2, 2) + chunk.shape[1:])

    query_key = head_chunk([dot(grads[j], normed, 0, 0).astype(BF) for j in range(2)])
    value_attn = head_chunk([dot(grads[2], normed, 0, 0).astype(BF), dot(context, mid_full, 0, 0).astype(BF)])
    query_key_half = send_rows(query_key)
    value_attn_half = send_units(value_attn, "yh", 1)
    grad_one = near_one + far_arrived
    grad_tokens = norm_backward(grad_one, normal_one, scale_one, gain_one)
    last_part = (grad_middle + grad_tokens).astype(BF)
    moved_last = exchange(cut(last_part))
    delta = (attn_part + near_delta + delta_far + out_shift).astype(BF)

    full_sums = jnp.stack(
        [
            jnp.sum(v, axis=0)
            for v in (
                grad_one * normal_one,
                grad_one,
                grad_middle,
                grad_two * normal_two,
                grad_two,
                grad_out,
            )
        ]
    )

    def head_sums(tensor):
        total = jnp.sum(tensor.astype(F32), axis=0).reshape(-1, part_heads, PAD)[:, :, :head_dim]
        if not split:
            blank = jnp.zeros((4,) + total.shape[1:], F32)
            total = lax.dynamic_update_slice_in_dim(blank, total, 2 * k, 0)
        return total.reshape(4, -1)

    part_sums = jnp.concatenate(
        [
            head_sums(grads[0]),
            head_sums(grads[2]),
            jnp.sum(grad_hidden.astype(F32), axis=0).reshape(4, half_units),
        ],
        axis=1,
    )
    full_sums = full_sums.reshape(full_count, 2, 2, 2, yl_size, features).transpose(1, 3, 2, 4, 0, 5)
    full_size = full_sums[0, 0].size
    flat = jnp.concatenate([full_sums.reshape(2, 2, -1), part_sums.reshape(2, 2, -1)], axis=2)
    flat_pieces = pieces_of(flat, "x")
    query_key_half, value_attn_half, flat_pieces = sync(query_key_half, value_attn_half, flat_pieces)
    query_key_half = send_units(summed(query_key_half), "yh", 1)
    value_attn_half = send_rows(summed(value_attn_half))
    flat_half = send_units(sum(flat_pieces), "yh", 1)
    moved_last, query_key_half, value_attn_half, delta_blocks, flat_half, unit_half = sync(
        moved_last, query_key_half, value_attn_half, cut(delta), flat_half, unit_half
    )
    moved_delta = exchange(delta_blocks)
    head_half = send_units(jnp.stack([summed(query_key_half), summed(value_attn_half)]), "zh", 1)

    def two_cores(total, two):
        last = total.ndim - 1
        kept = lax.dynamic_slice_in_dim(total, k * rows, rows, last)
        other = swap(lax.dynamic_slice_in_dim(total, (1 - k) * rows, rows, last), "k")
        if not two:
            return kept.astype(F32) + other.astype(F32)
        return jnp.stack(in_order([kept, other], "k"), axis=1).astype(F32)

    def kept_tokens(moved):
        moved = moved.reshape(2, 2, 2, yl_size, features, quarter).transpose(0, 2, 1, 3, 4, 5)
        kept = pick(moved, k, 0)
        other = swap(pick(moved, 1 - k, 0), "k")
        ordered = jnp.stack(in_order([kept, other], "k"))
        return ordered.reshape(2, clips, chips, features, quarter)

    def put(tokens, base=None):
        return put_positions(tokens, slot, pack_count, lanes, lines, base)

    flat_half = send_units(sum(flat_half), "zh", 0)
    input_grad, moved_delta, flat_half = sync(put(kept_tokens(moved_last)), moved_delta, flat_half)
    flat = sum(flat_half)
    full_flat, part_flat = flat[:full_size], flat[full_size:]

    by_chip = full_flat.reshape(chips, -1)
    mine = pick(by_chip, chip, 0)
    for d in range(1, chips):
        mine = mine + swap(pick(by_chip, chip ^ d, 0), GROUP, d)
    unit_cores = two_cores(summed(unit_half), True)
    grad_out_w = unit_cores[0].reshape(units, rows)
    grad_in_w = unit_cores[1].reshape(units, rows).T
    layer_out = put(kept_tokens(moved_delta), inputs)
    input_grad, head_half, mine = sync(input_grad, head_half, mine)
    head_cores = two_cores(summed(head_half), split)
    head_cores = head_cores.reshape(2, -1, 2, part_heads * head_dim, rows)
    grad_query_w, grad_key_w, grad_value_w, grad_attn_w = (
        head_cores[i, :, j].reshape(features, rows) for i in range(2) for j in range(2)
    )

    own_size = mine.shape[0]
    last_pair = pieces_of(jnp.concatenate([mine, part_flat]), "k")
    vec_one_gain, vec_one_bias, vec_battn, vec_two_gain, vec_two_bias, vec_bout = (
        last_pair[0][:own_size] + last_pair[1][:own_size]
    ).reshape(full_count, features)
    head_size = part_heads * head_dim
    cores = in_order([p[own_size:] for p in last_pair], "k")
    if split:
        vec_bquery = jnp.concatenate([c[:head_size] for c in cores])
        vec_bvalue = jnp.concatenate([c[head_size : 2 * head_size] for c in cores])
    else:
        vec_bquery = cores[0][:head_size] + cores[1][:head_size]
        vec_bvalue = cores[0][head_size : 2 * head_size] + cores[1][head_size : 2 * head_size]
    vec_bin = jnp.concatenate([c[2 * head_size :] for c in cores])

    return (
        layer_out,
        input_grad,
        vec_one_gain,
        vec_one_bias,
        grad_query_w.T,
        vec_bquery,
        grad_key_w.T,
        grad_value_w.T,
        vec_bvalue,
        grad_attn_w,
        vec_battn,
        vec_two_gain,
        vec_two_bias,
        grad_in_w,
        vec_bin,
        grad_out_w,
        vec_bout,
    )


def solution(mesh):
    row_size, col_size = mesh.shape["row"], mesh.shape["col"]
    shape = (row_size // 2, 2, 2, 2, 2, col_size // 8)
    row, col = ("x", "k"), ("zh", "zl", "yh", "yl")
    grid = Mesh(mesh.devices.reshape(shape), row + col)
    return jax.shard_map(
        local,
        mesh=grid,
        in_specs=(
            P(row, col),
            P(row),
            P(row, col),
            P(col),
            P(col),
            P(row, col),
            P(col),
            P(row, col),
            P(row, col),
            P(col),
            P(col, row),
            P(col),
            P(col),
            P(col),
            P(row, col),
            P(col),
            P(col, row),
            P(col),
        ),
        out_specs=(
            P(row, col),
            P(row, col),
            P(col),
            P(col),
            P(row, col),
            P(col),
            P(row, col),
            P(row, col),
            P(col),
            P(col, row),
            P(col),
            P(col),
            P(col),
            P(row, col),
            P(col),
            P(col, row),
            P(col),
        ),
        check_vma=False,
    )
```

```python
import functools

import jax
import jax.numpy as jnp
from jax import lax
from jax.experimental import pallas as pl
from jax.experimental.pallas import tpu as pltpu
from jax.sharding import Mesh
from jax.sharding import PartitionSpec as P

HEADS = 16
EPSILON = 1e-05
PAD = 128
LOG2E = 1.4426950408889634
LN2 = 0.6931471805599453
MASKED = -1e30
BF = jnp.bfloat16
F32 = jnp.float32


def dot(first, second, left, right):
    return lax.dot_general(
        first, second, (((left,), (right,)), ((), ())), preferred_element_type=F32
    )


GROUP = ("zl", "yl")
OTHERS = ("x", "zh", "yh")


def size_of(axis):
    names = axis if isinstance(axis, tuple) else (axis,)
    total = 1
    for name in names:
        total *= lax.axis_size(name)
    return total


def swap(tensor, axis, step=1):
    return lax.ppermute(tensor, axis, [(i, i ^ step) for i in range(size_of(axis))])


def in_order(pieces, axis):
    mine = lax.axis_index(axis)
    if len(pieces) == 1:
        return pieces
    if len(pieces) == 2:
        return [lax.select_n((mine ^ j) == 1, *pieces) for j in range(2)]
    return [lax.select_n(mine ^ j, *pieces) for j in range(len(pieces))]


def pieces_of(tensor, axis):
    return [tensor] + [swap(tensor, axis, d) for d in range(1, size_of(axis))]


def pick(tensor, index, axis):
    return lax.dynamic_index_in_dim(tensor, index, axis, keepdims=False)


def sync(*values):
    return lax.optimization_barrier(values)


def far_pieces(part):
    return [swap(part, GROUP, d) for d in range(1, size_of(GROUP))]


def with_core(part):
    return jnp.concatenate([part, swap(part, "k")], axis=0)


def cores_sum(product, blocks):
    given = swap(product(blocks[1]).astype(BF), "k").astype(F32)
    return product(blocks[0]) + given


def send_far(sums):
    total = swap(sums[0].astype(BF), GROUP, 1).astype(F32)
    for d in range(2, len(sums) + 1):
        total = total + swap(sums[d - 1].astype(BF), GROUP, d).astype(F32)
    return total


def send_units(total, axis, dim):
    mine = lax.axis_index(axis)
    return pick(total, mine, dim), swap(pick(total, 1 - mine, dim), axis)


def send_rows(total):
    x, count = lax.axis_index("x"), lax.axis_size("x")
    last = total.ndim - 1
    side = total.shape[last] // count
    parts = [lax.dynamic_slice_in_dim(total, (x ^ d) * side, side, last) for d in range(count)]
    return tuple(parts[:1] + [swap(parts[d], "x", d) for d in range(1, count)])


def summed(parts):
    return sum(p.astype(F32) for p in parts).astype(BF)


def join_body(padded, stack_ref, out_ref):
    count, blocks = stack_ref.shape[:2]
    side = stack_ref.shape[-1]
    for x in range(count):
        columns = slice(x * side, (x + 1) * side)
        if not padded:
            out_ref[:, columns] = stack_ref[x, 0, 0]
            continue
        head_dim = stack_ref.shape[-2]
        for p in range(blocks):
            for h in range(stack_ref.shape[3]):
                at = (p * stack_ref.shape[3] + h) * PAD
                out_ref[at : at + head_dim, columns] = stack_ref[x, p, 0, h]
                out_ref[at + head_dim : at + PAD, columns] = jnp.zeros((PAD - head_dim, side), BF)


def join_rows(stack, in_spec, grid, out_block, padded):
    width = stack.shape[-1] * stack.shape[0]
    return pl.pallas_call(
        functools.partial(join_body, padded),
        grid=(grid,),
        in_specs=[in_spec],
        out_specs=pl.BlockSpec((out_block, width), lambda i: (i, 0)),
        out_shape=jax.ShapeDtypeStruct((grid * out_block, width), BF),
        compiler_params=pltpu.CompilerParams(vmem_limit_bytes=32 * 2**20),
        cost_estimate=pl.CostEstimate(flops=1000, bytes_accessed=1000, transcendentals=0),
    )(stack)


def first_rows(slot, clips):
    return [[(slot * c - j + 7) // 8 for j in range(8)] for c in range(clips + 1)]


def take_body(starts, lanes, lines, packed_ref, out_ref, low):
    part = pl.program_id(0)
    count, packed_width = packed_ref.shape
    features = packed_width // 8
    choices = [(c, n) for c, row in enumerate(starts) for n in range(len(row))]

    @pl.when(part == 0)
    def _():
        packed = packed_ref[...].astype(F32)
        tail = max(row[-1][0] for row in starts) + lines - count
        packed = jnp.concatenate([packed, jnp.zeros((tail + -(tail + count) % 8, packed_width), F32)], axis=0)
        for at, (c, n) in enumerate(choices):
            start = starts[c][n][0]
            low[at] = packed[start : start + lines].astype(BF)

    source = lax.broadcasted_iota(jnp.int32, (packed_width, features), 0)
    target = lax.broadcasted_iota(jnp.int32, (packed_width, features), 1)
    for clip, row in enumerate(starts):
        taken = []
        for lane in range(lanes):
            position = part * lanes + lane
            choose = jnp.where(source == target * 8 + position, 1.0, 0.0).astype(BF)
            at = choices.index((clip, 0))
            for n in range(1, len(row)):
                at = jnp.where(position < row[n][1], choices.index((clip, n)), at)
            taken.append(dot(choose, low[at], 0, 1))
        out_ref[0, clip, 0] = jnp.concatenate(taken, axis=1).astype(BF)


def starts_by_clip(slot, clips):
    result = []
    for row in first_rows(slot, clips)[:-1]:
        result.append([(value, sum(v >= value for v in row)) for value in sorted(set(row))])
    return result


def take_positions(packed, slot, clips, lanes, lines):
    count, packed_width = packed.shape
    features = packed_width // 8
    starts = starts_by_clip(slot, clips)
    chips = 8 // (2 * lanes)
    return pl.pallas_call(
        functools.partial(take_body, starts, lanes, lines),
        grid=(8 // lanes,),
        in_specs=[pl.BlockSpec((count, packed_width), lambda j: (0, 0))],
        out_specs=pl.BlockSpec((1, clips, 1, features, lanes * lines), lambda j: (j % 2, 0, j // 2, 0, 0)),
        out_shape=jax.ShapeDtypeStruct((2, clips, chips, features, lanes * lines), BF),
        scratch_shapes=[pltpu.VMEM((sum(len(r) for r in starts), lines, packed_width), BF)],
        compiler_params=pltpu.CompilerParams(vmem_limit_bytes=32 * 2**20),
        cost_estimate=pl.CostEstimate(flops=1000, bytes_accessed=1000, transcendentals=0),
    )(packed)


def put_body(rows, lanes, lines, added, *refs):
    base_ref, tokens_ref, out_ref, total = refs if added else (None,) + refs
    half = pl.program_id(0)
    count, packed_width = out_ref.shape
    features = packed_width // 8
    chips = tokens_ref.shape[2]
    source = lax.broadcasted_iota(jnp.int32, (4 * features, packed_width), 0)
    target = lax.broadcasted_iota(jnp.int32, (4 * features, packed_width), 1)
    position = source // features
    wanted = (source - position * features) * 8 + position + 4 * half
    choose = jnp.where(wanted == target, 1.0, 0.0).astype(BF)
    line = lax.broadcasted_iota(jnp.int32, (lines, 1), 0)

    @pl.when(half == 0)
    def _():
        total[...] = jnp.zeros_like(total)

    for clip in range(len(rows) - 1):
        blocks = [
            tokens_ref[core, clip, chip][:, lane * lines : (lane + 1) * lines]
            for chip in range(chips)
            for core in range(2)
            for lane in range(lanes)
        ]
        placed = dot(jnp.concatenate(blocks, axis=0), choose, 0, 0)
        for h in range(2):
            start, stop = rows[clip][4 * h], rows[clip + 1][4 * h]

            @pl.when(half == h)
            def _(start=start, stop=stop, placed=placed):
                total[start : start + lines] += jnp.where(line < stop - start, placed, 0.0)

    @pl.when(half == 1)
    def _():
        out_ref[...] = total[:count] + base_ref[...] if added else total[:count]


def put_positions(tokens, slot, count, lanes, lines, base=None):
    _, clips, chips, features, quarter = tokens.shape
    packed_width = features * 8
    rows = first_rows(slot, clips)
    assert all(len(set(row[:4])) == 1 and len(set(row[4:])) == 1 for row in rows)
    whole = pl.BlockSpec((count, packed_width), lambda h: (0, 0))
    in_specs = [pl.BlockSpec((2, clips, chips // 2, features, quarter), lambda h: (0, 0, h, 0, 0))]
    given = [tokens]
    if base is not None:
        in_specs, given = [whole] + in_specs, [base] + given
    last = max(max(row) for row in rows[:-1]) + lines
    return pl.pallas_call(
        functools.partial(put_body, rows, lanes, lines, base is not None),
        grid=(2,),
        in_specs=in_specs,
        out_specs=whole,
        out_shape=jax.ShapeDtypeStruct((count, packed_width), F32),
        scratch_shapes=[pltpu.VMEM((-(-last // 16) * 16, packed_width), F32)],
        compiler_params=pltpu.CompilerParams(vmem_limit_bytes=40 * 2**20),
        cost_estimate=pl.CostEstimate(flops=1000, bytes_accessed=1000, transcendentals=0),
    )(*given)


def forward_body(query_ref, key_ref, value_ref, context_ref, wide_ref, weights_ref):
    scores = dot(key_ref[...], query_ref[...], 1, 1)
    top = jnp.max(scores, axis=0, keepdims=True)
    powers = jnp.exp2(scores - top)
    total = jnp.sum(powers, axis=0, keepdims=True)
    weights = (powers * (1.0 / total)).astype(BF)
    weights_ref[0] = weights
    context = dot(value_ref[...], weights, 0, 0).T
    context_ref[...] = context.astype(BF)
    wide_ref[...] = context


def attend(packed, heads, part):
    slots = packed.shape[0]
    block = slots // 2
    return pl.pallas_call(
        forward_body,
        grid=(heads,),
        in_specs=[
            pl.BlockSpec((block, PAD), lambda h: (part, h)),
            pl.BlockSpec((slots, PAD), lambda h: (0, heads + h)),
            pl.BlockSpec((slots, PAD), lambda h: (0, 2 * heads + h)),
        ],
        out_specs=[
            pl.BlockSpec((block, PAD), lambda h: (0, h)),
            pl.BlockSpec((block, PAD), lambda h: (0, h)),
            pl.BlockSpec((1, slots, block), lambda h: (h, 0, 0)),
        ],
        out_shape=[
            jax.ShapeDtypeStruct((block, heads * PAD), BF),
            jax.ShapeDtypeStruct((block, heads * PAD), F32),
            jax.ShapeDtypeStruct((heads, slots, block), BF),
        ],
        compiler_params=pltpu.CompilerParams(vmem_limit_bytes=50 * 2**20),
        cost_estimate=pl.CostEstimate(flops=1000, bytes_accessed=1000, transcendentals=0),
    )(packed, packed, packed)


def backward_part(head_dim, query, key, value, grad, context, weights):
    wide = grad.astype(F32)
    inner = jnp.sum(wide * context, axis=1, keepdims=True)
    inner_high = inner.astype(BF).astype(F32)
    lane = lax.broadcasted_iota(jnp.int32, grad.shape, 1)
    extended = jnp.where(
        lane == head_dim,
        inner_high,
        jnp.where(lane == head_dim + 1, inner - inner_high, wide),
    ).astype(BF)
    centered = dot(value, extended, 1, 1)
    grad_scores = (weights.astype(F32) * centered).astype(BF)
    grad_value = dot(weights, grad, 1, 0)
    grad_key = dot(grad_scores, query, 1, 0)
    grad_query = (dot(key, grad_scores, 0, 0) * head_dim**-0.5).T
    return grad_query.astype(BF), grad_key, grad_value


def first_body(head_dim, query, key, value, grad, context, weights, query_out, key_out, value_out):
    query_out[...], key_out[...], value_out[...] = backward_part(
        head_dim, query[...], key[...], value[...], grad[...], context[...], weights[0]
    )


def second_body(
    head_dim, query, key, value, grad, context, weights, first_query, first_key, first_value, out_ref
):
    grad_query, grad_key, grad_value = backward_part(
        head_dim, query[...], key[...], value[...], grad[...], context[...], weights[0]
    )
    block = grad_query.shape[0]
    out_ref[0, :block] = first_query[...]
    out_ref[0, block:] = grad_query
    out_ref[1] = ((grad_key + first_key[...]) * LN2).astype(BF)
    out_ref[2] = (grad_value + first_value[...]).astype(BF)


def attend_back(packed, grad_context, context, weights, heads, head_dim, part, first=None):
    slots = packed.shape[0]
    block = slots // 2
    half = pl.BlockSpec((block, PAD), lambda h: (0, h))
    whole = pl.BlockSpec((slots, PAD), lambda h: (0, h))
    in_specs = [
        pl.BlockSpec((block, PAD), lambda h: (part, h)),
        pl.BlockSpec((slots, PAD), lambda h: (0, heads + h)),
        pl.BlockSpec((slots, PAD), lambda h: (0, 2 * heads + h)),
        half,
        half,
        pl.BlockSpec((1, slots, block), lambda h: (h, 0, 0)),
    ]
    given = [packed, packed, packed, grad_context, context, weights]
    if first is None:
        body = first_body
        out_specs = [half, whole, whole]
        out_shape = [
            jax.ShapeDtypeStruct((block, heads * PAD), BF),
            jax.ShapeDtypeStruct((slots, heads * PAD), F32),
            jax.ShapeDtypeStruct((slots, heads * PAD), F32),
        ]
    else:
        body = second_body
        in_specs += [half, whole, whole]
        given += first
        out_specs = pl.BlockSpec((3, slots, PAD), lambda h: (0, 0, h))
        out_shape = jax.ShapeDtypeStruct((3, slots, heads * PAD), BF)
    return pl.pallas_call(
        functools.partial(body, head_dim),
        grid=(heads,),
        in_specs=in_specs,
        out_specs=out_specs,
        out_shape=out_shape,
        compiler_params=pltpu.CompilerParams(vmem_limit_bytes=56 * 2**20),
        cost_estimate=pl.CostEstimate(flops=1000, bytes_accessed=1000, transcendentals=0),
    )(*given)


def norm_forward(tensor, gain, shift):
    centered = tensor - jnp.mean(tensor, axis=1, keepdims=True)
    scale = lax.rsqrt(jnp.mean(centered * centered, axis=1, keepdims=True) + EPSILON)
    normal = centered * scale
    return normal, scale, (normal * gain + shift).astype(BF)


def norm_backward(grad, normal, scale, gain):
    weighted = grad * gain
    return scale * (
        weighted
        - jnp.mean(weighted, axis=1, keepdims=True)
        - normal * jnp.mean(weighted * normal, axis=1, keepdims=True)
    )


def local(
    inputs,
    lengths,
    cotangent,
    ln1_gain,
    ln1_bias,
    w_query,
    b_query,
    w_key,
    w_value,
    b_value,
    w_attn_out,
    b_attn_out,
    ln2_gain,
    ln2_bias,
    w_in,
    b_in,
    w_out,
    b_out,
):
    chips = size_of(GROUP)
    yl_size = lax.axis_size("yl")
    columns = 8 * yl_size
    k, zh, yh = (lax.axis_index(a) for a in ("k", "zh", "yh"))
    chip = lax.axis_index(GROUP)
    pack_count, packed_width = inputs.shape
    features = packed_width // 8
    width = features * columns
    clips = lengths.shape[0]
    slot = pack_count * 8 // clips
    group = 2 * chips
    lines = -(-(slot // 8 + 1) // 64) * 64
    lanes = 8 // group
    quarter = lanes * lines
    slots = 8 * lines
    half = slots // 2
    rows = w_query.shape[0]
    block_heads = HEADS // columns
    head_dim = width // HEADS
    split = block_heads % 2 == 0
    part_heads = block_heads // 2 if split else block_heads
    heads = 2 * block_heads
    units = w_in.shape[1]
    half_units = units // 2

    def start_of(clip, j):
        return (slot * clip - j + 7) // 8

    def order_tokens(own, other):
        ordered = jnp.stack(in_order([own, other], "k")).reshape(2, 2, 2, yl_size, features, quarter)
        return ordered.transpose(0, 2, 1, 3, 4, 5).reshape(columns, features, quarter)

    def exchange(blocks):
        return lax.all_to_all(blocks, ("zh", "zl", "yh", "yl"), 0, 0)

    def join(moved):
        return moved.reshape(width, quarter).T

    def cut(tensor):
        return tensor.T.reshape(columns, features, quarter)

    def by_core(tensor, parts):
        if not parts:
            return jnp.broadcast_to(tensor[None], (2,) + tensor.shape)
        return tensor.reshape((2, tensor.shape[0] // 2) + tensor.shape[1:])

    def gather_others(shard):
        return lax.all_gather(shard, OTHERS, axis=0)

    def arrange_heads(stack):
        stack = stack.reshape(-1, 4, 4, part_heads, head_dim, 2 * rows)
        if not split:
            stack = lax.dynamic_slice_in_dim(stack, 2 * k, 2, 1)
        block = stack.shape[:2] + (1,) + stack.shape[3:]
        return join_rows(stack, pl.BlockSpec(block, lambda i: (0, 0, i, 0, 0, 0)), 4, heads * PAD, True)

    def arrange_units(stack, which):
        stack = stack.reshape(-1, 4, 2, half_units, 2 * rows)
        block = (stack.shape[0], 1, 1) + stack.shape[3:]
        return join_rows(stack, pl.BlockSpec(block, lambda i: (0, i, which, 0, 0)), 4, half_units, False)

    full_vectors = jnp.stack([ln1_gain, ln1_bias, ln2_gain, ln2_bias, b_attn_out, b_out])
    part_vector = jnp.concatenate([b_query, b_value, b_in])
    full_count = full_vectors.shape[0]
    full_by = jnp.stack(in_order(pieces_of(full_vectors, GROUP), GROUP))
    all_lengths = jnp.concatenate(in_order(pieces_of(lengths, "k"), "k"))

    taken = take_positions(inputs, slot, clips, lanes, lines)
    own_tokens, other_tokens = pick(taken, k, 0), swap(pick(taken, 1 - k, 0), "k")
    turned = [t.astype(BF).T for t in (w_query, w_key, w_value)] + [w_attn_out.astype(BF)]
    head_parts = jnp.stack([by_core(t, split) for t in turned], axis=1)
    head_parts = head_parts.reshape(2, 4 * part_heads * head_dim, rows)
    own_parts, other_parts = pick(head_parts, k, 0), swap(pick(head_parts, 1 - k, 0), "k")
    head_shard = jnp.concatenate(in_order([own_parts, other_parts], "k"), axis=1)
    head_stacked = gather_others(head_shard)

    ordered, cotangent, w_in, w_out, full_by = sync(
        order_tokens(own_tokens, other_tokens), cotangent, w_in, w_out, full_by
    )
    moved = exchange(ordered)
    full_size = full_by.size
    vector_pieces = in_order(pieces_of(jnp.concatenate([full_by.reshape(-1), part_vector]), "zh"), "zh")
    vector_pieces = in_order(pieces_of(jnp.stack(vector_pieces), "yh"), "yh")
    unit_parts = jnp.stack([by_core(w_in.astype(BF).T, True), by_core(w_out.astype(BF), True)], axis=1)
    unit_parts = unit_parts.reshape(2, units, rows)
    own_parts, other_parts = pick(unit_parts, k, 0), swap(pick(unit_parts, 1 - k, 0), "k")
    unit_shard = jnp.concatenate(in_order([own_parts, other_parts], "k"), axis=1)
    unit_shard = unit_shard.reshape(2, half_units, 2 * rows)
    unit_stacked = gather_others(unit_shard)
    taken = take_positions(cotangent, slot, clips, lanes, lines)
    own_tokens, other_tokens = pick(taken, k, 0), swap(pick(taken, 1 - k, 0), "k")
    ordered_grads = order_tokens(own_tokens, other_tokens)

    all_vectors = jnp.stack(vector_pieces, axis=1)
    part_by = all_vectors[:, :, full_size:].reshape(4, -1)
    full_by = all_vectors[:, :, :full_size].reshape(2, 2, 2, yl_size, full_count, features)
    full_by = full_by.transpose(4, 0, 2, 1, 3, 5)
    gain_one, shift_one, gain_two, shift_two, attn_shift, out_shift = full_by.reshape(full_count, 1, width)

    def head_vector(tensor):
        tensor = tensor.reshape(4, block_heads, head_dim)
        if split:
            tensor = pick(tensor.reshape(4, 2, part_heads, head_dim), k, 1)
        else:
            tensor = lax.dynamic_slice_in_dim(tensor, 2 * k, 2, 0)
        tensor = tensor.reshape(heads, head_dim)
        return jnp.pad(tensor, ((0, 0), (0, PAD - head_dim)))

    query_shift = head_vector(part_by[:, :features])
    value_shift = head_vector(part_by[:, features : 2 * features])
    unit_shift = pick(part_by[:, 2 * features :].reshape(4, 2, half_units), k, 1).reshape(-1)

    clip_length = pick(all_lengths, zh * 2 + yh, 0)

    def slots_of(part):
        j = part * lanes + jnp.repeat(jnp.arange(lanes), lines)
        return 8 * (start_of(yh, j) + jnp.tile(jnp.arange(lines), lanes)) + j - slot * yh

    own_valid = slots_of(chip * 2 + k) < clip_length
    slot_order = jnp.concatenate([slots_of((chip ^ d) * 2 + (k ^ c)) for d in range(chips) for c in range(2)])
    key_mask = jnp.where(slot_order < clip_length, 0.0, MASKED)

    lane = jnp.arange(PAD)[None, :]
    none = jnp.zeros((heads, PAD), F32)
    is_first = jnp.broadcast_to(lane == head_dim, (heads, PAD)).astype(F32)
    is_extra = jnp.broadcast_to((lane >= head_dim) & (lane < head_dim + 2), (heads, PAD)).astype(F32)
    qkv_shift = jnp.concatenate([query_shift, none, value_shift]).reshape(1, -1)
    qkv_scale = jnp.concatenate([none + head_dim**-0.5 * LOG2E, none + 1, none + 1]).reshape(1, -1)
    qkv_extra = jnp.concatenate([is_first, none, -is_extra]).reshape(1, -1)
    mask_lane = jnp.concatenate([none, is_first, none]).reshape(1, -1)

    def blocks_of(tensor):
        count = tensor.shape[0] // (2 * quarter)
        return [
            [tensor[(2 * d + c) * quarter : (2 * d + c + 1) * quarter] for c in range(2)]
            for d in range(count)
        ]

    tokens = join(moved).astype(F32)
    normal_one, scale_one, normed_part = norm_forward(tokens, gain_one, shift_one)
    normed_far = far_pieces(normed_part)
    normed_near = with_core(normed_part)
    normed_near, head_stacked = sync(normed_near, head_stacked)
    head_weights = arrange_heads(head_stacked).reshape(4, heads * PAD, width)
    normed_far, ordered_grads = sync(normed_far, ordered_grads)
    moved_grads = exchange(ordered_grads)
    qkv_weights = head_weights[:3].reshape(3 * heads * PAD, width)
    attn_weights = head_weights[3]

    def qkv(rows_d, d):
        mask_d = key_mask[d * 2 * quarter : (d + 1) * 2 * quarter, None]
        product = (dot(rows_d, qkv_weights, 1, 1) + qkv_shift) * qkv_scale
        return (product + qkv_extra + mask_d * mask_lane).astype(BF)

    packed_near = qkv(normed_near, 0)
    normed_rows = [normed_near] + [with_core(v) for v in normed_far]
    packed = jnp.concatenate(
        [packed_near] + [qkv(v, d) for d, v in enumerate(normed_rows) if d], axis=0
    )
    far_context, far_wide, far_weights = attend(packed, heads, 1)

    def attn_product(v):
        return dot(v, attn_weights, 1, 0)

    near_chips = chips // 2
    far_sums = [cores_sum(attn_product, b).astype(BF) for b in blocks_of(far_context)]
    far_sums, packed, moved_grads = sync(far_sums, packed, moved_grads)
    far_total = send_far(far_sums) if near_chips == 1 else None
    near_context, near_wide, near_weights = attend(packed, heads, 0)
    normed = jnp.concatenate(normed_rows, axis=0)
    grad_low = jnp.where(own_valid[:, None], join(moved_grads), jnp.zeros((quarter, width), BF))
    if near_chips == 1:
        near_context, far_total, normed, grad_low = sync(near_context, far_total, normed, grad_low)
    near_sums = [cores_sum(attn_product, b) for b in blocks_of(near_context)]
    if near_chips > 1:
        far_total = send_far((near_sums + far_sums)[1:])
    grad_far = far_pieces(grad_low)
    grad_near = with_core(grad_low)
    attn_part = near_sums[0] + far_total + attn_shift
    middle = tokens + attn_part
    normal_two, scale_two, normed_two_part = norm_forward(middle, gain_two, shift_two)
    normed_two_part, grad_far = sync(normed_two_part, grad_far)
    two_near = with_core(normed_two_part)
    two_far = far_pieces(normed_two_part)
    two_near, unit_stacked = sync(two_near, unit_stacked)
    in_weights = arrange_units(unit_stacked, 0)
    out_weights = arrange_units(unit_stacked, 1)

    def feed(rows_d):
        hidden = dot(rows_d, in_weights, 1, 1) + unit_shift
        below = 0.5 * (1.0 + lax.erf(hidden * 0.5**0.5))
        slope = below + hidden * (jnp.exp(-0.5 * hidden * hidden) * (0.5 / jnp.pi) ** 0.5)
        return (hidden * below).astype(BF), slope

    def feed_back(grad_d, slope):
        return (dot(grad_d, out_weights, 1, 1) * slope).astype(BF)

    near_active, near_slope = feed(two_near)
    near_hidden = feed_back(grad_near, near_slope)
    near_hidden, two_far = sync(near_hidden, two_far)
    two_rows = [two_near] + [with_core(v) for v in two_far]
    far_feed = [feed(v) for v in two_rows[1:]]
    grad_rows = [grad_near] + [with_core(v) for v in grad_far]
    grad_hidden = jnp.concatenate(
        [near_hidden] + [feed_back(g, f[1]) for g, f in zip(grad_rows[1:], far_feed)], axis=0
    )
    active = jnp.concatenate([near_active] + [f[0] for f in far_feed], axis=0)

    def in_product(v):
        return dot(v, in_weights, 1, 0)

    hidden_blocks = blocks_of(grad_hidden)
    far_two = [cores_sum(in_product, b).astype(BF) for b in hidden_blocks[1:]]
    grad_hidden, near_blocks, far_two, active = sync(grad_hidden, hidden_blocks[0], far_two, active)
    near_two = cores_sum(in_product, near_blocks)
    normed_two = jnp.concatenate(two_rows, axis=0)
    grad_full = jnp.concatenate(grad_rows, axis=0)

    out_total = dot(active, grad_full, 0, 0).astype(BF).reshape(2, 2, half_units, width)
    in_total = dot(grad_hidden, normed_two, 0, 0).astype(BF).reshape(2, 2, half_units, width)
    two_arrived, active, out_total, in_total = sync(send_far(far_two), active, out_total, in_total)
    out_half = send_units(out_total, "yh", 1)
    in_half = send_rows(in_total)
    grad_two = near_two + two_arrived
    grad_out = grad_low.astype(F32)
    grad_middle = grad_out + norm_backward(grad_two, normal_two, scale_two, gain_two)
    grad_mid_part = grad_middle.astype(BF)
    mid_far = far_pieces(grad_mid_part)
    mid_near = with_core(grad_mid_part)

    def context_grad(v):
        return dot(v, attn_weights, 1, 1).astype(BF)

    def out_product(v):
        return dot(v, out_weights, 1, 0)

    mid_half = jnp.concatenate([mid_near] + [with_core(v) for v in mid_far[: near_chips - 1]], axis=0)
    near_grad = context_grad(mid_half)
    active_blocks = blocks_of(active)
    delta_given = swap(jnp.concatenate([out_product(b[1]).astype(BF) for b in active_blocks]), "k")
    delta_cores = [
        out_product(b[0]) + delta_given[d * quarter : (d + 1) * quarter].astype(F32)
        for d, b in enumerate(active_blocks)
    ]
    near_delta, far_delta = delta_cores[0], [v.astype(BF) for v in delta_cores[1:]]
    near_grad, near_delta, far_delta = sync(near_grad, near_delta, far_delta)
    first = attend_back(packed, near_grad, near_wide, near_weights, heads, head_dim, 0)
    first, mid_far, far_delta, out_half, in_half = sync(first, mid_far, far_delta, out_half, in_half)
    delta_far = send_far(far_delta)
    out_half = send_rows(summed(out_half))
    in_half = send_units(summed(in_half), "yh", 1)
    mid_rows = [mid_near] + [with_core(v) for v in mid_far]
    mid_full = jnp.concatenate(mid_rows, axis=0)
    far_grad = context_grad(mid_full[half:])
    grads = attend_back(packed, far_grad, far_wide, far_weights, heads, head_dim, 1, list(first))
    qkv_cube = qkv_weights.reshape(3, heads * PAD, width)

    def qkv_product(v):
        return sum(dot(v[j], qkv_cube[j], 1, 0) for j in range(3))

    grad_blocks = [
        [grads[:, (2 * d + c) * quarter : (2 * d + c + 1) * quarter] for c in range(2)] for d in range(chips)
    ]
    far_one = [cores_sum(qkv_product, b).astype(BF) for b in grad_blocks[1:]]
    grads, far_one, near_blocks, out_half, in_half = sync(grads, far_one, grad_blocks[0], out_half, in_half)
    far_arrived = send_far(far_one)
    near_one = cores_sum(qkv_product, near_blocks)
    unit_sums = jnp.stack([summed(out_half), summed(in_half)])
    far_arrived, unit_sums = sync(far_arrived, unit_sums)
    unit_half = send_units(unit_sums, "zh", 1)
    context = jnp.concatenate([near_context, far_context], axis=0)
    grads, near_one, delta_far, context, mid_rows = sync(grads, near_one, delta_far, context, mid_rows)
    mid_full = jnp.concatenate(mid_rows, axis=0)

    def trim(total):
        return total.reshape(-1, part_heads, PAD, width)[:, :, :head_dim].reshape(-1, part_heads * head_dim, width)

    def head_chunk(totals):
        chunk = jnp.stack([trim(t) for t in totals], axis=1).reshape(-1, len(totals) * part_heads * head_dim, width)
        if not split:
            blank = jnp.zeros((4,) + chunk.shape[1:], BF)
            chunk = lax.dynamic_update_slice_in_dim(blank, chunk, 2 * k, 0)
        return chunk.reshape((2, 2) + chunk.shape[1:])

    query_key = head_chunk([dot(grads[j], normed, 0, 0).astype(BF) for j in range(2)])
    value_attn = head_chunk([dot(grads[2], normed, 0, 0).astype(BF), dot(context, mid_full, 0, 0).astype(BF)])
    query_key_half = send_rows(query_key)
    value_attn_half = send_units(value_attn, "yh", 1)
    grad_one = near_one + far_arrived
    grad_tokens = norm_backward(grad_one, normal_one, scale_one, gain_one)
    last_part = (grad_middle + grad_tokens).astype(BF)
    moved_last = exchange(cut(last_part))
    delta = (attn_part + near_delta + delta_far + out_shift).astype(BF)

    full_sums = jnp.stack(
        [
            jnp.sum(v, axis=0)
            for v in (
                grad_one * normal_one,
                grad_one,
                grad_middle,
                grad_two * normal_two,
                grad_two,
                grad_out,
            )
        ]
    )

    def head_sums(tensor):
        total = jnp.sum(tensor.astype(F32), axis=0).reshape(-1, part_heads, PAD)[:, :, :head_dim]
        if not split:
            blank = jnp.zeros((4,) + total.shape[1:], F32)
            total = lax.dynamic_update_slice_in_dim(blank, total, 2 * k, 0)
        return total.reshape(4, -1)

    part_sums = jnp.concatenate(
        [
            head_sums(grads[0]),
            head_sums(grads[2]),
            jnp.sum(grad_hidden.astype(F32), axis=0).reshape(4, half_units),
        ],
        axis=1,
    )
    full_sums = full_sums.reshape(full_count, 2, 2, 2, yl_size, features).transpose(1, 3, 2, 4, 0, 5)
    full_size = full_sums[0, 0].size
    flat = jnp.concatenate([full_sums.reshape(2, 2, -1), part_sums.reshape(2, 2, -1)], axis=2)
    flat_pieces = pieces_of(flat, "x")
    query_key_half, value_attn_half, flat_pieces = sync(query_key_half, value_attn_half, flat_pieces)
    query_key_half = send_units(summed(query_key_half), "yh", 1)
    value_attn_half = send_rows(summed(value_attn_half))
    flat_half = send_units(sum(flat_pieces), "yh", 1)
    moved_last, query_key_half, value_attn_half, delta_blocks, flat_half, unit_half = sync(
        moved_last, query_key_half, value_attn_half, cut(delta), flat_half, unit_half
    )
    moved_delta = exchange(delta_blocks)
    head_half = send_units(jnp.stack([summed(query_key_half), summed(value_attn_half)]), "zh", 1)

    def two_cores(total, two):
        last = total.ndim - 1
        kept = lax.dynamic_slice_in_dim(total, k * rows, rows, last)
        other = swap(lax.dynamic_slice_in_dim(total, (1 - k) * rows, rows, last), "k")
        if not two:
            return kept.astype(F32) + other.astype(F32)
        return jnp.stack(in_order([kept, other], "k"), axis=1).astype(F32)

    def kept_tokens(moved):
        moved = moved.reshape(2, 2, 2, yl_size, features, quarter).transpose(0, 2, 1, 3, 4, 5)
        kept = pick(moved, k, 0)
        other = swap(pick(moved, 1 - k, 0), "k")
        ordered = jnp.stack(in_order([kept, other], "k"))
        return ordered.reshape(2, clips, chips, features, quarter)

    def put(tokens, base=None):
        return put_positions(tokens, slot, pack_count, lanes, lines, base)

    flat_half = send_units(sum(flat_half), "zh", 0)
    input_grad, moved_delta, flat_half = sync(put(kept_tokens(moved_last)), moved_delta, flat_half)
    flat = sum(flat_half)
    full_flat, part_flat = flat[:full_size], flat[full_size:]

    by_chip = full_flat.reshape(chips, -1)
    mine = pick(by_chip, chip, 0)
    for d in range(1, chips):
        mine = mine + swap(pick(by_chip, chip ^ d, 0), GROUP, d)
    unit_cores = two_cores(summed(unit_half), True)
    grad_out_w = unit_cores[0].reshape(units, rows)
    grad_in_w = unit_cores[1].reshape(units, rows).T
    layer_out = put(kept_tokens(moved_delta), inputs)
    input_grad, head_half, mine = sync(input_grad, head_half, mine)
    head_cores = two_cores(summed(head_half), split)
    head_cores = head_cores.reshape(2, -1, 2, part_heads * head_dim, rows)
    grad_query_w, grad_key_w, grad_value_w, grad_attn_w = (
        head_cores[i, :, j].reshape(features, rows) for i in range(2) for j in range(2)
    )

    own_size = mine.shape[0]
    last_pair = pieces_of(jnp.concatenate([mine, part_flat]), "k")
    vec_one_gain, vec_one_bias, vec_battn, vec_two_gain, vec_two_bias, vec_bout = (
        last_pair[0][:own_size] + last_pair[1][:own_size]
    ).reshape(full_count, features)
    head_size = part_heads * head_dim
    cores = in_order([p[own_size:] for p in last_pair], "k")
    if split:
        vec_bquery = jnp.concatenate([c[:head_size] for c in cores])
        vec_bvalue = jnp.concatenate([c[head_size : 2 * head_size] for c in cores])
    else:
        vec_bquery = cores[0][:head_size] + cores[1][:head_size]
        vec_bvalue = cores[0][head_size : 2 * head_size] + cores[1][head_size : 2 * head_size]
    vec_bin = jnp.concatenate([c[2 * head_size :] for c in cores])

    return (
        layer_out,
        input_grad,
        vec_one_gain,
        vec_one_bias,
        grad_query_w.T,
        vec_bquery,
        grad_key_w.T,
        grad_value_w.T,
        vec_bvalue,
        grad_attn_w,
        vec_battn,
        vec_two_gain,
        vec_two_bias,
        grad_in_w,
        vec_bin,
        grad_out_w,
        vec_bout,
    )


def solution(mesh):
    row_size, col_size = mesh.shape["row"], mesh.shape["col"]
    shape = (row_size // 2, 2, 2, 2, 2, col_size // 8)
    row, col = ("x", "k"), ("zh", "zl", "yh", "yl")
    grid = Mesh(mesh.devices.reshape(shape), row + col)
    return jax.shard_map(
        local,
        mesh=grid,
        in_specs=(
            P(row, col),
            P(row),
            P(row, col),
            P(col),
            P(col),
            P(row, col),
            P(col),
            P(row, col),
            P(row, col),
            P(col),
            P(col, row),
            P(col),
            P(col),
            P(col),
            P(row, col),
            P(col),
            P(col, row),
            P(col),
        ),
        out_specs=(
            P(row, col),
            P(row, col),
            P(col),
            P(col),
            P(row, col),
            P(col),
            P(row, col),
            P(row, col),
            P(col),
            P(col, row),
            P(col),
            P(col),
            P(col),
            P(row, col),
            P(col),
            P(col, row),
            P(col),
        ),
        check_vma=False,
    )
```

```python
import functools

import jax
import jax.numpy as jnp
from jax import lax
from jax.experimental import pallas as pl
from jax.experimental.pallas import tpu as pltpu
from jax.sharding import Mesh
from jax.sharding import PartitionSpec as P

HEADS = 16
EPSILON = 1e-05
PAD = 128
LOG2E = 1.4426950408889634
LN2 = 0.6931471805599453
MASKED = -1e30
BF = jnp.bfloat16
F32 = jnp.float32


def dot(first, second, left, right):
    return lax.dot_general(
        first, second, (((left,), (right,)), ((), ())), preferred_element_type=F32
    )


GROUP = ("zl", "yl")
OTHERS = ("x", "zh", "yh")


def size_of(axis):
    names = axis if isinstance(axis, tuple) else (axis,)
    total = 1
    for name in names:
        total *= lax.axis_size(name)
    return total


def swap(tensor, axis, step=1):
    return lax.ppermute(tensor, axis, [(i, i ^ step) for i in range(size_of(axis))])


def in_order(pieces, axis):
    mine = lax.axis_index(axis)
    if len(pieces) == 1:
        return pieces
    if len(pieces) == 2:
        return [lax.select_n((mine ^ j) == 1, *pieces) for j in range(2)]
    return [lax.select_n(mine ^ j, *pieces) for j in range(len(pieces))]


def pieces_of(tensor, axis):
    return [tensor] + [swap(tensor, axis, d) for d in range(1, size_of(axis))]


def pick(tensor, index, axis):
    return lax.dynamic_index_in_dim(tensor, index, axis, keepdims=False)


def sync(*values):
    return lax.optimization_barrier(values)


def far_pieces(part):
    return [swap(part, GROUP, d) for d in range(1, size_of(GROUP))]


def with_core(part):
    return jnp.concatenate([part, swap(part, "k")], axis=0)


def cores_sum(product, blocks):
    given = swap(product(blocks[1]).astype(BF), "k").astype(F32)
    return product(blocks[0]) + given


def send_far(sums):
    total = swap(sums[0].astype(BF), GROUP, 1).astype(F32)
    for d in range(2, len(sums) + 1):
        total = total + swap(sums[d - 1].astype(BF), GROUP, d).astype(F32)
    return total


def send_units(total, axis, dim):
    mine = lax.axis_index(axis)
    return pick(total, mine, dim), swap(pick(total, 1 - mine, dim), axis)


def send_rows(total):
    x, count = lax.axis_index("x"), lax.axis_size("x")
    last = total.ndim - 1
    side = total.shape[last] // count
    parts = [lax.dynamic_slice_in_dim(total, (x ^ d) * side, side, last) for d in range(count)]
    return tuple(parts[:1] + [swap(parts[d], "x", d) for d in range(1, count)])


def summed(parts):
    return sum(p.astype(F32) for p in parts).astype(BF)


def join_body(padded, stack_ref, out_ref):
    count, blocks = stack_ref.shape[:2]
    side = stack_ref.shape[-1]
    for x in range(count):
        columns = slice(x * side, (x + 1) * side)
        if not padded:
            out_ref[:, columns] = stack_ref[x, 0, 0]
            continue
        head_dim = stack_ref.shape[-2]
        for p in range(blocks):
            for h in range(stack_ref.shape[3]):
                at = (p * stack_ref.shape[3] + h) * PAD
                out_ref[at : at + head_dim, columns] = stack_ref[x, p, 0, h]
                out_ref[at + head_dim : at + PAD, columns] = jnp.zeros((PAD - head_dim, side), BF)


def join_rows(stack, in_spec, grid, out_block, padded):
    width = stack.shape[-1] * stack.shape[0]
    return pl.pallas_call(
        functools.partial(join_body, padded),
        grid=(grid,),
        in_specs=[in_spec],
        out_specs=pl.BlockSpec((out_block, width), lambda i: (i, 0)),
        out_shape=jax.ShapeDtypeStruct((grid * out_block, width), BF),
        compiler_params=pltpu.CompilerParams(vmem_limit_bytes=32 * 2**20),
        cost_estimate=pl.CostEstimate(flops=1000, bytes_accessed=1000, transcendentals=0),
    )(stack)


def first_rows(slot, clips):
    return [[(slot * c - j + 7) // 8 for j in range(8)] for c in range(clips + 1)]


def take_body(starts, lanes, lines, packed_ref, out_ref, low):
    part = pl.program_id(0)
    count, packed_width = packed_ref.shape
    features = packed_width // 8
    choices = [(c, n) for c, row in enumerate(starts) for n in range(len(row))]

    @pl.when(part == 0)
    def _():
        packed = packed_ref[...].astype(F32)
        tail = max(row[-1][0] for row in starts) + lines - count
        packed = jnp.concatenate([packed, jnp.zeros((tail + -(tail + count) % 8, packed_width), F32)], axis=0)
        for at, (c, n) in enumerate(choices):
            start = starts[c][n][0]
            low[at] = packed[start : start + lines].astype(BF)

    source = lax.broadcasted_iota(jnp.int32, (packed_width, features), 0)
    target = lax.broadcasted_iota(jnp.int32, (packed_width, features), 1)
    for clip, row in enumerate(starts):
        taken = []
        for lane in range(lanes):
            position = part * lanes + lane
            choose = jnp.where(source == target * 8 + position, 1.0, 0.0).astype(BF)
            at = choices.index((clip, 0))
            for n in range(1, len(row)):
                at = jnp.where(position < row[n][1], choices.index((clip, n)), at)
            taken.append(dot(choose, low[at], 0, 1))
        out_ref[0, clip, 0] = jnp.concatenate(taken, axis=1).astype(BF)


def starts_by_clip(slot, clips):
    result = []
    for row in first_rows(slot, clips)[:-1]:
        result.append([(value, sum(v >= value for v in row)) for value in sorted(set(row))])
    return result


def take_positions(packed, slot, clips, lanes, lines):
    count, packed_width = packed.shape
    features = packed_width // 8
    starts = starts_by_clip(slot, clips)
    chips = 8 // (2 * lanes)
    return pl.pallas_call(
        functools.partial(take_body, starts, lanes, lines),
        grid=(8 // lanes,),
        in_specs=[pl.BlockSpec((count, packed_width), lambda j: (0, 0))],
        out_specs=pl.BlockSpec((1, clips, 1, features, lanes * lines), lambda j: (j % 2, 0, j // 2, 0, 0)),
        out_shape=jax.ShapeDtypeStruct((2, clips, chips, features, lanes * lines), BF),
        scratch_shapes=[pltpu.VMEM((sum(len(r) for r in starts), lines, packed_width), BF)],
        compiler_params=pltpu.CompilerParams(vmem_limit_bytes=32 * 2**20),
        cost_estimate=pl.CostEstimate(flops=1000, bytes_accessed=1000, transcendentals=0),
    )(packed)


def put_body(rows, lanes, lines, added, *refs):
    base_ref, tokens_ref, out_ref, total = refs if added else (None,) + refs
    half = pl.program_id(0)
    count, packed_width = out_ref.shape
    features = packed_width // 8
    chips = tokens_ref.shape[2]
    source = lax.broadcasted_iota(jnp.int32, (4 * features, packed_width), 0)
    target = lax.broadcasted_iota(jnp.int32, (4 * features, packed_width), 1)
    position = source // features
    wanted = (source - position * features) * 8 + position + 4 * half
    choose = jnp.where(wanted == target, 1.0, 0.0).astype(BF)
    line = lax.broadcasted_iota(jnp.int32, (lines, 1), 0)

    @pl.when(half == 0)
    def _():
        total[...] = jnp.zeros_like(total)

    for clip in range(len(rows) - 1):
        blocks = [
            tokens_ref[core, clip, chip][:, lane * lines : (lane + 1) * lines]
            for chip in range(chips)
            for core in range(2)
            for lane in range(lanes)
        ]
        placed = dot(jnp.concatenate(blocks, axis=0), choose, 0, 0)
        for h in range(2):
            start, stop = rows[clip][4 * h], rows[clip + 1][4 * h]

            @pl.when(half == h)
            def _(start=start, stop=stop, placed=placed):
                total[start : start + lines] += jnp.where(line < stop - start, placed, 0.0)

    @pl.when(half == 1)
    def _():
        out_ref[...] = total[:count] + base_ref[...] if added else total[:count]


def put_positions(tokens, slot, count, lanes, lines, base=None):
    _, clips, chips, features, quarter = tokens.shape
    packed_width = features * 8
    rows = first_rows(slot, clips)
    assert all(len(set(row[:4])) == 1 and len(set(row[4:])) == 1 for row in rows)
    whole = pl.BlockSpec((count, packed_width), lambda h: (0, 0))
    in_specs = [pl.BlockSpec((2, clips, chips // 2, features, quarter), lambda h: (0, 0, h, 0, 0))]
    given = [tokens]
    if base is not None:
        in_specs, given = [whole] + in_specs, [base] + given
    last = max(max(row) for row in rows[:-1]) + lines
    return pl.pallas_call(
        functools.partial(put_body, rows, lanes, lines, base is not None),
        grid=(2,),
        in_specs=in_specs,
        out_specs=whole,
        out_shape=jax.ShapeDtypeStruct((count, packed_width), F32),
        scratch_shapes=[pltpu.VMEM((-(-last // 16) * 16, packed_width), F32)],
        compiler_params=pltpu.CompilerParams(vmem_limit_bytes=40 * 2**20),
        cost_estimate=pl.CostEstimate(flops=1000, bytes_accessed=1000, transcendentals=0),
    )(*given)


def forward_body(query_ref, key_ref, value_ref, context_ref, wide_ref, weights_ref):
    scores = dot(key_ref[...], query_ref[...], 1, 1)
    top = jnp.max(scores, axis=0, keepdims=True)
    powers = jnp.exp2(scores - top)
    total = jnp.sum(powers, axis=0, keepdims=True)
    weights = (powers * (1.0 / total)).astype(BF)
    weights_ref[0] = weights
    context = dot(value_ref[...], weights, 0, 0).T
    context_ref[...] = context.astype(BF)
    wide_ref[...] = context


def attend(packed, heads, part):
    slots = packed.shape[0]
    block = slots // 2
    return pl.pallas_call(
        forward_body,
        grid=(heads,),
        in_specs=[
            pl.BlockSpec((block, PAD), lambda h: (part, h)),
            pl.BlockSpec((slots, PAD), lambda h: (0, heads + h)),
            pl.BlockSpec((slots, PAD), lambda h: (0, 2 * heads + h)),
        ],
        out_specs=[
            pl.BlockSpec((block, PAD), lambda h: (0, h)),
            pl.BlockSpec((block, PAD), lambda h: (0, h)),
            pl.BlockSpec((1, slots, block), lambda h: (h, 0, 0)),
        ],
        out_shape=[
            jax.ShapeDtypeStruct((block, heads * PAD), BF),
            jax.ShapeDtypeStruct((block, heads * PAD), F32),
            jax.ShapeDtypeStruct((heads, slots, block), BF),
        ],
        compiler_params=pltpu.CompilerParams(vmem_limit_bytes=50 * 2**20),
        cost_estimate=pl.CostEstimate(flops=1000, bytes_accessed=1000, transcendentals=0),
    )(packed, packed, packed)


def backward_part(head_dim, query, key, value, grad, context, weights):
    wide = grad.astype(F32)
    inner = jnp.sum(wide * context, axis=1, keepdims=True)
    inner_high = inner.astype(BF).astype(F32)
    lane = lax.broadcasted_iota(jnp.int32, grad.shape, 1)
    extended = jnp.where(
        lane == head_dim,
        inner_high,
        jnp.where(lane == head_dim + 1, inner - inner_high, wide),
    ).astype(BF)
    centered = dot(value, extended, 1, 1)
    grad_scores = (weights.astype(F32) * centered).astype(BF)
    grad_value = dot(weights, grad, 1, 0)
    grad_key = dot(grad_scores, query, 1, 0)
    grad_query = (dot(key, grad_scores, 0, 0) * head_dim**-0.5).T
    return grad_query.astype(BF), grad_key, grad_value


def first_body(head_dim, query, key, value, grad, context, weights, query_out, key_out, value_out):
    query_out[...], key_out[...], value_out[...] = backward_part(
        head_dim, query[...], key[...], value[...], grad[...], context[...], weights[0]
    )


def second_body(
    head_dim, query, key, value, grad, context, weights, first_query, first_key, first_value, out_ref
):
    grad_query, grad_key, grad_value = backward_part(
        head_dim, query[...], key[...], value[...], grad[...], context[...], weights[0]
    )
    block = grad_query.shape[0]
    out_ref[0, :block] = first_query[...]
    out_ref[0, block:] = grad_query
    out_ref[1] = ((grad_key + first_key[...]) * LN2).astype(BF)
    out_ref[2] = (grad_value + first_value[...]).astype(BF)


def attend_back(packed, grad_context, context, weights, heads, head_dim, part, first=None):
    slots = packed.shape[0]
    block = slots // 2
    half = pl.BlockSpec((block, PAD), lambda h: (0, h))
    whole = pl.BlockSpec((slots, PAD), lambda h: (0, h))
    in_specs = [
        pl.BlockSpec((block, PAD), lambda h: (part, h)),
        pl.BlockSpec((slots, PAD), lambda h: (0, heads + h)),
        pl.BlockSpec((slots, PAD), lambda h: (0, 2 * heads + h)),
        half,
        half,
        pl.BlockSpec((1, slots, block), lambda h: (h, 0, 0)),
    ]
    given = [packed, packed, packed, grad_context, context, weights]
    if first is None:
        body = first_body
        out_specs = [half, whole, whole]
        out_shape = [
            jax.ShapeDtypeStruct((block, heads * PAD), BF),
            jax.ShapeDtypeStruct((slots, heads * PAD), F32),
            jax.ShapeDtypeStruct((slots, heads * PAD), F32),
        ]
    else:
        body = second_body
        in_specs += [half, whole, whole]
        given += first
        out_specs = pl.BlockSpec((3, slots, PAD), lambda h: (0, 0, h))
        out_shape = jax.ShapeDtypeStruct((3, slots, heads * PAD), BF)
    return pl.pallas_call(
        functools.partial(body, head_dim),
        grid=(heads,),
        in_specs=in_specs,
        out_specs=out_specs,
        out_shape=out_shape,
        compiler_params=pltpu.CompilerParams(vmem_limit_bytes=56 * 2**20),
        cost_estimate=pl.CostEstimate(flops=1000, bytes_accessed=1000, transcendentals=0),
    )(*given)


def norm_forward(tensor, gain, shift):
    centered = tensor - jnp.mean(tensor, axis=1, keepdims=True)
    scale = lax.rsqrt(jnp.mean(centered * centered, axis=1, keepdims=True) + EPSILON)
    normal = centered * scale
    return normal, scale, (normal * gain + shift).astype(BF)


def norm_backward(grad, normal, scale, gain):
    weighted = grad * gain
    return scale * (
        weighted
        - jnp.mean(weighted, axis=1, keepdims=True)
        - normal * jnp.mean(weighted * normal, axis=1, keepdims=True)
    )


def local(
    inputs,
    lengths,
    cotangent,
    ln1_gain,
    ln1_bias,
    w_query,
    b_query,
    w_key,
    w_value,
    b_value,
    w_attn_out,
    b_attn_out,
    ln2_gain,
    ln2_bias,
    w_in,
    b_in,
    w_out,
    b_out,
):
    chips = size_of(GROUP)
    yl_size = lax.axis_size("yl")
    columns = 8 * yl_size
    k, zh, yh = (lax.axis_index(a) for a in ("k", "zh", "yh"))
    chip = lax.axis_index(GROUP)
    pack_count, packed_width = inputs.shape
    features = packed_width // 8
    width = features * columns
    clips = lengths.shape[0]
    slot = pack_count * 8 // clips
    group = 2 * chips
    lines = -(-(slot // 8 + 1) // 64) * 64
    lanes = 8 // group
    quarter = lanes * lines
    slots = 8 * lines
    half = slots // 2
    rows = w_query.shape[0]
    block_heads = HEADS // columns
    head_dim = width // HEADS
    split = block_heads % 2 == 0
    part_heads = block_heads // 2 if split else block_heads
    heads = 2 * block_heads
    units = w_in.shape[1]
    half_units = units // 2

    def start_of(clip, j):
        return (slot * clip - j + 7) // 8

    def order_tokens(own, other):
        ordered = jnp.stack(in_order([own, other], "k")).reshape(2, 2, 2, yl_size, features, quarter)
        return ordered.transpose(0, 2, 1, 3, 4, 5).reshape(columns, features, quarter)

    def exchange(blocks):
        return lax.all_to_all(blocks, ("zh", "zl", "yh", "yl"), 0, 0)

    def join(moved):
        return moved.reshape(width, quarter).T

    def cut(tensor):
        return tensor.T.reshape(columns, features, quarter)

    def by_core(tensor, parts):
        if not parts:
            return jnp.broadcast_to(tensor[None], (2,) + tensor.shape)
        return tensor.reshape((2, tensor.shape[0] // 2) + tensor.shape[1:])

    def gather_others(shard):
        return lax.all_gather(shard, OTHERS, axis=0)

    def arrange_heads(stack):
        stack = stack.reshape(-1, 4, 4, part_heads, head_dim, 2 * rows)
        if not split:
            stack = lax.dynamic_slice_in_dim(stack, 2 * k, 2, 1)
        block = stack.shape[:2] + (1,) + stack.shape[3:]
        return join_rows(stack, pl.BlockSpec(block, lambda i: (0, 0, i, 0, 0, 0)), 4, heads * PAD, True)

    def arrange_units(stack, which):
        stack = stack.reshape(-1, 4, 2, half_units, 2 * rows)
        block = (stack.shape[0], 1, 1) + stack.shape[3:]
        return join_rows(stack, pl.BlockSpec(block, lambda i: (0, i, which, 0, 0)), 4, half_units, False)

    full_vectors = jnp.stack([ln1_gain, ln1_bias, ln2_gain, ln2_bias, b_attn_out, b_out])
    part_vector = jnp.concatenate([b_query, b_value, b_in])
    full_count = full_vectors.shape[0]
    full_by = jnp.stack(in_order(pieces_of(full_vectors, GROUP), GROUP))
    all_lengths = jnp.concatenate(in_order(pieces_of(lengths, "k"), "k"))

    taken = take_positions(inputs, slot, clips, lanes, lines)
    own_tokens, other_tokens = pick(taken, k, 0), swap(pick(taken, 1 - k, 0), "k")
    turned = [t.astype(BF).T for t in (w_query, w_key, w_value)] + [w_attn_out.astype(BF)]
    head_parts = jnp.stack([by_core(t, split) for t in turned], axis=1)
    head_parts = head_parts.reshape(2, 4 * part_heads * head_dim, rows)
    own_parts, other_parts = pick(head_parts, k, 0), swap(pick(head_parts, 1 - k, 0), "k")
    head_shard = jnp.concatenate(in_order([own_parts, other_parts], "k"), axis=1)
    head_stacked = gather_others(head_shard)

    ordered, cotangent, w_in, w_out, full_by = sync(
        order_tokens(own_tokens, other_tokens), cotangent, w_in, w_out, full_by
    )
    moved = exchange(ordered)
    full_size = full_by.size
    vector_pieces = in_order(pieces_of(jnp.concatenate([full_by.reshape(-1), part_vector]), "zh"), "zh")
    vector_pieces = in_order(pieces_of(jnp.stack(vector_pieces), "yh"), "yh")
    unit_parts = jnp.stack([by_core(w_in.astype(BF).T, True), by_core(w_out.astype(BF), True)], axis=1)
    unit_parts = unit_parts.reshape(2, units, rows)
    own_parts, other_parts = pick(unit_parts, k, 0), swap(pick(unit_parts, 1 - k, 0), "k")
    unit_shard = jnp.concatenate(in_order([own_parts, other_parts], "k"), axis=1)
    unit_shard = unit_shard.reshape(2, half_units, 2 * rows)
    unit_stacked = gather_others(unit_shard)
    taken = take_positions(cotangent, slot, clips, lanes, lines)
    own_tokens, other_tokens = pick(taken, k, 0), swap(pick(taken, 1 - k, 0), "k")
    ordered_grads = order_tokens(own_tokens, other_tokens)

    all_vectors = jnp.stack(vector_pieces, axis=1)
    part_by = all_vectors[:, :, full_size:].reshape(4, -1)
    full_by = all_vectors[:, :, :full_size].reshape(2, 2, 2, yl_size, full_count, features)
    full_by = full_by.transpose(4, 0, 2, 1, 3, 5)
    gain_one, shift_one, gain_two, shift_two, attn_shift, out_shift = full_by.reshape(full_count, 1, width)

    def head_vector(tensor):
        tensor = tensor.reshape(4, block_heads, head_dim)
        if split:
            tensor = pick(tensor.reshape(4, 2, part_heads, head_dim), k, 1)
        else:
            tensor = lax.dynamic_slice_in_dim(tensor, 2 * k, 2, 0)
        tensor = tensor.reshape(heads, head_dim)
        return jnp.pad(tensor, ((0, 0), (0, PAD - head_dim)))

    query_shift = head_vector(part_by[:, :features])
    value_shift = head_vector(part_by[:, features : 2 * features])
    unit_shift = pick(part_by[:, 2 * features :].reshape(4, 2, half_units), k, 1).reshape(-1)

    clip_length = pick(all_lengths, zh * 2 + yh, 0)

    def slots_of(part):
        j = part * lanes + jnp.repeat(jnp.arange(lanes), lines)
        return 8 * (start_of(yh, j) + jnp.tile(jnp.arange(lines), lanes)) + j - slot * yh

    own_valid = slots_of(chip * 2 + k) < clip_length
    slot_order = jnp.concatenate([slots_of((chip ^ d) * 2 + (k ^ c)) for d in range(chips) for c in range(2)])
    key_mask = jnp.where(slot_order < clip_length, 0.0, MASKED)

    lane = jnp.arange(PAD)[None, :]
    none = jnp.zeros((heads, PAD), F32)
    is_first = jnp.broadcast_to(lane == head_dim, (heads, PAD)).astype(F32)
    is_extra = jnp.broadcast_to((lane >= head_dim) & (lane < head_dim + 2), (heads, PAD)).astype(F32)
    qkv_shift = jnp.concatenate([query_shift, none, value_shift]).reshape(1, -1)
    qkv_scale = jnp.concatenate([none + head_dim**-0.5 * LOG2E, none + 1, none + 1]).reshape(1, -1)
    qkv_extra = jnp.concatenate([is_first, none, -is_extra]).reshape(1, -1)
    mask_lane = jnp.concatenate([none, is_first, none]).reshape(1, -1)

    def blocks_of(tensor):
        count = tensor.shape[0] // (2 * quarter)
        return [
            [tensor[(2 * d + c) * quarter : (2 * d + c + 1) * quarter] for c in range(2)]
            for d in range(count)
        ]

    tokens = join(moved).astype(F32)
    normal_one, scale_one, normed_part = norm_forward(tokens, gain_one, shift_one)
    normed_far = far_pieces(normed_part)
    normed_near = with_core(normed_part)
    normed_near, head_stacked = sync(normed_near, head_stacked)
    head_weights = arrange_heads(head_stacked).reshape(4, heads * PAD, width)
    normed_far, ordered_grads = sync(normed_far, ordered_grads)
    moved_grads = exchange(ordered_grads)
    qkv_weights = head_weights[:3].reshape(3 * heads * PAD, width)
    attn_weights = head_weights[3]

    def qkv(rows_d, d):
        mask_d = key_mask[d * 2 * quarter : (d + 1) * 2 * quarter, None]
        product = (dot(rows_d, qkv_weights, 1, 1) + qkv_shift) * qkv_scale
        return (product + qkv_extra + mask_d * mask_lane).astype(BF)

    packed_near = qkv(normed_near, 0)
    normed_rows = [normed_near] + [with_core(v) for v in normed_far]
    packed = jnp.concatenate(
        [packed_near] + [qkv(v, d) for d, v in enumerate(normed_rows) if d], axis=0
    )
    far_context, far_wide, far_weights = attend(packed, heads, 1)

    def attn_product(v):
        return dot(v, attn_weights, 1, 0)

    near_chips = chips // 2
    far_sums = [cores_sum(attn_product, b).astype(BF) for b in blocks_of(far_context)]
    far_sums, packed, moved_grads = sync(far_sums, packed, moved_grads)
    far_total = send_far(far_sums) if near_chips == 1 else None
    near_context, near_wide, near_weights = attend(packed, heads, 0)
    normed = jnp.concatenate(normed_rows, axis=0)
    grad_low = jnp.where(own_valid[:, None], join(moved_grads), jnp.zeros((quarter, width), BF))
    if near_chips == 1:
        near_context, far_total, normed, grad_low = sync(near_context, far_total, normed, grad_low)
    near_sums = [cores_sum(attn_product, b) for b in blocks_of(near_context)]
    if near_chips > 1:
        far_total = send_far((near_sums + far_sums)[1:])
    grad_far = far_pieces(grad_low)
    grad_near = with_core(grad_low)
    attn_part = near_sums[0] + far_total + attn_shift
    middle = tokens + attn_part
    normal_two, scale_two, normed_two_part = norm_forward(middle, gain_two, shift_two)
    normed_two_part, grad_far = sync(normed_two_part, grad_far)
    two_near = with_core(normed_two_part)
    two_far = far_pieces(normed_two_part)
    two_near, unit_stacked = sync(two_near, unit_stacked)
    in_weights = arrange_units(unit_stacked, 0)
    out_weights = arrange_units(unit_stacked, 1)

    def feed(rows_d):
        hidden = dot(rows_d, in_weights, 1, 1) + unit_shift
        below = 0.5 * (1.0 + lax.erf(hidden * 0.5**0.5))
        slope = below + hidden * (jnp.exp(-0.5 * hidden * hidden) * (0.5 / jnp.pi) ** 0.5)
        return (hidden * below).astype(BF), slope

    def feed_back(grad_d, slope):
        return (dot(grad_d, out_weights, 1, 1) * slope).astype(BF)

    near_active, near_slope = feed(two_near)
    near_hidden = feed_back(grad_near, near_slope)
    near_hidden, two_far = sync(near_hidden, two_far)
    two_rows = [two_near] + [with_core(v) for v in two_far]
    far_feed = [feed(v) for v in two_rows[1:]]
    grad_rows = [grad_near] + [with_core(v) for v in grad_far]
    grad_hidden = jnp.concatenate(
        [near_hidden] + [feed_back(g, f[1]) for g, f in zip(grad_rows[1:], far_feed)], axis=0
    )
    active = jnp.concatenate([near_active] + [f[0] for f in far_feed], axis=0)

    def in_product(v):
        return dot(v, in_weights, 1, 0)

    hidden_blocks = blocks_of(grad_hidden)
    far_two = [cores_sum(in_product, b).astype(BF) for b in hidden_blocks[1:]]
    grad_hidden, near_blocks, far_two, active = sync(grad_hidden, hidden_blocks[0], far_two, active)
    near_two = cores_sum(in_product, near_blocks)
    normed_two = jnp.concatenate(two_rows, axis=0)
    grad_full = jnp.concatenate(grad_rows, axis=0)

    out_total = dot(active, grad_full, 0, 0).astype(BF).reshape(2, 2, half_units, width)
    in_total = dot(grad_hidden, normed_two, 0, 0).astype(BF).reshape(2, 2, half_units, width)
    two_arrived, active, out_total, in_total = sync(send_far(far_two), active, out_total, in_total)
    out_half = send_units(out_total, "yh", 1)
    in_half = send_rows(in_total)
    grad_two = near_two + two_arrived
    grad_out = grad_low.astype(F32)
    grad_middle = grad_out + norm_backward(grad_two, normal_two, scale_two, gain_two)
    grad_mid_part = grad_middle.astype(BF)
    mid_far = far_pieces(grad_mid_part)
    mid_near = with_core(grad_mid_part)

    def context_grad(v):
        return dot(v, attn_weights, 1, 1).astype(BF)

    def out_product(v):
        return dot(v, out_weights, 1, 0)

    mid_half = jnp.concatenate([mid_near] + [with_core(v) for v in mid_far[: near_chips - 1]], axis=0)
    near_grad = context_grad(mid_half)
    active_blocks = blocks_of(active)
    delta_given = swap(jnp.concatenate([out_product(b[1]).astype(BF) for b in active_blocks]), "k")
    delta_cores = [
        out_product(b[0]) + delta_given[d * quarter : (d + 1) * quarter].astype(F32)
        for d, b in enumerate(active_blocks)
    ]
    near_delta, far_delta = delta_cores[0], [v.astype(BF) for v in delta_cores[1:]]
    near_grad, near_delta, far_delta = sync(near_grad, near_delta, far_delta)
    first = attend_back(packed, near_grad, near_wide, near_weights, heads, head_dim, 0)
    first, mid_far, far_delta, out_half, in_half = sync(first, mid_far, far_delta, out_half, in_half)
    delta_far = send_far(far_delta)
    out_half = send_rows(summed(out_half))
    in_half = send_units(summed(in_half), "yh", 1)
    mid_rows = [mid_near] + [with_core(v) for v in mid_far]
    mid_full = jnp.concatenate(mid_rows, axis=0)
    far_grad = context_grad(mid_full[half:])
    grads = attend_back(packed, far_grad, far_wide, far_weights, heads, head_dim, 1, list(first))
    qkv_cube = qkv_weights.reshape(3, heads * PAD, width)

    def qkv_product(v):
        return sum(dot(v[j], qkv_cube[j], 1, 0) for j in range(3))

    grad_blocks = [
        [grads[:, (2 * d + c) * quarter : (2 * d + c + 1) * quarter] for c in range(2)] for d in range(chips)
    ]
    far_one = [cores_sum(qkv_product, b).astype(BF) for b in grad_blocks[1:]]
    grads, far_one, near_blocks, out_half, in_half = sync(grads, far_one, grad_blocks[0], out_half, in_half)
    far_arrived = send_far(far_one)
    near_one = cores_sum(qkv_product, near_blocks)
    unit_sums = jnp.stack([summed(out_half), summed(in_half)])
    far_arrived, unit_sums = sync(far_arrived, unit_sums)
    unit_half = send_units(unit_sums, "zh", 1)
    context = jnp.concatenate([near_context, far_context], axis=0)
    grads, near_one, delta_far, context, mid_rows = sync(grads, near_one, delta_far, context, mid_rows)
    mid_full = jnp.concatenate(mid_rows, axis=0)

    def trim(total):
        return total.reshape(-1, part_heads, PAD, width)[:, :, :head_dim].reshape(-1, part_heads * head_dim, width)

    def head_chunk(totals):
        chunk = jnp.stack([trim(t) for t in totals], axis=1).reshape(-1, len(totals) * part_heads * head_dim, width)
        if not split:
            blank = jnp.zeros((4,) + chunk.shape[1:], BF)
            chunk = lax.dynamic_update_slice_in_dim(blank, chunk, 2 * k, 0)
        return chunk.reshape((2, 2) + chunk.shape[1:])

    query_key = head_chunk([dot(grads[j], normed, 0, 0).astype(BF) for j in range(2)])
    value_attn = head_chunk([dot(grads[2], normed, 0, 0).astype(BF), dot(context, mid_full, 0, 0).astype(BF)])
    query_key_half = send_rows(query_key)
    value_attn_half = send_units(value_attn, "yh", 1)
    grad_one = near_one + far_arrived
    grad_tokens = norm_backward(grad_one, normal_one, scale_one, gain_one)
    last_part = (grad_middle + grad_tokens).astype(BF)
    moved_last = exchange(cut(last_part))
    delta = (attn_part + near_delta + delta_far + out_shift).astype(BF)

    full_sums = jnp.stack(
        [
            jnp.sum(v, axis=0)
            for v in (
                grad_one * normal_one,
                grad_one,
                grad_middle,
                grad_two * normal_two,
                grad_two,
                grad_out,
            )
        ]
    )

    def head_sums(tensor):
        total = jnp.sum(tensor.astype(F32), axis=0).reshape(-1, part_heads, PAD)[:, :, :head_dim]
        if not split:
            blank = jnp.zeros((4,) + total.shape[1:], F32)
            total = lax.dynamic_update_slice_in_dim(blank, total, 2 * k, 0)
        return total.reshape(4, -1)

    part_sums = jnp.concatenate(
        [
            head_sums(grads[0]),
            head_sums(grads[2]),
            jnp.sum(grad_hidden.astype(F32), axis=0).reshape(4, half_units),
        ],
        axis=1,
    )
    full_sums = full_sums.reshape(full_count, 2, 2, 2, yl_size, features).transpose(1, 3, 2, 4, 0, 5)
    full_size = full_sums[0, 0].size
    flat = jnp.concatenate([full_sums.reshape(2, 2, -1), part_sums.reshape(2, 2, -1)], axis=2)
    flat_pieces = pieces_of(flat, "x")
    query_key_half, value_attn_half, flat_pieces = sync(query_key_half, value_attn_half, flat_pieces)
    query_key_half = send_units(summed(query_key_half), "yh", 1)
    value_attn_half = send_rows(summed(value_attn_half))
    flat_half = send_units(sum(flat_pieces), "yh", 1)
    moved_last, query_key_half, value_attn_half, delta_blocks, flat_half, unit_half = sync(
        moved_last, query_key_half, value_attn_half, cut(delta), flat_half, unit_half
    )
    moved_delta = exchange(delta_blocks)
    head_half = send_units(jnp.stack([summed(query_key_half), summed(value_attn_half)]), "zh", 1)

    def two_cores(total, two):
        last = total.ndim - 1
        kept = lax.dynamic_slice_in_dim(total, k * rows, rows, last)
        other = swap(lax.dynamic_slice_in_dim(total, (1 - k) * rows, rows, last), "k")
        if not two:
            return kept.astype(F32) + other.astype(F32)
        return jnp.stack(in_order([kept, other], "k"), axis=1).astype(F32)

    def kept_tokens(moved):
        moved = moved.reshape(2, 2, 2, yl_size, features, quarter).transpose(0, 2, 1, 3, 4, 5)
        kept = pick(moved, k, 0)
        other = swap(pick(moved, 1 - k, 0), "k")
        ordered = jnp.stack(in_order([kept, other], "k"))
        return ordered.reshape(2, clips, chips, features, quarter)

    def put(tokens, base=None):
        return put_positions(tokens, slot, pack_count, lanes, lines, base)

    flat_half = send_units(sum(flat_half), "zh", 0)
    input_grad, moved_delta, flat_half = sync(put(kept_tokens(moved_last)), moved_delta, flat_half)
    delta_tokens, head_half, flat = sync(kept_tokens(moved_delta), head_half, sum(flat_half))
    full_flat, part_flat = flat[:full_size], flat[full_size:]

    by_chip = full_flat.reshape(chips, -1)
    mine = pick(by_chip, chip, 0)
    for d in range(1, chips):
        mine = mine + swap(pick(by_chip, chip ^ d, 0), GROUP, d)
    unit_cores = two_cores(summed(unit_half), True)
    grad_out_w = unit_cores[0].reshape(units, rows)
    grad_in_w = unit_cores[1].reshape(units, rows).T
    layer_out = put(delta_tokens, inputs)
    head_cores = two_cores(summed(head_half), split)
    head_cores = head_cores.reshape(2, -1, 2, part_heads * head_dim, rows)
    grad_query_w, grad_key_w, grad_value_w, grad_attn_w = (
        head_cores[i, :, j].reshape(features, rows) for i in range(2) for j in range(2)
    )

    own_size = mine.shape[0]
    last_pair = pieces_of(jnp.concatenate([mine, part_flat]), "k")
    vec_one_gain, vec_one_bias, vec_battn, vec_two_gain, vec_two_bias, vec_bout = (
        last_pair[0][:own_size] + last_pair[1][:own_size]
    ).reshape(full_count, features)
    head_size = part_heads * head_dim
    cores = in_order([p[own_size:] for p in last_pair], "k")
    if split:
        vec_bquery = jnp.concatenate([c[:head_size] for c in cores])
        vec_bvalue = jnp.concatenate([c[head_size : 2 * head_size] for c in cores])
    else:
        vec_bquery = cores[0][:head_size] + cores[1][:head_size]
        vec_bvalue = cores[0][head_size : 2 * head_size] + cores[1][head_size : 2 * head_size]
    vec_bin = jnp.concatenate([c[2 * head_size :] for c in cores])

    return (
        layer_out,
        input_grad,
        vec_one_gain,
        vec_one_bias,
        grad_query_w.T,
        vec_bquery,
        grad_key_w.T,
        grad_value_w.T,
        vec_bvalue,
        grad_attn_w,
        vec_battn,
        vec_two_gain,
        vec_two_bias,
        grad_in_w,
        vec_bin,
        grad_out_w,
        vec_bout,
    )


def solution(mesh):
    row_size, col_size = mesh.shape["row"], mesh.shape["col"]
    shape = (row_size // 2, 2, 2, 2, 2, col_size // 8)
    row, col = ("x", "k"), ("zh", "zl", "yh", "yl")
    grid = Mesh(mesh.devices.reshape(shape), row + col)
    return jax.shard_map(
        local,
        mesh=grid,
        in_specs=(
            P(row, col),
            P(row),
            P(row, col),
            P(col),
            P(col),
            P(row, col),
            P(col),
            P(row, col),
            P(row, col),
            P(col),
            P(col, row),
            P(col),
            P(col),
            P(col),
            P(row, col),
            P(col),
            P(col, row),
            P(col),
        ),
        out_specs=(
            P(row, col),
            P(row, col),
            P(col),
            P(col),
            P(row, col),
            P(col),
            P(row, col),
            P(row, col),
            P(col),
            P(col, row),
            P(col),
            P(col),
            P(col),
            P(row, col),
            P(col),
            P(col, row),
            P(col),
        ),
        check_vma=False,
    )
```
